128 devices in a mesh: region: 8 (over z_hi, y), group: 16 (over x, z_lo, core).
Axes of the slice: x: 4, y: 4, z: 4 (z_hi: 2, z_lo: 2; z = z_hi * 2 + z_lo), core: 2. Of those that a mesh axis runs over, the one named last changes fastest.
Arguments:
- tracers: float32 [32, 32, 64, 512], P('group', None, 'region'), may hold values from -6 to 6
- velocity: float32 [3, 32, 64, 512], P(None, None, 'region', 'group'), may hold values from -0.3 to 0.3
- sea_mask: int32 [32, 64, 512], P(None, 'region'), may hold values 0 or 1
- coupling: float32 [32, 32], replicated, may hold values from -1 to 1
- mixing: float32 [32], replicated, may hold values from 0.05 to 0.2
Outputs:
- fields: float32 [32, 32, 64, 512], P('group', None, 'region')
The draws below stay inside these ranges and needn't reach their ends.
Inputs may be any that keep to these rules, and one draw needn't show every extreme that they name: `sea_mask`: 1 marks an ocean cell, 0 land.
All inputs are finite; a program needn't handle non-finite values. No bound on the sum of `sea_mask` on one device may be relied on, other than what follows from the above.
Results may differ from the reference program's by a relative error of at most 0.0003.
Values sent between devices are 32-bit elements; how exact they have to be, the bound alone decides.
A program may use at most 128 MiB of HBM per device.

```python
import math
import jax
import jax.numpy as jnp
from jax import lax

NZ = 32
STEPS = 2
TRACERS = 32
NX = 64
NY = 512


def plant(result, key, least, largest):
    longest = result.shape.index(max(result.shape))
    spots = []
    for shift in (0, 1):
        where = [jax.random.randint(jax.random.fold_in(key, axis), (), 0, length) for axis, length in enumerate(result.shape)]
        where[longest] = (where[longest] + shift) % result.shape[longest]
        spots.append(tuple(where))
    return result.at[spots[0]].set(least).at[spots[1]].set(largest)


def levels(stream_key, extent, shards, least, largest):
    loudness, own = 1.0, jax.random.fold_in(stream_key, 6)
    for axis_at, blocks in shards:
        heights = jnp.exp(jax.random.uniform(jax.random.fold_in(own, axis_at), (blocks,), jnp.float32, least / len(shards), largest / len(shards)))
        loudness = loudness * jnp.repeat(heights, extent[axis_at] // blocks).reshape([-1 if axis == axis_at else 1 for axis in range(len(extent))])
    return loudness


def gaussian(rng, shape, deviation, reach, split=(), held_as=jnp.bfloat16):
    drawn = deviation * jax.random.normal(rng, shape, jnp.float32)
    if split:
        drawn = drawn * levels(rng, shape, split, -0.22, 0.18)
    return jnp.clip(drawn, -reach, reach).astype(held_as)


def setup_inputs(seed: int = 0) -> dict:
    key_of = jax.random.split(jax.random.key(seed), 6)
    return {
        "tracers": gaussian(key_of[0], (TRACERS, NZ, NX, NY), 1.0, 6.0, ((0, 16), (2, 8)), jnp.float32),
        "velocity": jnp.clip(jax.random.uniform(key_of[1], (3, NZ, NX, NY), jnp.float32, -0.3, 0.3) * levels(key_of[1], (3, NZ, NX, NY), ((2, 8), (3, 16)), -0.4, 0.0), -0.3, 0.3),
        "sea_mask": plant((jax.random.randint(key_of[2], (NZ, NX, NY), 0, 5) < 4).astype(jnp.int32), jax.random.fold_in(key_of[2], 1), 0, 1),
        "coupling": gaussian(key_of[3], (TRACERS, TRACERS), TRACERS ** -0.5, 1.0, (), jnp.float32),
        "mixing": jnp.clip(jnp.exp(jax.random.uniform(key_of[4], (NZ,), jnp.float32, math.log(0.05), math.log(0.2))), 0.05, 0.2),
    }


def minmod(former, latter):
    return 0.5 * (jnp.sign(former) + jnp.sign(latter)) * jnp.minimum(jnp.abs(former), jnp.abs(latter))


def face_flux(fields, sea_cells, courant_pad, direction):
    length = fields.shape[direction]

    def section(values_in, begin, finish):
        return lax.slice_in_dim(values_in, begin, finish, axis=direction)

    opened = section(sea_cells, 0, length - 1) * section(sea_cells, 1, length)
    jump_face = (section(fields, 1, length) - section(fields, 0, length - 1)) * opened
    slopes = minmod(section(jump_face, 0, length - 2), section(jump_face, 1, length - 1))
    courant = section(courant_pad, 1, length - 2)
    upwind = section(fields, 1, length - 2) + 0.5 * (1.0 - courant) * section(slopes, 0, length - 3)
    downwind = section(fields, 2, length - 1) - 0.5 * (1.0 + courant) * section(slopes, 1, length - 2)
    transport = courant * jnp.where(courant > 0, upwind, downwind) * section(opened, 1, length - 2)
    return transport, section(jump_face, 1, length - 2)


def advect(fields_pad, static_pad, vertical, mixing):
    sea_pad = static_pad[0:1]
    east_pad = static_pad[1:2]
    north_pad = static_pad[2:3]
    east_flux, _ = face_flux(fields_pad[:, :, :, 2:-2], sea_pad[:, :, :, 2:-2], east_pad[:, :, :, 2:-2], 2)
    north_flux, _ = face_flux(fields_pad[:, :, 2:-2, :], sea_pad[:, :, 2:-2, :], north_pad[:, :, 2:-2, :], 3)
    interior = fields_pad[:, :, 2:-2, 2:-2]
    sea_inner = sea_pad[:, :, 2:-2, 2:-2]
    depth_pad = ((0, 0), (2, 2), (0, 0), (0, 0))
    down_flux, down_jumps = face_flux(jnp.pad(interior, depth_pad), jnp.pad(sea_inner, depth_pad), jnp.pad(vertical[None], depth_pad), 1)
    mixing_faces = jnp.pad(mixing, 2)[1:-2].reshape(1, -1, 1, 1)
    down_flux = down_flux - mixing_faces * down_jumps
    return (interior - (east_flux[:, :, 1:] - east_flux[:, :, :-1])
            - (north_flux[:, :, :, 1:] - north_flux[:, :, :, :-1])
            - (down_flux[:, 1:] - down_flux[:, :-1]))


def react(fields, coupling):
    attenuation = 0.05 + 0.1 * fields[0] * fields[0]
    light_left = jnp.exp(-(jnp.cumsum(attenuation, axis=0) - attenuation))
    response = jnp.einsum("ts,szxy->tzxy", coupling, jnp.tanh(fields), precision=lax.Precision.HIGHEST)
    return (0.5 + light_left)[None] * response


def reference(tracers, velocity, sea_mask, coupling, mixing):
    sea_cells = sea_mask.astype(velocity.dtype)
    sides_pad = ((0, 0), (0, 0), (2, 2), (2, 2))
    static_pad = jnp.pad(jnp.concatenate([sea_cells[None], velocity[0:2]], 0), sides_pad)
    fields = tracers

    def advect_single(single):
        return advect(jnp.pad(single[None], sides_pad), static_pad, velocity[2], mixing)[0]

    for repeat in range(STEPS):
        fields = lax.map(advect_single, fields)
        fields = fields + sea_cells[None] * react(fields, coupling)
    return fields
```

```python
import functools

import jax
import jax.numpy as jnp
import numpy as np
from jax import lax
from jax.experimental import pallas as pl
from jax.experimental.pallas import tpu as pltpu
from jax.sharding import PartitionSpec as P

MESH = pl.DeviceIdType.MESH
STEPS = 2
NZ, NT, X, YB, G, R = 32, 32, 8, 32, 16, 8
XE, YE = X + 4, YB + 4
QUADS = ((0, 1, 6, 7), (2, 3, 4, 5))
NC = 10
OX, CX, QX, OY, CY, QY, OZ, CZ, QZ, SEA = range(NC)


def minmod(a, b):
    return jnp.maximum(jnp.minimum(a, b), jnp.minimum(jnp.maximum(a, b), 0.0))


def face(cell, following, slope, slope_following, c, q):
    forward = c > 0
    return c * (jnp.where(forward, cell, following) + q * jnp.where(forward, slope, slope_following))


def halves(value):
    high = value.astype(jnp.bfloat16)
    return high, (value - high.astype(jnp.float32)).astype(jnp.bfloat16)


def block_swap(v, lane):
    low, even = lane < 64, (lane // 32) % 2 == 0
    axis = v[0].ndim - 1
    a = [None] * 4
    for n in (0, 1):
        a[n] = jnp.where(low, v[n], pltpu.roll(v[n + 2], 64, axis))
        a[n + 2] = jnp.where(low, pltpu.roll(v[n], 64, axis), v[n + 2])
    b = [None] * 4
    for n in (0, 2):
        b[n] = jnp.where(even, a[n], pltpu.roll(a[n + 1], 32, axis))
        b[n + 1] = jnp.where(even, pltpu.roll(a[n], 96, axis), a[n + 1])
    return b


def kernel(tr, coef_in, spread, weights, own_mat, past_mat, mix, out,
           wmat, tin, tout, sb, rb, fa, fb, adv, coef, so, ro,
           tiles_in, tiles_out, send_in, recv_in, send_halo, recv_x, recv_y, send_out, recv_out, local_sem):
    r, g = lax.axis_index("region"), lax.axis_index("group")
    lane = lax.broadcasted_iota(jnp.int32, (8, 128), 1)
    row = lax.broadcasted_iota(jnp.int32, (8, 128), 0)
    fa2, fb2 = fa.reshape(XE * YE * 8, 128), fb.reshape(XE * YE * 8, 128)
    rb2, so2 = rb.reshape(2 * 4 * NT * 8, 128), so.reshape(2 * 4 * NT * 8, 128)

    def fetch(j):
        return pltpu.make_async_copy(tr.at[:, pl.ds(j * 128, 128)], tin.at[j], tiles_in.at[j])

    def put(j):
        return pltpu.make_async_copy(tout.at[j], out.at[:, pl.ds(j * 128, 128)], tiles_out.at[j])

    for j in range(4):
        fetch(j).start()

    for f in (fa, fb):
        f[0:2, 2:34] = jnp.zeros((2, 32, 8, 128), jnp.float32)
        f[10:12, 2:34] = jnp.zeros((2, 32, 8, 128), jnp.float32)
        f[2:10, 0:2] = jnp.zeros((8, 2, 8, 128), jnp.float32)
        f[2:10, 34:36] = jnp.zeros((8, 2, 8, 128), jnp.float32)

    barrier = pltpu.get_barrier_semaphore()

    def greet(d, carry):
        pl.semaphore_signal(barrier, inc=1, device_id=(r, lax.rem(g + d, G)), device_id_type=MESH)
        return carry

    lax.fori_loop(1, G, greet, 0)

    @pl.when(r > 0)
    def _():
        pl.semaphore_signal(barrier, inc=1, device_id=(r - 1, g), device_id_type=MESH)

    @pl.when(r < R - 1)
    def _():
        pl.semaphore_signal(barrier, inc=1, device_id=(r + 1, g), device_id_type=MESH)

    for j in range(4):
        fetch(j).wait()

    for h, quad in enumerate(QUADS):
        def regroup(n, carry, h=h, quad=quad):
            t, zq = n // 4, n % 4
            for j in range(4):
                v = [tin[j, pl.ds((t * NZ + zq * 8) * X + x, 8, stride=8), :] for x in quad]
                for i, b in enumerate(block_swap(v, lane)):
                    sb[4 * j + i, h, zq, t] = b
            return carry

        lax.fori_loop(0, 8, regroup, 0)
        if h == 0:
            pl.semaphore_wait(barrier, G - 1 + jnp.minimum(r, 1) + jnp.minimum(R - 1 - r, 1))

        def send(d, carry, h=h):
            to = lax.rem(g + d, G)
            pltpu.make_async_remote_copy(
                src_ref=sb.at[to, h], dst_ref=rb.at[h, :, pl.ds(2 * g, 2)],
                send_sem=send_in.at[h], recv_sem=recv_in.at[h],
                device_id=(r, to), device_id_type=MESH).start()
            return carry

        lax.fori_loop(1, G, send, 0)
        pltpu.make_async_copy(sb.at[g, h], rb.at[h, :, pl.ds(2 * g, 2)], local_sem.at[h]).start()

    high, low = halves(weights[...])
    wmat[...] = jnp.concatenate([jnp.concatenate([high, low], 1), jnp.concatenate([high, jnp.zeros_like(low)], 1)], 0)

    def spread_one(zr, carry):
        d = coef_in[zr]
        high = d.astype(jnp.bfloat16).astype(jnp.float32)
        rest = d - high
        mid = rest.astype(jnp.bfloat16).astype(jnp.float32)
        low = rest - mid
        stack = jnp.concatenate([high, mid, low, jnp.zeros((8, 512), jnp.float32)], axis=0)
        turned = stack.T.astype(jnp.bfloat16)
        for k in range(NC):
            wide = jnp.dot(turned, spread[k], preferred_element_type=jnp.float32)
            coef.at[k].reshape(XE * YE * 8, 128)[pl.ds(zr, XE * YE, stride=8), :] = wide[:XE * YE]
        return carry

    lax.fori_loop(0, 8, spread_one, 0)

    def x_halo(f, s, do):
        @pl.when(r > 0)
        def _():
            do(pltpu.make_async_remote_copy(
                src_ref=f.at[2:4, 2:34], dst_ref=f.at[10:12, 2:34],
                send_sem=send_halo.at[s, 0], recv_sem=recv_x.at[s, 1],
                device_id=(r - 1, g), device_id_type=MESH))

        @pl.when(r < R - 1)
        def _():
            do(pltpu.make_async_remote_copy(
                src_ref=f.at[8:10, 2:34], dst_ref=f.at[0:2, 2:34],
                send_sem=send_halo.at[s, 1], recv_sem=recv_x.at[s, 0],
                device_id=(r + 1, g), device_id_type=MESH))

    def y_halo(f, s, do):
        @pl.when(g > 0)
        def _():
            do(pltpu.make_async_remote_copy(
                src_ref=f.at[2:10, 2:4], dst_ref=f.at[2:10, 34:36],
                send_sem=send_halo.at[s, 2], recv_sem=recv_y.at[s, 1],
                device_id=(r, g - 1), device_id_type=MESH))

        @pl.when(g < G - 1)
        def _():
            do(pltpu.make_async_remote_copy(
                src_ref=f.at[2:10, 32:34], dst_ref=f.at[2:10, 0:2],
                send_sem=send_halo.at[s, 3], recv_sem=recv_y.at[s, 0],
                device_id=(r, g + 1), device_id_type=MESH))

    def begin(copy):
        copy.start()

    def arrive(f, s):
        def landed(ref, sem):
            pltpu.make_async_copy(ref, ref, sem).wait()

        @pl.when(r > 0)
        def _():
            landed(f.at[0:2, 2:34], recv_x.at[s, 0])

        @pl.when(r < R - 1)
        def _():
            landed(f.at[10:12, 2:34], recv_x.at[s, 1])

        @pl.when(g > 0)
        def _():
            landed(f.at[2:10, 0:2], recv_y.at[s, 0])

        @pl.when(g < G - 1)
        def _():
            landed(f.at[2:10, 34:36], recv_y.at[s, 1])

    for h, quad in enumerate(QUADS):
        some = rb.at[h, :, 0:2 * (G - 1)]
        pltpu.make_async_copy(some, some, recv_in.at[h]).wait()
        pltpu.make_async_copy(sb.at[g, h], rb.at[h, :, pl.ds(2 * g, 2)], local_sem.at[h]).wait()

        def turn(zr, carry, h=h, quad=quad):
            turned = rb2[pl.ds(h * 4 * NT * 8 + zr, 128, stride=8), :].T
            for n, x in enumerate(quad):
                fa2[pl.ds(((x + 2) * YE + 2) * 8 + zr, YB, stride=8), :] = turned[n * YB:(n + 1) * YB]
            return carry

        lax.fori_loop(0, 8, turn, 0)
        if h == 0:
            x_halo(fa, 0, begin)
    y_halo(fa, 0, begin)

    def z_up(v):
        s = pltpu.roll(v, 7, 1)
        return jnp.where(row == 7, pltpu.roll(s, 96, 2), s)

    def z_down(v):
        s = pltpu.roll(v, 1, 1)
        return jnp.where(row == 0, pltpu.roll(s, 32, 2), s)

    def advect(f):
        def cells(e):
            return f[2:10, e]

        def along(k, e):
            return coef[k, 2:10, e]

        f1, f2 = cells(1), cells(2)
        j0 = (f1 - cells(0)) * along(OY, 0)
        j1 = (f2 - f1) * along(OY, 1)
        j2 = (cells(3) - f2) * along(OY, 2)
        s1, s2 = minmod(j0, j1), minmod(j1, j2)
        start = (j2, s2, face(f1, f2, s1, s2, along(CY, 1), along(QY, 1)))

        def column(y, carry):
            jump, slope, before = carry
            e = y + 2
            fx = f[:, e]
            inner, following = fx[2:10], cells(e + 1)
            jump_next = (cells(e + 2) - following) * along(OY, e + 1)
            slope_next = minmod(jump, jump_next)
            after = face(inner, following, slope, slope_next, along(CY, e), along(QY, e))
            total = inner - (after - before)
            jx = (fx[1:] - fx[:-1]) * coef[OX, 0:11, e]
            sx = minmod(jx[:-1], jx[1:])
            flux = face(fx[1:10], fx[2:11], sx[:-1], sx[1:], coef[CX, 1:10, e], coef[QX, 1:10, e])
            total = total - (flux[1:] - flux[:-1])
            below = z_up(inner)
            jz = (below - inner) * along(OZ, e)
            sz = minmod(z_down(jz), jz)
            down = face(inner, below, sz, z_up(sz), along(CZ, e), along(QZ, e)) - mix[...] * jz
            adv[:, y] = total - (down - z_down(down))
            return jump_next, slope_next, after

        lax.fori_loop(0, YB, column, start)

    def react(x, f):
        a = adv[x]
        att = 0.05 + 0.1 * a * a
        inc = att
        for step in (1, 2, 4):
            inc = inc + jnp.where(row >= step, pltpu.roll(inc, step, 1), 0.0)
        exc = (inc - att).reshape(256, 128)
        ahead = jnp.dot(jnp.concatenate(halves(exc), axis=1), own_mat[...], preferred_element_type=jnp.float32)
        past = jnp.dot(jnp.concatenate(halves(inc.reshape(256, 128)), axis=1), past_mat[...],
                       preferred_element_type=jnp.float32).reshape(YB, 8, 128)
        light = jnp.exp(-(ahead.reshape(YB, 8, 128) + past[:, 7:8, :]))
        both = jnp.dot(jnp.concatenate(halves(jnp.tanh(a).reshape(256, 128)), axis=1), wmat[...],
                       preferred_element_type=jnp.float32)
        response = (both[:, :128] + both[:, 128:]).reshape(YB, 8, 128)
        f[x + 2, 2:34] = a + coef[SEA, x + 2, 2:34] * ((0.5 + light) * response)

    arrive(fa, 0)
    advect(fa)
    for h, quad in enumerate(QUADS):
        for x in quad:
            react(x, fb)
        if h == 0:
            x_halo(fb, 1, begin)
    y_halo(fb, 1, begin)
    arrive(fb, 1)
    advect(fb)
    for s, f in ((0, fa), (1, fb)):
        x_halo(f, s, lambda copy: copy.wait_send())
        y_halo(f, s, lambda copy: copy.wait_send())

    for h, quad in enumerate(QUADS):
        for x in quad:
            react(x, fa)

        def turn_back(zr, carry, h=h, quad=quad):
            stack = [fa2[pl.ds(((x + 2) * YE + 2) * 8 + zr, YB, stride=8), :] for x in quad]
            so2[pl.ds(h * 4 * NT * 8 + zr, 128, stride=8), :] = jnp.concatenate(stack, axis=0).T
            return carry

        lax.fori_loop(0, 8, turn_back, 0)

        def send_back(d, carry, h=h):
            to = lax.rem(g + d, G)
            pltpu.make_async_remote_copy(
                src_ref=so.at[h, :, pl.ds(2 * to, 2)], dst_ref=ro.at[h, g],
                send_sem=send_out.at[h], recv_sem=recv_out.at[h],
                device_id=(r, to), device_id_type=MESH).start()
            return carry

        lax.fori_loop(1, G, send_back, 0)
        pltpu.make_async_copy(so.at[h, :, pl.ds(2 * g, 2)], ro.at[h, g], local_sem.at[2 + h]).start()

    for h, quad in enumerate(QUADS):
        some = ro.at[h, 0:G - 1]
        pltpu.make_async_copy(some, some, recv_out.at[h]).wait()
        pltpu.make_async_copy(so.at[h, :, pl.ds(2 * g, 2)], ro.at[h, g], local_sem.at[2 + h]).wait()

        def restore(n, carry, h=h, quad=quad):
            t, zq = n // 4, n % 4
            for j in range(4):
                v = block_swap([ro[h, 4 * j + i, zq, t] for i in range(4)], lane)
                for x, b in zip(quad, v):
                    tout[j, pl.ds((t * NZ + zq * 8) * X + x, 8, stride=8), :] = b
            return carry

        lax.fori_loop(0, 8, restore, 0)

    for j in range(4):
        put(j).start()
    for h in range(2):
        some = sb.at[0:G - 1, h]
        pltpu.make_async_copy(some, some, send_in.at[h]).wait()
        some = ro.at[h, 0:G - 1]
        pltpu.make_async_copy(some, some, send_out.at[h]).wait()
    for j in range(4):
        put(j).wait()


def neighbours(value, axis, shift):
    size = lax.axis_size(axis)
    pairs = [(i, i + shift) for i in range(size) if 0 <= i + shift < size]
    return lax.ppermute(value, axis, pairs)


def face_coefficients(velocity, sea_mask, coupling):
    g = lax.axis_index("group")
    sea = jnp.pad(sea_mask.astype(jnp.float32), ((0, 0), (0, 0), (2, 2)))
    sea = lax.dynamic_slice_in_dim(sea, g * YB, YE, axis=2)
    vx, vy, vz = velocity[0], velocity[1], velocity[2]
    low = neighbours(jnp.concatenate([sea[:, 6:8, 2:34], vx[:, 7:8]], axis=1), "region", 1)
    high = neighbours(sea[:, 0:2, 2:34], "region", -1)
    vy_low = neighbours(vy[:, :, 31:32], "group", 1)
    edges = ((0, 0), (0, 0), (2, 2))
    sea = jnp.concatenate([jnp.pad(low[:, 0:2], edges), sea, jnp.pad(high, edges)], axis=1)
    vx = jnp.pad(jnp.concatenate([low[:, 2:3], vx], axis=1), ((0, 0), (1, 2), (2, 2)))
    vy = jnp.pad(jnp.concatenate([vy_low, vy], axis=2), ((0, 0), (2, 2), (1, 2)))
    vz = jnp.pad(vz, ((0, 0), (2, 2), (2, 2)))
    ends = [(0, 0)] * 3
    parts = []
    for axis, c in ((1, vx), (2, vy), (0, vz)):
        pad = [(0, 1) if n == axis else (0, 0) for n in range(3)]
        following = jnp.pad(lax.slice_in_dim(sea, 1, sea.shape[axis], axis=axis), pad)
        opened = sea * following
        parts += [opened, c * opened, 0.5 * jnp.sign(c) - 0.5 * c]
    parts.append(sea)
    whole = jnp.stack(parts, 0).reshape(NC, 4, 8, XE * YE)
    whole = jnp.moveaxis(whole, 2, 0).reshape(8, NC * 4, XE * YE)
    return jnp.pad(whole, ((0, 0), (0, 0), (0, 512 - XE * YE)))


def shards(tracers, velocity, sea_mask, coupling, mixing):
    coef_in = face_coefficients(velocity, sea_mask, coupling)
    spread = np.zeros((NC, 3, NC, 4, 4, NT), np.float32)
    for k in range(NC):
        for b in range(4):
            spread[k, :, k, b, b] = 1
    spread = np.pad(spread.reshape(NC, 3 * NC * 4, 128), ((0, 0), (0, 8), (0, 0)))
    own = np.zeros((4, NT, 4, NT), np.float32)
    past = np.zeros((4, NT, 4, NT), np.float32)
    for a in range(4):
        own[a, 0, a] = 1
        past[a, 0, a + 1:] = 1
    own, past = own.reshape(128, 128), past.reshape(128, 128)
    own, past = np.concatenate([own, own], 0), np.concatenate([past, past], 0)
    block = np.kron(np.eye(4, dtype=np.float32), np.ones((NT, NT), np.float32))
    weights = jnp.tile(coupling.T, (4, 4)) * block
    mix = jnp.broadcast_to(mixing.reshape(4, 8).T[:, :, None], (8, 4, NT)).reshape(8, 128)

    vmem = pl.BlockSpec(memory_space=pltpu.VMEM)
    f32 = jnp.float32
    dma = pltpu.SemaphoreType.DMA
    out = pl.pallas_call(
        kernel,
        out_shape=jax.ShapeDtypeStruct((2 * NZ * X, G * YB), f32),
        in_specs=[pl.BlockSpec(memory_space=pl.ANY)] + [vmem] * 6,
        out_specs=pl.BlockSpec(memory_space=pl.ANY),
        scratch_shapes=[
            pltpu.VMEM((256, 256), jnp.bfloat16),
            pltpu.VMEM((4, 2 * NZ * X, 128), f32),
            pltpu.VMEM((4, 2 * NZ * X, 128), f32),
            pltpu.VMEM((G, 2, 4, 2, 8, 128), f32),
            pltpu.VMEM((2, 4, NT, 8, 128), f32),
            pltpu.VMEM((XE, YE, 8, 128), f32),
            pltpu.VMEM((XE, YE, 8, 128), f32),
            pltpu.VMEM((X, YB, 8, 128), f32),
            pltpu.VMEM((NC, XE, YE, 8, 128), f32),
            pltpu.VMEM((2, 4, NT, 8, 128), f32),
            pltpu.VMEM((2, G, 4, 2, 8, 128), f32),
            dma((4,)), dma((4,)), dma((2,)), dma((2,)), dma((2, 4)), dma((2, 2)), dma((2, 2)), dma((2,)), dma((2,)), dma((4,)),
        ],
        compiler_params=pltpu.CompilerParams(
            collective_id=0, has_side_effects=True, vmem_limit_bytes=48 * 2**20),
    )(tracers.reshape(2 * NZ * X, G * YB), coef_in,
      jnp.asarray(spread, jnp.bfloat16), weights, jnp.asarray(own, jnp.bfloat16),
      jnp.asarray(past, jnp.bfloat16), mix)
    return out.reshape(tracers.shape)


def solution(mesh):
    placed = (
        P("group", None, "region", None),
        P(None, None, "region", "group"),
        P(None, "region", None),
        P(),
        P(),
    )
    return jax.shard_map(
        shards,
        mesh=mesh,
        in_specs=placed,
        out_specs=P("group", None, "region", None),
        check_vma=False,
    )
```

```python
import functools

import jax
import jax.numpy as jnp
import numpy as np
from jax import lax
from jax.experimental import pallas as pl
from jax.experimental.pallas import tpu as pltpu
from jax.sharding import PartitionSpec as P

MESH = pl.DeviceIdType.MESH
STEPS = 2
NZ, NT, X, YB, G, R = 32, 32, 8, 32, 16, 8
XE, YE = X + 4, YB + 4
QUADS = ((0, 1, 6, 7), (2, 3, 4, 5))
NC = 10
OX, CX, QX, OY, CY, QY, OZ, CZ, QZ, SEA = range(NC)


def minmod(a, b):
    return jnp.maximum(jnp.minimum(a, b), jnp.minimum(jnp.maximum(a, b), 0.0))


def face(cell, following, slope, slope_following, c, q):
    forward = c > 0
    return c * (jnp.where(forward, cell, following) + q * jnp.where(forward, slope, slope_following))


def halves(value):
    high = value.astype(jnp.bfloat16)
    return high, (value - high.astype(jnp.float32)).astype(jnp.bfloat16)


def block_swap(v, lane):
    low, even = lane < 64, (lane // 32) % 2 == 0
    axis = v[0].ndim - 1
    a = [None] * 4
    for n in (0, 1):
        a[n] = jnp.where(low, v[n], pltpu.roll(v[n + 2], 64, axis))
        a[n + 2] = jnp.where(low, pltpu.roll(v[n], 64, axis), v[n + 2])
    b = [None] * 4
    for n in (0, 2):
        b[n] = jnp.where(even, a[n], pltpu.roll(a[n + 1], 32, axis))
        b[n + 1] = jnp.where(even, pltpu.roll(a[n], 96, axis), a[n + 1])
    return b


def kernel(tr, coef_in, spread, weights, own_mat, past_mat, mix, out,
           wmat, tin, tout, sb, rb, fa, fb, adv, edge, coef, so, ro,
           tiles_in, tiles_out, send_in, recv_in, send_halo, recv_x, recv_y, send_out, recv_out, local_sem):
    r, g = lax.axis_index("region"), lax.axis_index("group")
    lane = lax.broadcasted_iota(jnp.int32, (8, 128), 1)
    row = lax.broadcasted_iota(jnp.int32, (8, 128), 0)
    fa2, fb2 = fa.reshape(XE * YE * 8, 128), fb.reshape(XE * YE * 8, 128)
    rb2, so2 = rb.reshape(2 * 4 * NT * 8, 128), so.reshape(2 * 4 * NT * 8, 128)

    def fetch(j):
        return pltpu.make_async_copy(tr.at[:, pl.ds(j * 128, 128)], tin.at[j], tiles_in.at[j])

    def put(j):
        return pltpu.make_async_copy(tout.at[j], out.at[:, pl.ds(j * 128, 128)], tiles_out.at[j])

    for j in range(4):
        fetch(j).start()

    for f in (fa, fb):
        f[0:2, 2:34] = jnp.zeros((2, 32, 8, 128), jnp.float32)
        f[10:12, 2:34] = jnp.zeros((2, 32, 8, 128), jnp.float32)
        f[2:10, 0:2] = jnp.zeros((8, 2, 8, 128), jnp.float32)
        f[2:10, 34:36] = jnp.zeros((8, 2, 8, 128), jnp.float32)

    barrier = pltpu.get_barrier_semaphore()

    def greet(d, carry):
        pl.semaphore_signal(barrier, inc=1, device_id=(r, lax.rem(g + d, G)), device_id_type=MESH)
        return carry

    lax.fori_loop(1, G, greet, 0)

    @pl.when(r > 0)
    def _():
        pl.semaphore_signal(barrier, inc=1, device_id=(r - 1, g), device_id_type=MESH)

    @pl.when(r < R - 1)
    def _():
        pl.semaphore_signal(barrier, inc=1, device_id=(r + 1, g), device_id_type=MESH)

    for j in range(4):
        fetch(j).wait()

    for h, quad in enumerate(QUADS):
        def regroup(n, carry, h=h, quad=quad):
            t, zq = n // 4, n % 4
            for j in range(4):
                v = [tin[j, pl.ds((t * NZ + zq * 8) * X + x, 8, stride=8), :] for x in quad]
                for i, b in enumerate(block_swap(v, lane)):
                    sb[4 * j + i, h, zq, t] = b
            return carry

        lax.fori_loop(0, 8, regroup, 0)
        if h == 0:
            pl.semaphore_wait(barrier, G - 1 + jnp.minimum(r, 1) + jnp.minimum(R - 1 - r, 1))

        def send(d, carry, h=h):
            to = lax.rem(g + d, G)
            pltpu.make_async_remote_copy(
                src_ref=sb.at[to, h], dst_ref=rb.at[h, :, pl.ds(2 * g, 2)],
                send_sem=send_in.at[h], recv_sem=recv_in.at[h],
                device_id=(r, to), device_id_type=MESH).start()
            return carry

        lax.fori_loop(1, G, send, 0)
        pltpu.make_async_copy(sb.at[g, h], rb.at[h, :, pl.ds(2 * g, 2)], local_sem.at[h]).start()

    high, low = halves(weights[...])
    wmat[...] = jnp.concatenate([jnp.concatenate([high, low], 1), jnp.concatenate([high, jnp.zeros_like(low)], 1)], 0)

    def spread_one(zr, carry):
        d = coef_in[zr]
        high = d.astype(jnp.bfloat16).astype(jnp.float32)
        rest = d - high
        mid = rest.astype(jnp.bfloat16).astype(jnp.float32)
        low = rest - mid
        stack = jnp.concatenate([high, mid, low, jnp.zeros((8, 512), jnp.float32)], axis=0)
        turned = stack.T.astype(jnp.bfloat16)
        for k in range(NC):
            wide = jnp.dot(turned, spread[k], preferred_element_type=jnp.float32)
            coef.at[k].reshape(XE * YE * 8, 128)[pl.ds(zr, XE * YE, stride=8), :] = wide[:XE * YE]
        return carry

    lax.fori_loop(0, 8, spread_one, 0)

    def x_halo(f, s, do):
        @pl.when(r > 0)
        def _():
            do(pltpu.make_async_remote_copy(
                src_ref=f.at[2:4, 2:34], dst_ref=f.at[10:12, 2:34],
                send_sem=send_halo.at[s, 0], recv_sem=recv_x.at[s, 1],
                device_id=(r - 1, g), device_id_type=MESH))

        @pl.when(r < R - 1)
        def _():
            do(pltpu.make_async_remote_copy(
                src_ref=f.at[8:10, 2:34], dst_ref=f.at[0:2, 2:34],
                send_sem=send_halo.at[s, 1], recv_sem=recv_x.at[s, 0],
                device_id=(r + 1, g), device_id_type=MESH))

    def y_halo(f, s, do):
        @pl.when(g > 0)
        def _():
            do(pltpu.make_async_remote_copy(
                src_ref=f.at[2:10, 2:4], dst_ref=f.at[2:10, 34:36],
                send_sem=send_halo.at[s, 2], recv_sem=recv_y.at[s, 1],
                device_id=(r, g - 1), device_id_type=MESH))

        @pl.when(g < G - 1)
        def _():
            do(pltpu.make_async_remote_copy(
                src_ref=f.at[2:10, 32:34], dst_ref=f.at[2:10, 0:2],
                send_sem=send_halo.at[s, 3], recv_sem=recv_y.at[s, 0],
                device_id=(r, g + 1), device_id_type=MESH))

    def begin(copy):
        copy.start()

    def arrive(f, s):
        def landed(ref, sem):
            pltpu.make_async_copy(ref, ref, sem).wait()

        @pl.when(r > 0)
        def _():
            landed(f.at[0:2, 2:34], recv_x.at[s, 0])

        @pl.when(r < R - 1)
        def _():
            landed(f.at[10:12, 2:34], recv_x.at[s, 1])

        @pl.when(g > 0)
        def _():
            landed(f.at[2:10, 0:2], recv_y.at[s, 0])

        @pl.when(g < G - 1)
        def _():
            landed(f.at[2:10, 34:36], recv_y.at[s, 1])

    for h, quad in enumerate(QUADS):
        some = rb.at[h, :, 0:2 * (G - 1)]
        pltpu.make_async_copy(some, some, recv_in.at[h]).wait()
        pltpu.make_async_copy(sb.at[g, h], rb.at[h, :, pl.ds(2 * g, 2)], local_sem.at[h]).wait()

        def turn(zr, carry, h=h, quad=quad):
            turned = rb2[pl.ds(h * 4 * NT * 8 + zr, 128, stride=8), :].T
            for n, x in enumerate(quad):
                fa2[pl.ds(((x + 2) * YE + 2) * 8 + zr, YB, stride=8), :] = turned[n * YB:(n + 1) * YB]
            return carry

        lax.fori_loop(0, 8, turn, 0)
        if h == 0:
            x_halo(fa, 0, begin)
    y_halo(fa, 0, begin)

    def z_edges(f):
        def rows(ref, k):
            return ref.reshape(ref.shape[0] * ref.shape[1] * 8, 128)[pl.ds(2 * YE * 8 + k, X * YE, stride=8), :]

        def static(k, n):
            return rows(coef.at[k], n)

        next0 = pltpu.roll(rows(f, 0), 96, 1)
        next1 = pltpu.roll(rows(f, 1), 96, 1)
        last = rows(f, 7)
        jump = (next0 - last) * static(OZ, 7)
        slope = minmod((last - rows(f, 6)) * static(OZ, 6), jump)
        slope_next = minmod(jump, (next1 - next0) * pltpu.roll(static(OZ, 0), 96, 1))
        flux = face(last, next0, slope, slope_next, static(CZ, 7), static(QZ, 7)) - mix[7:8, :] * jump
        for n, k, v in ((0, 7, next0), (0, 0, pltpu.roll(jump, 32, 1)), (1, 7, slope_next), (1, 0, pltpu.roll(flux, 32, 1))):
            edge.at[n].reshape(X * YE * 8, 128)[pl.ds(k, X * YE, stride=8), :] = v

    def advect(f):
        z_edges(f)

        def cells(e):
            return f[2:10, e]

        def along(k, e):
            return coef[k, 2:10, e]

        f1, f2 = cells(1), cells(2)
        j0 = (f1 - cells(0)) * along(OY, 0)
        j1 = (f2 - f1) * along(OY, 1)
        j2 = (cells(3) - f2) * along(OY, 2)
        s1, s2 = minmod(j0, j1), minmod(j1, j2)
        start = (j2, s2, face(f1, f2, s1, s2, along(CY, 1), along(QY, 1)))

        def column(y, carry):
            jump, slope, before = carry
            e = y + 2
            fx = f[:, e]
            inner, following = fx[2:10], cells(e + 1)
            jump_next = (cells(e + 2) - following) * along(OY, e + 1)
            slope_next = minmod(jump, jump_next)
            after = face(inner, following, slope, slope_next, along(CY, e), along(QY, e))
            total = inner - (after - before)
            jx = (fx[1:] - fx[:-1]) * coef[OX, 0:11, e]
            sx = minmod(jx[:-1], jx[1:])
            flux = face(fx[1:10], fx[2:11], sx[:-1], sx[1:], coef[CX, 1:10, e], coef[QX, 1:10, e])
            total = total - (flux[1:] - flux[:-1])
            edge0, edge1 = edge[0, :, e], edge[1, :, e]
            below = jnp.where(row == 7, edge0, pltpu.roll(inner, 7, 1))
            jz = (below - inner) * along(OZ, e)
            sz = minmod(jnp.where(row == 0, edge0, pltpu.roll(jz, 1, 1)), jz)
            sz_next = jnp.where(row == 7, edge1, pltpu.roll(sz, 7, 1))
            down = face(inner, below, sz, sz_next, along(CZ, e), along(QZ, e)) - mix[...] * jz
            adv[:, y] = total - (down - jnp.where(row == 0, edge1, pltpu.roll(down, 1, 1)))
            return jump_next, slope_next, after

        lax.fori_loop(0, YB, column, start)

    def react(x, f):
        a = adv[x]
        att = 0.05 + 0.1 * a * a
        inc = att
        for step in (1, 2, 4):
            inc = inc + jnp.where(row >= step, pltpu.roll(inc, step, 1), 0.0)
        exc = (inc - att).reshape(256, 128)
        ahead = jnp.dot(jnp.concatenate(halves(exc), axis=1), own_mat[...], preferred_element_type=jnp.float32)
        past = jnp.dot(jnp.concatenate(halves(inc.reshape(256, 128)), axis=1), past_mat[...],
                       preferred_element_type=jnp.float32).reshape(YB, 8, 128)
        light = jnp.exp(-(ahead.reshape(YB, 8, 128) + past[:, 7:8, :]))
        both = jnp.dot(jnp.concatenate(halves(jnp.tanh(a).reshape(256, 128)), axis=1), wmat[...],
                       preferred_element_type=jnp.float32)
        response = (both[:, :128] + both[:, 128:]).reshape(YB, 8, 128)
        f[x + 2, 2:34] = a + coef[SEA, x + 2, 2:34] * ((0.5 + light) * response)

    arrive(fa, 0)
    advect(fa)
    for h, quad in enumerate(QUADS):
        for x in quad:
            react(x, fb)
        if h == 0:
            x_halo(fb, 1, begin)
    y_halo(fb, 1, begin)
    arrive(fb, 1)
    advect(fb)
    for s, f in ((0, fa), (1, fb)):
        x_halo(f, s, lambda copy: copy.wait_send())
        y_halo(f, s, lambda copy: copy.wait_send())

    for h, quad in enumerate(QUADS):
        for x in quad:
            react(x, fa)

        def turn_back(zr, carry, h=h, quad=quad):
            stack = [fa2[pl.ds(((x + 2) * YE + 2) * 8 + zr, YB, stride=8), :] for x in quad]
            so2[pl.ds(h * 4 * NT * 8 + zr, 128, stride=8), :] = jnp.concatenate(stack, axis=0).T
            return carry

        lax.fori_loop(0, 8, turn_back, 0)

        def send_back(d, carry, h=h):
            to = lax.rem(g + d, G)
            pltpu.make_async_remote_copy(
                src_ref=so.at[h, :, pl.ds(2 * to, 2)], dst_ref=ro.at[h, g],
                send_sem=send_out.at[h], recv_sem=recv_out.at[h],
                device_id=(r, to), device_id_type=MESH).start()
            return carry

        lax.fori_loop(1, G, send_back, 0)
        pltpu.make_async_copy(so.at[h, :, pl.ds(2 * g, 2)], ro.at[h, g], local_sem.at[2 + h]).start()

    for h, quad in enumerate(QUADS):
        some = ro.at[h, 0:G - 1]
        pltpu.make_async_copy(some, some, recv_out.at[h]).wait()
        pltpu.make_async_copy(so.at[h, :, pl.ds(2 * g, 2)], ro.at[h, g], local_sem.at[2 + h]).wait()

        def restore(n, carry, h=h, quad=quad):
            t, zq = n // 4, n % 4
            for j in range(4):
                v = block_swap([ro[h, 4 * j + i, zq, t] for i in range(4)], lane)
                for x, b in zip(quad, v):
                    tout[j, pl.ds((t * NZ + zq * 8) * X + x, 8, stride=8), :] = b
            return carry

        lax.fori_loop(0, 8, restore, 0)

    for j in range(4):
        put(j).start()
    for h in range(2):
        some = sb.at[0:G - 1, h]
        pltpu.make_async_copy(some, some, send_in.at[h]).wait()
        some = ro.at[h, 0:G - 1]
        pltpu.make_async_copy(some, some, send_out.at[h]).wait()
    for j in range(4):
        put(j).wait()


def neighbours(value, axis, shift):
    size = lax.axis_size(axis)
    pairs = [(i, i + shift) for i in range(size) if 0 <= i + shift < size]
    return lax.ppermute(value, axis, pairs)


def face_coefficients(velocity, sea_mask, coupling):
    g = lax.axis_index("group")
    sea = jnp.pad(sea_mask.astype(jnp.float32), ((0, 0), (0, 0), (2, 2)))
    sea = lax.dynamic_slice_in_dim(sea, g * YB, YE, axis=2)
    vx, vy, vz = velocity[0], velocity[1], velocity[2]
    low = neighbours(jnp.concatenate([sea[:, 6:8, 2:34], vx[:, 7:8]], axis=1), "region", 1)
    high = neighbours(sea[:, 0:2, 2:34], "region", -1)
    vy_low = neighbours(vy[:, :, 31:32], "group", 1)
    edges = ((0, 0), (0, 0), (2, 2))
    sea = jnp.concatenate([jnp.pad(low[:, 0:2], edges), sea, jnp.pad(high, edges)], axis=1)
    vx = jnp.pad(jnp.concatenate([low[:, 2:3], vx], axis=1), ((0, 0), (1, 2), (2, 2)))
    vy = jnp.pad(jnp.concatenate([vy_low, vy], axis=2), ((0, 0), (2, 2), (1, 2)))
    vz = jnp.pad(vz, ((0, 0), (2, 2), (2, 2)))
    ends = [(0, 0)] * 3
    parts = []
    for axis, c in ((1, vx), (2, vy), (0, vz)):
        pad = [(0, 1) if n == axis else (0, 0) for n in range(3)]
        following = jnp.pad(lax.slice_in_dim(sea, 1, sea.shape[axis], axis=axis), pad)
        opened = sea * following
        parts += [opened, c * opened, 0.5 * jnp.sign(c) - 0.5 * c]
    parts.append(sea)
    whole = jnp.stack(parts, 0).reshape(NC, 4, 8, XE * YE)
    whole = jnp.moveaxis(whole, 2, 0).reshape(8, NC * 4, XE * YE)
    return jnp.pad(whole, ((0, 0), (0, 0), (0, 512 - XE * YE)))


def shards(tracers, velocity, sea_mask, coupling, mixing):
    coef_in = face_coefficients(velocity, sea_mask, coupling)
    spread = np.zeros((NC, 3, NC, 4, 4, NT), np.float32)
    for k in range(NC):
        for b in range(4):
            spread[k, :, k, b, b] = 1
    spread = np.pad(spread.reshape(NC, 3 * NC * 4, 128), ((0, 0), (0, 8), (0, 0)))
    own = np.zeros((4, NT, 4, NT), np.float32)
    past = np.zeros((4, NT, 4, NT), np.float32)
    for a in range(4):
        own[a, 0, a] = 1
        past[a, 0, a + 1:] = 1
    own, past = own.reshape(128, 128), past.reshape(128, 128)
    own, past = np.concatenate([own, own], 0), np.concatenate([past, past], 0)
    block = np.kron(np.eye(4, dtype=np.float32), np.ones((NT, NT), np.float32))
    weights = jnp.tile(coupling.T, (4, 4)) * block
    mix = jnp.broadcast_to(mixing.reshape(4, 8).T[:, :, None], (8, 4, NT)).reshape(8, 128)

    vmem = pl.BlockSpec(memory_space=pltpu.VMEM)
    f32 = jnp.float32
    dma = pltpu.SemaphoreType.DMA
    out = pl.pallas_call(
        kernel,
        out_shape=jax.ShapeDtypeStruct((2 * NZ * X, G * YB), f32),
        in_specs=[pl.BlockSpec(memory_space=pl.ANY)] + [vmem] * 6,
        out_specs=pl.BlockSpec(memory_space=pl.ANY),
        scratch_shapes=[
            pltpu.VMEM((256, 256), jnp.bfloat16),
            pltpu.VMEM((4, 2 * NZ * X, 128), f32),
            pltpu.VMEM((4, 2 * NZ * X, 128), f32),
            pltpu.VMEM((G, 2, 4, 2, 8, 128), f32),
            pltpu.VMEM((2, 4, NT, 8, 128), f32),
            pltpu.VMEM((XE, YE, 8, 128), f32),
            pltpu.VMEM((XE, YE, 8, 128), f32),
            pltpu.VMEM((X, YB, 8, 128), f32),
            pltpu.VMEM((2, X, YE, 8, 128), f32),
            pltpu.VMEM((NC, XE, YE, 8, 128), f32),
            pltpu.VMEM((2, 4, NT, 8, 128), f32),
            pltpu.VMEM((2, G, 4, 2, 8, 128), f32),
            dma((4,)), dma((4,)), dma((2,)), dma((2,)), dma((2, 4)), dma((2, 2)), dma((2, 2)), dma((2,)), dma((2,)), dma((4,)),
        ],
        compiler_params=pltpu.CompilerParams(
            collective_id=0, has_side_effects=True, vmem_limit_bytes=48 * 2**20),
    )(tracers.reshape(2 * NZ * X, G * YB), coef_in,
      jnp.asarray(spread, jnp.bfloat16), weights, jnp.asarray(own, jnp.bfloat16),
      jnp.asarray(past, jnp.bfloat16), mix)
    return out.reshape(tracers.shape)


def solution(mesh):
    placed = (
        P("group", None, "region", None),
        P(None, None, "region", "group"),
        P(None, "region", None),
        P(),
        P(),
    )
    return jax.shard_map(
        shards,
        mesh=mesh,
        in_specs=placed,
        out_specs=P("group", None, "region", None),
        check_vma=False,
    )
```

```python
import jax
import jax.numpy as jnp
from jax import lax
from jax.experimental import pallas as pl
from jax.experimental.pallas import tpu as pltpu
from jax.sharding import PartitionSpec as P

MESH = pl.DeviceIdType.MESH
STEPS = 2
NZ, NT, X, YB, G, R = 32, 32, 8, 32, 16, 8
XE, YE = X + 4, YB + 4
QUADS = ((0, 1, 6, 7), (2, 3, 4, 5))
NC = 10
OX, CX, QX, OY, CY, QY, OZ, CZ, QZ, SEA = range(NC)


def minmod(a, b):
    return jnp.maximum(jnp.minimum(a, b), jnp.minimum(jnp.maximum(a, b), 0.0))


def face(cell, following, slope, slope_following, c, q):
    forward = c > 0
    return c * (jnp.where(forward, cell, following) + q * jnp.where(forward, slope, slope_following))


def halves(value):
    high = value.astype(jnp.bfloat16)
    return high, (value - high.astype(jnp.float32)).astype(jnp.bfloat16)


def block_swap(v, lane):
    low, even = lane < 64, (lane // 32) % 2 == 0
    axis = v[0].ndim - 1
    a = [None] * 4
    for n in (0, 1):
        a[n] = jnp.where(low, v[n], pltpu.roll(v[n + 2], 64, axis))
        a[n + 2] = jnp.where(low, pltpu.roll(v[n], 64, axis), v[n + 2])
    b = [None] * 4
    for n in (0, 2):
        b[n] = jnp.where(even, a[n], pltpu.roll(a[n + 1], 32, axis))
        b[n + 1] = jnp.where(even, pltpu.roll(a[n], 96, axis), a[n + 1])
    return b


def kernel(tr, velocity, mask, coupling, mixing, out,
           spread, own_mat, past_mat, mix, wmat, vel, sea3, q, dc, pack_up, pack_down, pack_y, got_low, got_high, got_y,
           tin, tout, sb, rb, fa, fb, adv, edge, coef, so, ro,
           statics_in, send_static, recv_static,
           tiles_in, tiles_out, send_in, recv_in, send_halo, recv_x, recv_y, send_out, recv_out, local_sem):
    r, g = lax.axis_index("region"), lax.axis_index("group")
    lane = lax.broadcasted_iota(jnp.int32, (8, 128), 1)
    row = lax.broadcasted_iota(jnp.int32, (8, 128), 0)
    fa2, fb2 = fa.reshape(XE * YE * 8, 128), fb.reshape(XE * YE * 8, 128)
    rb2, so2 = rb.reshape(2 * 4 * NT * 8, 128), so.reshape(2 * 4 * NT * 8, 128)

    def fetch(j):
        return pltpu.make_async_copy(tr.at[:, pl.ds(j * 128, 128)], tin.at[j], tiles_in.at[j])

    def put(j):
        return pltpu.make_async_copy(tout.at[j], out.at[:, pl.ds(j * 128, 128)], tiles_out.at[j])

    at = lax.div(g, 4)
    spots = (at, jnp.maximum(at - 1, 0), jnp.minimum(at + 1, 3))
    fetches = [pltpu.make_async_copy(velocity, vel, statics_in.at[0])]
    for n, spot in enumerate(spots):
        fetches.append(pltpu.make_async_copy(
            mask.at[:, :, pl.ds(pl.multiple_of(spot * 128, 128), 128)], sea3.at[n], statics_in.at[n + 1]))
    for copy in fetches:
        copy.start()
    for j in range(4):
        fetch(j).start()

    for f in (fa, fb):
        f[0:2, 2:34] = jnp.zeros((2, 32, 8, 128), jnp.float32)
        f[10:12, 2:34] = jnp.zeros((2, 32, 8, 128), jnp.float32)
        f[2:10, 0:2] = jnp.zeros((8, 2, 8, 128), jnp.float32)
        f[2:10, 34:36] = jnp.zeros((8, 2, 8, 128), jnp.float32)

    barrier = pltpu.get_barrier_semaphore()

    def greet(d, carry):
        pl.semaphore_signal(barrier, inc=1, device_id=(r, lax.rem(g + d, G)), device_id_type=MESH)
        return carry

    lax.fori_loop(1, G, greet, 0)

    @pl.when(r > 0)
    def _():
        pl.semaphore_signal(barrier, inc=1, device_id=(r - 1, g), device_id_type=MESH)

    @pl.when(r < R - 1)
    def _():
        pl.semaphore_signal(barrier, inc=1, device_id=(r + 1, g), device_id_type=MESH)

    q[...] = jnp.zeros(q.shape, jnp.float32)
    for copy in fetches:
        copy.wait()
    for k in range(3):
        q[k, :, 2:10, 2:34] = vel[k]
    place = lax.rem(g, 4)
    has_left = jnp.minimum(at, 1).astype(jnp.float32)
    has_right = jnp.minimum(3 - at, 1).astype(jnp.float32)
    centre = sea3[0].astype(jnp.float32)
    left = sea3[1].astype(jnp.float32) * has_left
    right = sea3[2].astype(jnp.float32) * has_right
    centre = jnp.where(jnp.logical_and(lane >= 126, place == 0), left, centre)
    centre = jnp.where(jnp.logical_and(lane < 2, place == 3), right, centre)
    q[3, :, 2:10, :] = pltpu.roll(centre, lax.rem(130 - 32 * place, 128), 2)

    def level_rows(k, e):
        return q.at[k].reshape(NZ * 16, 128)[pl.ds(e, NZ, stride=16), :]

    def put_rows(k, e, value):
        q.at[k].reshape(NZ * 16, 128)[pl.ds(e, NZ, stride=16), :] = value

    pack_up[0], pack_up[1], pack_up[2] = level_rows(3, 8), level_rows(3, 9), level_rows(0, 9)
    pack_down[0], pack_down[1] = level_rows(3, 2), level_rows(3, 3)

    def pack_level(z, p):
        return jnp.where(lane == z, pltpu.roll(q[1, z, 2:10, :], lax.rem(z + 95, 128), 1), p)

    pack_y[...] = lax.fori_loop(0, NZ, pack_level, jnp.zeros((8, 128), jnp.float32))

    for j in range(4):
        fetch(j).wait()

    def begin(copy):
        copy.start()

    def static_halo(do):
        @pl.when(r < R - 1)
        def _():
            do(pltpu.make_async_remote_copy(
                src_ref=pack_up, dst_ref=got_low, send_sem=send_static.at[0], recv_sem=recv_static.at[0],
                device_id=(r + 1, g), device_id_type=MESH))

        @pl.when(r > 0)
        def _():
            do(pltpu.make_async_remote_copy(
                src_ref=pack_down, dst_ref=got_high, send_sem=send_static.at[1], recv_sem=recv_static.at[1],
                device_id=(r - 1, g), device_id_type=MESH))

        @pl.when(g < G - 1)
        def _():
            do(pltpu.make_async_remote_copy(
                src_ref=pack_y, dst_ref=got_y, send_sem=send_static.at[2], recv_sem=recv_static.at[2],
                device_id=(r, g + 1), device_id_type=MESH))

    for h, quad in enumerate(QUADS):
        def regroup(n, carry, h=h, quad=quad):
            t, zq = n // 4, n % 4
            for j in range(4):
                v = [tin[j, pl.ds((t * NZ + zq * 8) * X + x, 8, stride=8), :] for x in quad]
                for i, b in enumerate(block_swap(v, lane)):
                    sb[4 * j + i, h, zq, t] = b
            return carry

        lax.fori_loop(0, 8, regroup, 0)
        if h == 0:
            pl.semaphore_wait(barrier, G - 1 + jnp.minimum(r, 1) + jnp.minimum(R - 1 - r, 1))
            static_halo(begin)

        def send(d, carry, h=h):
            to = lax.rem(g + d, G)
            pltpu.make_async_remote_copy(
                src_ref=sb.at[to, h], dst_ref=rb.at[h, :, pl.ds(2 * g, 2)],
                send_sem=send_in.at[h], recv_sem=recv_in.at[h],
                device_id=(r, to), device_id_type=MESH).start()
            return carry

        lax.fori_loop(1, G, send, 0)
        pltpu.make_async_copy(sb.at[g, h], rb.at[h, :, pl.ds(2 * g, 2)], local_sem.at[h]).start()

    def iota(shape, axis):
        return lax.broadcasted_iota(jnp.int32, shape, axis)

    square = (128, 128)
    block_in, block_out = iota(square, 0) // 32, iota(square, 1) // 32
    for k in range(NC):
        place_k = iota(square, 0) - (4 * k + block_out)
        hit = jnp.logical_or(place_k == 0, jnp.logical_or(place_k == 4 * NC, place_k == 8 * NC))
        spread[k] = jnp.where(hit, 1.0, 0.0).astype(jnp.bfloat16)
    first = iota(square, 0) % 32 == 0
    own = jnp.where(jnp.logical_and(first, block_in == block_out), 1.0, 0.0).astype(jnp.bfloat16)
    past = jnp.where(jnp.logical_and(first, block_in < block_out), 1.0, 0.0).astype(jnp.bfloat16)
    own_mat[...] = jnp.concatenate([own, own], 0)
    past_mat[...] = jnp.concatenate([past, past], 0)
    across = jnp.concatenate([coupling[...].T] * 4, 1)
    weights = jnp.where(block_in == block_out, jnp.concatenate([across] * 4, 0), 0.0)
    high, low = halves(weights)
    wmat[...] = jnp.concatenate([jnp.concatenate([high, low], 1), jnp.concatenate([high, jnp.zeros_like(low)], 1)], 0)
    tile = jnp.zeros((8, 128), jnp.float32)
    for z in range(NZ):
        tile = jnp.where(jnp.logical_and(row == z % 8, lane // 32 == z // 8), mixing[z], tile)
    mix[...] = tile

    @pl.when(r > 0)
    def _():
        pltpu.make_async_copy(got_low, got_low, recv_static.at[0]).wait()
        put_rows(3, 0, got_low[0])
        put_rows(3, 1, got_low[1])
        put_rows(0, 1, got_low[2])

    @pl.when(r < R - 1)
    def _():
        pltpu.make_async_copy(got_high, got_high, recv_static.at[1]).wait()
        put_rows(3, 10, got_high[0])
        put_rows(3, 11, got_high[1])

    @pl.when(g > 0)
    def _():
        pltpu.make_async_copy(got_y, got_y, recv_static.at[2]).wait()

        def unpack_level(z, carry):
            q[1, z, 2:10, :] = jnp.where(
                lane == 1, pltpu.roll(got_y[...], lax.rem(129 - z, 128), 1), q[1, z, 2:10, :])
            return carry

        lax.fori_loop(0, NZ, unpack_level, 0)

    sea = q[3]
    follow = (pltpu.roll(sea, 15, 1), pltpu.roll(sea, 127, 2),
              jnp.concatenate([sea[1:], jnp.zeros((1, 16, 128), jnp.float32)], 0))
    for k in range(3):
        opened, c = sea * follow[k], q[k]
        dc[3 * k] = opened
        dc[3 * k + 1] = c * opened
        dc[3 * k + 2] = jnp.where(c > 0, 0.5, -0.5) - 0.5 * c
    dc[SEA] = sea

    def spread_one(n, carry):
        e, zr = n // 8, n % 8
        d = dc.reshape(NC * NZ * 16, 128)[pl.ds(zr * 16 + e, NC * 4, stride=128), :]
        high = d.astype(jnp.bfloat16).astype(jnp.float32)
        rest = d - high
        mid = rest.astype(jnp.bfloat16).astype(jnp.float32)
        low = rest - mid
        stack = jnp.concatenate([high, mid, low, jnp.zeros((8, 128), jnp.float32)], axis=0)
        turned = stack.T[:48].astype(jnp.bfloat16)
        for k in range(NC):
            wide = jnp.dot(turned, spread[k], preferred_element_type=jnp.float32)
            coef.at[k].reshape(XE * YE * 8, 128)[pl.ds(e * YE * 8 + zr, YE, stride=8), :] = wide[:YE]
        return carry

    lax.fori_loop(0, XE * 8, spread_one, 0)

    def x_halo(f, s, do):
        @pl.when(r > 0)
        def _():
            do(pltpu.make_async_remote_copy(
                src_ref=f.at[2:4, 2:34], dst_ref=f.at[10:12, 2:34],
                send_sem=send_halo.at[s, 0], recv_sem=recv_x.at[s, 1],
                device_id=(r - 1, g), device_id_type=MESH))

        @pl.when(r < R - 1)
        def _():
            do(pltpu.make_async_remote_copy(
                src_ref=f.at[8:10, 2:34], dst_ref=f.at[0:2, 2:34],
                send_sem=send_halo.at[s, 1], recv_sem=recv_x.at[s, 0],
                device_id=(r + 1, g), device_id_type=MESH))

    def y_halo(f, s, do):
        @pl.when(g > 0)
        def _():
            do(pltpu.make_async_remote_copy(
                src_ref=f.at[2:10, 2:4], dst_ref=f.at[2:10, 34:36],
                send_sem=send_halo.at[s, 2], recv_sem=recv_y.at[s, 1],
                device_id=(r, g - 1), device_id_type=MESH))

        @pl.when(g < G - 1)
        def _():
            do(pltpu.make_async_remote_copy(
                src_ref=f.at[2:10, 32:34], dst_ref=f.at[2:10, 0:2],
                send_sem=send_halo.at[s, 3], recv_sem=recv_y.at[s, 0],
                device_id=(r, g + 1), device_id_type=MESH))

    def arrive(f, s):
        def landed(ref, sem):
            pltpu.make_async_copy(ref, ref, sem).wait()

        @pl.when(r > 0)
        def _():
            landed(f.at[0:2, 2:34], recv_x.at[s, 0])

        @pl.when(r < R - 1)
        def _():
            landed(f.at[10:12, 2:34], recv_x.at[s, 1])

        @pl.when(g > 0)
        def _():
            landed(f.at[2:10, 0:2], recv_y.at[s, 0])

        @pl.when(g < G - 1)
        def _():
            landed(f.at[2:10, 34:36], recv_y.at[s, 1])

    for h, quad in enumerate(QUADS):
        some = rb.at[h, :, 0:2 * (G - 1)]
        pltpu.make_async_copy(some, some, recv_in.at[h]).wait()
        pltpu.make_async_copy(sb.at[g, h], rb.at[h, :, pl.ds(2 * g, 2)], local_sem.at[h]).wait()

        def turn(zr, carry, h=h, quad=quad):
            turned = rb2[pl.ds(h * 4 * NT * 8 + zr, 128, stride=8), :].T
            for n, x in enumerate(quad):
                fa2[pl.ds(((x + 2) * YE + 2) * 8 + zr, YB, stride=8), :] = turned[n * YB:(n + 1) * YB]
            return carry

        lax.fori_loop(0, 8, turn, 0)
        if h == 0:
            x_halo(fa, 0, begin)
    y_halo(fa, 0, begin)

    def z_edges(f):
        def rows(ref, k):
            return ref.reshape(ref.shape[0] * ref.shape[1] * 8, 128)[pl.ds(2 * YE * 8 + k, X * YE, stride=8), :]

        def static(k, n):
            return rows(coef.at[k], n)

        next0 = pltpu.roll(rows(f, 0), 96, 1)
        next1 = pltpu.roll(rows(f, 1), 96, 1)
        last = rows(f, 7)
        jump = (next0 - last) * static(OZ, 7)
        slope = minmod((last - rows(f, 6)) * static(OZ, 6), jump)
        slope_next = minmod(jump, (next1 - next0) * pltpu.roll(static(OZ, 0), 96, 1))
        flux = face(last, next0, slope, slope_next, static(CZ, 7), static(QZ, 7)) - mix[7:8, :] * jump
        for n, k, v in ((0, 7, next0), (0, 0, pltpu.roll(jump, 32, 1)), (1, 7, slope_next), (1, 0, pltpu.roll(flux, 32, 1))):
            edge.at[n].reshape(X * YE * 8, 128)[pl.ds(k, X * YE, stride=8), :] = v

    def advect(f):
        z_edges(f)

        def cells(e):
            return f[2:10, e]

        def along(k, e):
            return coef[k, 2:10, e]

        f1, f2 = cells(1), cells(2)
        j0 = (f1 - cells(0)) * along(OY, 0)
        j1 = (f2 - f1) * along(OY, 1)
        j2 = (cells(3) - f2) * along(OY, 2)
        s1, s2 = minmod(j0, j1), minmod(j1, j2)
        start = (j2, s2, face(f1, f2, s1, s2, along(CY, 1), along(QY, 1)))

        def column(y, carry):
            jump, slope, before = carry
            e = y + 2
            fx = f[:, e]
            inner, following = fx[2:10], cells(e + 1)
            jump_next = (cells(e + 2) - following) * along(OY, e + 1)
            slope_next = minmod(jump, jump_next)
            after = face(inner, following, slope, slope_next, along(CY, e), along(QY, e))
            total = inner - (after - before)
            jx = (fx[1:] - fx[:-1]) * coef[OX, 0:11, e]
            sx = minmod(jx[:-1], jx[1:])
            flux = face(fx[1:10], fx[2:11], sx[:-1], sx[1:], coef[CX, 1:10, e], coef[QX, 1:10, e])
            total = total - (flux[1:] - flux[:-1])
            edge0, edge1 = edge[0, :, e], edge[1, :, e]
            below = jnp.where(row == 7, edge0, pltpu.roll(inner, 7, 1))
            jz = (below - inner) * along(OZ, e)
            sz = minmod(jnp.where(row == 0, edge0, pltpu.roll(jz, 1, 1)), jz)
            sz_next = jnp.where(row == 7, edge1, pltpu.roll(sz, 7, 1))
            down = face(inner, below, sz, sz_next, along(CZ, e), along(QZ, e)) - mix[...] * jz
            adv[:, y] = total - (down - jnp.where(row == 0, edge1, pltpu.roll(down, 1, 1)))
            return jump_next, slope_next, after

        lax.fori_loop(0, YB, column, start)

    def react(x, f):
        a = adv[x]
        att = 0.05 + 0.1 * a * a
        inc = att
        for step in (1, 2, 4):
            inc = inc + jnp.where(row >= step, pltpu.roll(inc, step, 1), 0.0)
        exc = (inc - att).reshape(256, 128)
        ahead = jnp.dot(jnp.concatenate(halves(exc), axis=1), own_mat[...], preferred_element_type=jnp.float32)
        past = jnp.dot(jnp.concatenate(halves(inc.reshape(256, 128)), axis=1), past_mat[...],
                       preferred_element_type=jnp.float32).reshape(YB, 8, 128)
        light = jnp.exp(-(ahead.reshape(YB, 8, 128) + past[:, 7:8, :]))
        both = jnp.dot(jnp.concatenate(halves(jnp.tanh(a).reshape(256, 128)), axis=1), wmat[...],
                       preferred_element_type=jnp.float32)
        response = (both[:, :128] + both[:, 128:]).reshape(YB, 8, 128)
        f[x + 2, 2:34] = a + coef[SEA, x + 2, 2:34] * ((0.5 + light) * response)

    arrive(fa, 0)
    advect(fa)
    for h, quad in enumerate(QUADS):
        for x in quad:
            react(x, fb)
        if h == 0:
            x_halo(fb, 1, begin)
    y_halo(fb, 1, begin)
    arrive(fb, 1)
    advect(fb)
    static_halo(lambda copy: copy.wait_send())
    for s, f in ((0, fa), (1, fb)):
        x_halo(f, s, lambda copy: copy.wait_send())
        y_halo(f, s, lambda copy: copy.wait_send())

    for h, quad in enumerate(QUADS):
        for x in quad:
            react(x, fa)

        def turn_back(zr, carry, h=h, quad=quad):
            stack = [fa2[pl.ds(((x + 2) * YE + 2) * 8 + zr, YB, stride=8), :] for x in quad]
            so2[pl.ds(h * 4 * NT * 8 + zr, 128, stride=8), :] = jnp.concatenate(stack, axis=0).T
            return carry

        lax.fori_loop(0, 8, turn_back, 0)

        def send_back(d, carry, h=h):
            to = lax.rem(g + d, G)
            pltpu.make_async_remote_copy(
                src_ref=so.at[h, :, pl.ds(2 * to, 2)], dst_ref=ro.at[h, g],
                send_sem=send_out.at[h], recv_sem=recv_out.at[h],
                device_id=(r, to), device_id_type=MESH).start()
            return carry

        lax.fori_loop(1, G, send_back, 0)
        pltpu.make_async_copy(so.at[h, :, pl.ds(2 * g, 2)], ro.at[h, g], local_sem.at[2 + h]).start()

    for h, quad in enumerate(QUADS):
        some = ro.at[h, 0:G - 1]
        pltpu.make_async_copy(some, some, recv_out.at[h]).wait()
        pltpu.make_async_copy(so.at[h, :, pl.ds(2 * g, 2)], ro.at[h, g], local_sem.at[2 + h]).wait()

        def restore(n, carry, h=h, quad=quad):
            t, zq = n // 4, n % 4
            for j in range(4):
                v = block_swap([ro[h, 4 * j + i, zq, t] for i in range(4)], lane)
                for x, b in zip(quad, v):
                    tout[j, pl.ds((t * NZ + zq * 8) * X + x, 8, stride=8), :] = b
            return carry

        lax.fori_loop(0, 8, restore, 0)

    for j in range(4):
        put(j).start()
    for h in range(2):
        some = sb.at[0:G - 1, h]
        pltpu.make_async_copy(some, some, send_in.at[h]).wait()
        some = ro.at[h, 0:G - 1]
        pltpu.make_async_copy(some, some, send_out.at[h]).wait()
    for j in range(4):
        put(j).wait()


def shards(tracers, velocity, sea_mask, coupling, mixing):
    anywhere = pl.BlockSpec(memory_space=pl.ANY)
    vmem = pl.BlockSpec(memory_space=pltpu.VMEM)
    f32 = jnp.float32
    dma = pltpu.SemaphoreType.DMA
    out = pl.pallas_call(
        kernel,
        out_shape=jax.ShapeDtypeStruct((2 * NZ * X, G * YB), f32),
        in_specs=[anywhere] * 3 + [vmem, pl.BlockSpec(memory_space=pltpu.SMEM)],
        out_specs=anywhere,
        scratch_shapes=[
            pltpu.VMEM((NC, 128, 128), jnp.bfloat16),
            pltpu.VMEM((256, 128), jnp.bfloat16),
            pltpu.VMEM((256, 128), jnp.bfloat16),
            pltpu.VMEM((8, 128), f32),
            pltpu.VMEM((256, 256), jnp.bfloat16),
            pltpu.VMEM((3, NZ, X, YB), f32),
            pltpu.VMEM((3, NZ, X, 128), jnp.int32),
            pltpu.VMEM((4, NZ, 16, 128), f32),
            pltpu.VMEM((NC, NZ, 16, 128), f32),
            pltpu.VMEM((3, NZ, 128), f32),
            pltpu.VMEM((2, NZ, 128), f32),
            pltpu.VMEM((8, 128), f32),
            pltpu.VMEM((3, NZ, 128), f32),
            pltpu.VMEM((2, NZ, 128), f32),
            pltpu.VMEM((8, 128), f32),
            pltpu.VMEM((4, 2 * NZ * X, 128), f32),
            pltpu.VMEM((4, 2 * NZ * X, 128), f32),
            pltpu.VMEM((G, 2, 4, 2, 8, 128), f32),
            pltpu.VMEM((2, 4, NT, 8, 128), f32),
            pltpu.VMEM((XE, YE, 8, 128), f32),
            pltpu.VMEM((XE, YE, 8, 128), f32),
            pltpu.VMEM((X, YB, 8, 128), f32),
            pltpu.VMEM((2, X, YE, 8, 128), f32),
            pltpu.VMEM((NC, XE, YE, 8, 128), f32),
            pltpu.VMEM((2, 4, NT, 8, 128), f32),
            pltpu.VMEM((2, G, 4, 2, 8, 128), f32),
            dma((4,)), dma((3,)), dma((3,)),
            dma((4,)), dma((4,)), dma((2,)), dma((2,)), dma((2, 4)), dma((2, 2)), dma((2, 2)), dma((2,)), dma((2,)), dma((4,)),
        ],
        compiler_params=pltpu.CompilerParams(
            collective_id=0, has_side_effects=True, vmem_limit_bytes=48 * 2**20),
    )(tracers.reshape(2 * NZ * X, G * YB), velocity, sea_mask, coupling, mixing)
    return out.reshape(tracers.shape)


def solution(mesh):
    placed = (
        P("group", None, "region", None),
        P(None, None, "region", "group"),
        P(None, "region", None),
        P(),
        P(),
    )
    return jax.shard_map(
        shards,
        mesh=mesh,
        in_specs=placed,
        out_specs=P("group", None, "region", None),
        check_vma=False,
    )
```

```python
import jax
import jax.numpy as jnp
from jax import lax
from jax.experimental import pallas as pl
from jax.experimental.pallas import tpu as pltpu
from jax.sharding import PartitionSpec as P

MESH = pl.DeviceIdType.MESH
STEPS = 2
NZ, NT, X, YB, G, R = 32, 32, 8, 32, 16, 8
XE, YE = X + 4, YB + 4
QUADS = ((0, 1, 6, 7), (2, 3, 4, 5))
NC = 5
CX, CY, CZ, SEA, OZ = range(NC)


def minmod(a, b):
    return jnp.maximum(jnp.minimum(a, b), jnp.minimum(jnp.maximum(a, b), 0.0))


def face(cell, following, slope, slope_following, c):
    forward = c > 0
    q = jnp.where(forward, 0.5, -0.5) - 0.5 * c
    return c * (jnp.where(forward, cell, following) + q * jnp.where(forward, slope, slope_following))


def halves(value):
    high = value.astype(jnp.bfloat16)
    return high, (value - high.astype(jnp.float32)).astype(jnp.bfloat16)


def block_swap(v, lane):
    low, even = lane < 64, (lane // 32) % 2 == 0
    axis = v[0].ndim - 1
    a = [None] * 4
    for n in (0, 1):
        a[n] = jnp.where(low, v[n], pltpu.roll(v[n + 2], 64, axis))
        a[n + 2] = jnp.where(low, pltpu.roll(v[n], 64, axis), v[n + 2])
    b = [None] * 4
    for n in (0, 2):
        b[n] = jnp.where(even, a[n], pltpu.roll(a[n + 1], 32, axis))
        b[n + 1] = jnp.where(even, pltpu.roll(a[n], 96, axis), a[n + 1])
    return b


def kernel(tr, velocity, mask, coupling, mixing, out,
           spread, stacked, own_mat, past_mat, mix, wmat, vel, sea3, q, dc, pack_up, pack_down, pack_y, got_low, got_high, got_y,
           tin, tout, sb, rb, fa, fb, adv, edge, coef, so, ro,
           statics_in, send_static, recv_static,
           tiles_in, tiles_out, send_in, recv_in, send_halo, recv_x, recv_y, send_out, recv_out, local_sem):
    r, g = lax.axis_index("region"), lax.axis_index("group")
    lane = lax.broadcasted_iota(jnp.int32, (8, 128), 1)
    row = lax.broadcasted_iota(jnp.int32, (8, 128), 0)
    fa2, fb2 = fa.reshape(XE * YE * 8, 128), fb.reshape(XE * YE * 8, 128)
    rb2, so2 = rb.reshape(2 * 4 * NT * 8, 128), so.reshape(2 * 4 * NT * 8, 128)

    def fetch(j):
        return pltpu.make_async_copy(tr.at[:, pl.ds(j * 128, 128)], tin.at[j], tiles_in.at[j])

    def put(j):
        return pltpu.make_async_copy(tout.at[j], out.at[:, pl.ds(j * 128, 128)], tiles_out.at[j])

    at = lax.div(g, 4)
    spots = (at, jnp.maximum(at - 1, 0), jnp.minimum(at + 1, 3))
    fetches = [pltpu.make_async_copy(velocity, vel, statics_in.at[0])]
    for n, spot in enumerate(spots):
        fetches.append(pltpu.make_async_copy(
            mask.at[:, :, pl.ds(pl.multiple_of(spot * 128, 128), 128)], sea3.at[n], statics_in.at[n + 1]))
    for copy in fetches:
        copy.start()
    for j in range(4):
        fetch(j).start()

    for f in (fa, fb):
        f[0:2, 2:34] = jnp.zeros((2, 32, 8, 128), jnp.float32)
        f[10:12, 2:34] = jnp.zeros((2, 32, 8, 128), jnp.float32)
        f[2:10, 0:2] = jnp.zeros((8, 2, 8, 128), jnp.float32)
        f[2:10, 34:36] = jnp.zeros((8, 2, 8, 128), jnp.float32)

    barrier = pltpu.get_barrier_semaphore()

    def greet(d, carry):
        pl.semaphore_signal(barrier, inc=1, device_id=(r, lax.rem(g + d, G)), device_id_type=MESH)
        return carry

    lax.fori_loop(1, G, greet, 0)

    @pl.when(r > 0)
    def _():
        pl.semaphore_signal(barrier, inc=1, device_id=(r - 1, g), device_id_type=MESH)

    @pl.when(r < R - 1)
    def _():
        pl.semaphore_signal(barrier, inc=1, device_id=(r + 1, g), device_id_type=MESH)

    q[...] = jnp.zeros(q.shape, jnp.float32)
    for copy in fetches:
        copy.wait()
    for k in range(3):
        q[k, :, 2:10, 2:34] = vel[k]
    place = lax.rem(g, 4)
    has_left = jnp.minimum(at, 1).astype(jnp.float32)
    has_right = jnp.minimum(3 - at, 1).astype(jnp.float32)
    centre = sea3[0].astype(jnp.float32)
    left = sea3[1].astype(jnp.float32) * has_left
    right = sea3[2].astype(jnp.float32) * has_right
    centre = jnp.where(jnp.logical_and(lane >= 126, place == 0), left, centre)
    centre = jnp.where(jnp.logical_and(lane < 2, place == 3), right, centre)
    q[3, :, 2:10, :] = pltpu.roll(centre, lax.rem(130 - 32 * place, 128), 2)

    def level_rows(k, e):
        return q.at[k].reshape(NZ * 16, 128)[pl.ds(e, NZ, stride=16), :]

    def put_rows(k, e, value):
        q.at[k].reshape(NZ * 16, 128)[pl.ds(e, NZ, stride=16), :] = value

    pack_up[0], pack_up[1], pack_up[2] = level_rows(3, 8), level_rows(3, 9), level_rows(0, 9)
    pack_down[0], pack_down[1] = level_rows(3, 2), level_rows(3, 3)

    def pack_level(z, p):
        return jnp.where(lane == z, pltpu.roll(q[1, z, 2:10, :], lax.rem(z + 95, 128), 1), p)

    pack_y[...] = lax.fori_loop(0, NZ, pack_level, jnp.zeros((8, 128), jnp.float32))

    for j in range(4):
        fetch(j).wait()

    def begin(copy):
        copy.start()

    def static_halo(do):
        @pl.when(r < R - 1)
        def _():
            do(pltpu.make_async_remote_copy(
                src_ref=pack_up, dst_ref=got_low, send_sem=send_static.at[0], recv_sem=recv_static.at[0],
                device_id=(r + 1, g), device_id_type=MESH))

        @pl.when(r > 0)
        def _():
            do(pltpu.make_async_remote_copy(
                src_ref=pack_down, dst_ref=got_high, send_sem=send_static.at[1], recv_sem=recv_static.at[1],
                device_id=(r - 1, g), device_id_type=MESH))

        @pl.when(g < G - 1)
        def _():
            do(pltpu.make_async_remote_copy(
                src_ref=pack_y, dst_ref=got_y, send_sem=send_static.at[2], recv_sem=recv_static.at[2],
                device_id=(r, g + 1), device_id_type=MESH))

    for h, quad in enumerate(QUADS):
        def regroup(n, carry, h=h, quad=quad):
            t, zq = n // 4, n % 4
            for j in range(4):
                v = [tin[j, pl.ds((t * NZ + zq * 8) * X + x, 8, stride=8), :] for x in quad]
                for i, b in enumerate(block_swap(v, lane)):
                    sb[4 * j + i, h, zq, t] = b
            return carry

        lax.fori_loop(0, 8, regroup, 0)
        if h == 0:
            pl.semaphore_wait(barrier, G - 1 + jnp.minimum(r, 1) + jnp.minimum(R - 1 - r, 1))
            static_halo(begin)

        def send(d, carry, h=h):
            to = lax.rem(g + d, G)
            pltpu.make_async_remote_copy(
                src_ref=sb.at[to, h], dst_ref=rb.at[h, :, pl.ds(2 * g, 2)],
                send_sem=send_in.at[h], recv_sem=recv_in.at[h],
                device_id=(r, to), device_id_type=MESH).start()
            return carry

        lax.fori_loop(1, G, send, 0)
        pltpu.make_async_copy(sb.at[g, h], rb.at[h, :, pl.ds(2 * g, 2)], local_sem.at[h]).start()

    def iota(shape, axis):
        return lax.broadcasted_iota(jnp.int32, shape, axis)

    square = (128, 128)
    block_in, block_out = iota(square, 0) // 32, iota(square, 1) // 32
    for level in range(4):
        for k in range(NC):
            base = 32 * level + (24 + 4 * (k - 3) if k >= 3 else 4 * k)
            place_k = iota(square, 0) - (base + block_out)
            hit = place_k == 0 if k >= 3 else jnp.logical_or(place_k == 0, place_k == 12)
            spread[level, k] = jnp.where(hit, 1.0, 0.0).astype(jnp.bfloat16)
    first = iota(square, 0) % 32 == 0
    own = jnp.where(jnp.logical_and(first, block_in == block_out), 1.0, 0.0).astype(jnp.bfloat16)
    past = jnp.where(jnp.logical_and(first, block_in < block_out), 1.0, 0.0).astype(jnp.bfloat16)
    own_mat[...] = jnp.concatenate([own, own], 0)
    past_mat[...] = jnp.concatenate([past, past], 0)
    across = jnp.concatenate([coupling[...].T] * 4, 1)
    weights = jnp.where(block_in == block_out, jnp.concatenate([across] * 4, 0), 0.0)
    high, low = halves(weights)
    wmat[...] = jnp.concatenate([jnp.concatenate([high, low], 1), jnp.concatenate([high, jnp.zeros_like(low)], 1)], 0)
    tile = jnp.zeros((8, 128), jnp.float32)
    for z in range(NZ):
        tile = jnp.where(jnp.logical_and(row == z % 8, lane // 32 == z // 8), mixing[z], tile)
    mix[...] = tile

    @pl.when(r > 0)
    def _():
        pltpu.make_async_copy(got_low, got_low, recv_static.at[0]).wait()
        put_rows(3, 0, got_low[0])
        put_rows(3, 1, got_low[1])
        put_rows(0, 1, got_low[2])

    @pl.when(r < R - 1)
    def _():
        pltpu.make_async_copy(got_high, got_high, recv_static.at[1]).wait()
        put_rows(3, 10, got_high[0])
        put_rows(3, 11, got_high[1])

    @pl.when(g > 0)
    def _():
        pltpu.make_async_copy(got_y, got_y, recv_static.at[2]).wait()

        def unpack_level(z, carry):
            q[1, z, 2:10, :] = jnp.where(
                lane == 1, pltpu.roll(got_y[...], lax.rem(129 - z, 128), 1), q[1, z, 2:10, :])
            return carry

        lax.fori_loop(0, NZ, unpack_level, 0)

    sea = q[3]
    follow = (pltpu.roll(sea, 15, 1), pltpu.roll(sea, 127, 2),
              jnp.concatenate([sea[1:], jnp.zeros((1, 16, 128), jnp.float32)], 0))
    for k in range(3):
        opened = sea * follow[k]
        c = q[k] * opened
        high = c.astype(jnp.bfloat16).astype(jnp.float32)
        dc[k] = high
        dc[3 + k] = c - high
    dc[6] = sea
    dc[7] = opened

    def stack_one(e, carry):
        for half in range(2):
            rows = [dc.reshape(8 * NZ * 16, 128)[pl.ds((half * 4 + n) * 16 + e, 32, stride=128), :] for n in range(4)]
            stacked[half, pl.ds(pl.multiple_of(e * 48, 16), 48), :] = (
                jnp.concatenate(rows, axis=0).T[:48].astype(jnp.bfloat16))
        return carry

    lax.fori_loop(0, XE, stack_one, 0)

    def spread_one(zr, carry):
        for k in range(NC):
            wide = jnp.dot(stacked[zr // 4], spread[zr % 4, k], preferred_element_type=jnp.float32)
            for e in range(XE):
                coef.at[k].reshape(XE * YE * 8, 128)[pl.ds(e * YE * 8 + zr, YE, stride=8), :] = wide[e * 48:e * 48 + YE]
        return carry

    lax.fori_loop(0, 8, spread_one, 0)

    def x_halo(f, s, do):
        @pl.when(r > 0)
        def _():
            do(pltpu.make_async_remote_copy(
                src_ref=f.at[2:4, 2:34], dst_ref=f.at[10:12, 2:34],
                send_sem=send_halo.at[s, 0], recv_sem=recv_x.at[s, 1],
                device_id=(r - 1, g), device_id_type=MESH))

        @pl.when(r < R - 1)
        def _():
            do(pltpu.make_async_remote_copy(
                src_ref=f.at[8:10, 2:34], dst_ref=f.at[0:2, 2:34],
                send_sem=send_halo.at[s, 1], recv_sem=recv_x.at[s, 0],
                device_id=(r + 1, g), device_id_type=MESH))

    def y_halo(f, s, do):
        @pl.when(g > 0)
        def _():
            do(pltpu.make_async_remote_copy(
                src_ref=f.at[2:10, 2:4], dst_ref=f.at[2:10, 34:36],
                send_sem=send_halo.at[s, 2], recv_sem=recv_y.at[s, 1],
                device_id=(r, g - 1), device_id_type=MESH))

        @pl.when(g < G - 1)
        def _():
            do(pltpu.make_async_remote_copy(
                src_ref=f.at[2:10, 32:34], dst_ref=f.at[2:10, 0:2],
                send_sem=send_halo.at[s, 3], recv_sem=recv_y.at[s, 0],
                device_id=(r, g + 1), device_id_type=MESH))

    def arrive(f, s):
        def landed(ref, sem):
            pltpu.make_async_copy(ref, ref, sem).wait()

        @pl.when(r > 0)
        def _():
            landed(f.at[0:2, 2:34], recv_x.at[s, 0])

        @pl.when(r < R - 1)
        def _():
            landed(f.at[10:12, 2:34], recv_x.at[s, 1])

        @pl.when(g > 0)
        def _():
            landed(f.at[2:10, 0:2], recv_y.at[s, 0])

        @pl.when(g < G - 1)
        def _():
            landed(f.at[2:10, 34:36], recv_y.at[s, 1])

    for h, quad in enumerate(QUADS):
        some = rb.at[h, :, 0:2 * (G - 1)]
        pltpu.make_async_copy(some, some, recv_in.at[h]).wait()
        pltpu.make_async_copy(sb.at[g, h], rb.at[h, :, pl.ds(2 * g, 2)], local_sem.at[h]).wait()

        def turn(zr, carry, h=h, quad=quad):
            turned = rb2[pl.ds(h * 4 * NT * 8 + zr, 128, stride=8), :].T
            for n, x in enumerate(quad):
                fa2[pl.ds(((x + 2) * YE + 2) * 8 + zr, YB, stride=8), :] = turned[n * YB:(n + 1) * YB]
            return carry

        lax.fori_loop(0, 8, turn, 0)
        if h == 0:
            x_halo(fa, 0, begin)
    y_halo(fa, 0, begin)

    def z_edges(f):
        def rows(ref, k):
            return ref.reshape(ref.shape[0] * ref.shape[1] * 8, 128)[pl.ds(2 * YE * 8 + k, X * YE, stride=8), :]

        def static(k, n):
            return rows(coef.at[k], n)

        next0 = pltpu.roll(rows(f, 0), 96, 1)
        next1 = pltpu.roll(rows(f, 1), 96, 1)
        last = rows(f, 7)
        jump = (next0 - last) * static(OZ, 7)
        slope = minmod((last - rows(f, 6)) * static(OZ, 6), jump)
        slope_next = minmod(jump, (next1 - next0) * pltpu.roll(static(OZ, 0), 96, 1))
        flux = face(last, next0, slope, slope_next, static(CZ, 7)) - mix[7:8, :] * jump
        for n, k, v in ((0, 7, next0), (0, 0, pltpu.roll(jump, 32, 1)), (1, 7, slope_next), (1, 0, pltpu.roll(flux, 32, 1))):
            edge.at[n].reshape(X * YE * 8, 128)[pl.ds(k, X * YE, stride=8), :] = v

    def advect(f):
        z_edges(f)

        def cells(e):
            return f[2:10, e]

        def along(k, e):
            return coef[k, 2:10, e]

        f1, f2 = cells(1), cells(2)
        def open_y(e):
            return along(SEA, e) * along(SEA, e + 1)

        j0 = (f1 - cells(0)) * open_y(0)
        j1 = (f2 - f1) * open_y(1)
        j2 = (cells(3) - f2) * open_y(2)
        s1, s2 = minmod(j0, j1), minmod(j1, j2)
        start = (j2, s2, face(f1, f2, s1, s2, along(CY, 1)))

        def column(y, carry):
            jump, slope, before = carry
            e = y + 2
            fx = f[:, e]
            inner, following = fx[2:10], cells(e + 1)
            jump_next = (cells(e + 2) - following) * open_y(e + 1)
            slope_next = minmod(jump, jump_next)
            after = face(inner, following, slope, slope_next, along(CY, e))
            total = inner - (after - before)
            sea_x = coef[SEA, :, e]
            jx = (fx[1:] - fx[:-1]) * (sea_x[1:] * sea_x[:-1])
            sx = minmod(jx[:-1], jx[1:])
            flux = face(fx[1:10], fx[2:11], sx[:-1], sx[1:], coef[CX, 1:10, e])
            total = total - (flux[1:] - flux[:-1])
            edge0, edge1 = edge[0, :, e], edge[1, :, e]
            below = jnp.where(row == 7, edge0, pltpu.roll(inner, 7, 1))
            jz = (below - inner) * along(OZ, e)
            sz = minmod(jnp.where(row == 0, edge0, pltpu.roll(jz, 1, 1)), jz)
            sz_next = jnp.where(row == 7, edge1, pltpu.roll(sz, 7, 1))
            down = face(inner, below, sz, sz_next, along(CZ, e)) - mix[...] * jz
            adv[:, y] = total - (down - jnp.where(row == 0, edge1, pltpu.roll(down, 1, 1)))
            return jump_next, slope_next, after

        lax.fori_loop(0, YB, column, start)

    def react(x, f):
        a = adv[x]
        att = 0.05 + 0.1 * a * a
        inc = att
        for step in (1, 2, 4):
            inc = inc + jnp.where(row >= step, pltpu.roll(inc, step, 1), 0.0)
        exc = (inc - att).reshape(256, 128)
        ahead = jnp.dot(jnp.concatenate(halves(exc), axis=1), own_mat[...], preferred_element_type=jnp.float32)
        past = jnp.dot(jnp.concatenate(halves(inc.reshape(256, 128)), axis=1), past_mat[...],
                       preferred_element_type=jnp.float32).reshape(YB, 8, 128)
        light = jnp.exp(-(ahead.reshape(YB, 8, 128) + past[:, 7:8, :]))
        both = jnp.dot(jnp.concatenate(halves(jnp.tanh(a).reshape(256, 128)), axis=1), wmat[...],
                       preferred_element_type=jnp.float32)
        response = (both[:, :128] + both[:, 128:]).reshape(YB, 8, 128)
        f[x + 2, 2:34] = a + coef[SEA, x + 2, 2:34] * ((0.5 + light) * response)

    arrive(fa, 0)
    advect(fa)
    for h, quad in enumerate(QUADS):
        for x in quad:
            react(x, fb)
        if h == 0:
            x_halo(fb, 1, begin)
    y_halo(fb, 1, begin)
    arrive(fb, 1)
    advect(fb)
    static_halo(lambda copy: copy.wait_send())
    for s, f in ((0, fa), (1, fb)):
        x_halo(f, s, lambda copy: copy.wait_send())
        y_halo(f, s, lambda copy: copy.wait_send())

    for h, quad in enumerate(QUADS):
        for x in quad:
            react(x, fa)

        def turn_back(zr, carry, h=h, quad=quad):
            stack = [fa2[pl.ds(((x + 2) * YE + 2) * 8 + zr, YB, stride=8), :] for x in quad]
            so2[pl.ds(h * 4 * NT * 8 + zr, 128, stride=8), :] = jnp.concatenate(stack, axis=0).T
            return carry

        lax.fori_loop(0, 8, turn_back, 0)

        def send_back(d, carry, h=h):
            to = lax.rem(g + d, G)
            pltpu.make_async_remote_copy(
                src_ref=so.at[h, :, pl.ds(2 * to, 2)], dst_ref=ro.at[h, g],
                send_sem=send_out.at[h], recv_sem=recv_out.at[h],
                device_id=(r, to), device_id_type=MESH).start()
            return carry

        lax.fori_loop(1, G, send_back, 0)
        pltpu.make_async_copy(so.at[h, :, pl.ds(2 * g, 2)], ro.at[h, g], local_sem.at[2 + h]).start()

    for h, quad in enumerate(QUADS):
        some = ro.at[h, 0:G - 1]
        pltpu.make_async_copy(some, some, recv_out.at[h]).wait()
        pltpu.make_async_copy(so.at[h, :, pl.ds(2 * g, 2)], ro.at[h, g], local_sem.at[2 + h]).wait()

        def restore(n, carry, h=h, quad=quad):
            t, zq = n // 4, n % 4
            for j in range(4):
                v = block_swap([ro[h, 4 * j + i, zq, t] for i in range(4)], lane)
                for x, b in zip(quad, v):
                    tout[j, pl.ds((t * NZ + zq * 8) * X + x, 8, stride=8), :] = b
            return carry

        lax.fori_loop(0, 8, restore, 0)

    for j in range(4):
        put(j).start()
    for h in range(2):
        some = sb.at[0:G - 1, h]
        pltpu.make_async_copy(some, some, send_in.at[h]).wait()
        some = ro.at[h, 0:G - 1]
        pltpu.make_async_copy(some, some, send_out.at[h]).wait()
    for j in range(4):
        put(j).wait()


def shards(tracers, velocity, sea_mask, coupling, mixing):
    anywhere = pl.BlockSpec(memory_space=pl.ANY)
    vmem = pl.BlockSpec(memory_space=pltpu.VMEM)
    f32 = jnp.float32
    dma = pltpu.SemaphoreType.DMA
    out = pl.pallas_call(
        kernel,
        out_shape=jax.ShapeDtypeStruct((2 * NZ * X, G * YB), f32),
        in_specs=[anywhere] * 3 + [vmem, pl.BlockSpec(memory_space=pltpu.SMEM)],
        out_specs=anywhere,
        scratch_shapes=[
            pltpu.VMEM((4, NC, 128, 128), jnp.bfloat16),
            pltpu.VMEM((2, XE * 48, 128), jnp.bfloat16),
            pltpu.VMEM((256, 128), jnp.bfloat16),
            pltpu.VMEM((256, 128), jnp.bfloat16),
            pltpu.VMEM((8, 128), f32),
            pltpu.VMEM((256, 256), jnp.bfloat16),
            pltpu.VMEM((3, NZ, X, YB), f32),
            pltpu.VMEM((3, NZ, X, 128), jnp.int32),
            pltpu.VMEM((4, NZ, 16, 128), f32),
            pltpu.VMEM((8, NZ, 16, 128), f32),
            pltpu.VMEM((3, NZ, 128), f32),
            pltpu.VMEM((2, NZ, 128), f32),
            pltpu.VMEM((8, 128), f32),
            pltpu.VMEM((3, NZ, 128), f32),
            pltpu.VMEM((2, NZ, 128), f32),
            pltpu.VMEM((8, 128), f32),
            pltpu.VMEM((4, 2 * NZ * X, 128), f32),
            pltpu.VMEM((4, 2 * NZ * X, 128), f32),
            pltpu.VMEM((G, 2, 4, 2, 8, 128), f32),
            pltpu.VMEM((2, 4, NT, 8, 128), f32),
            pltpu.VMEM((XE, YE, 8, 128), f32),
            pltpu.VMEM((XE, YE, 8, 128), f32),
            pltpu.VMEM((X, YB, 8, 128), f32),
            pltpu.VMEM((2, X, YE, 8, 128), f32),
            pltpu.VMEM((NC, XE, YE, 8, 128), f32),
            pltpu.VMEM((2, 4, NT, 8, 128), f32),
            pltpu.VMEM((2, G, 4, 2, 8, 128), f32),
            dma((4,)), dma((3,)), dma((3,)),
            dma((4,)), dma((4,)), dma((2,)), dma((2,)), dma((2, 4)), dma((2, 2)), dma((2, 2)), dma((2,)), dma((2,)), dma((4,)),
        ],
        compiler_params=pltpu.CompilerParams(
            collective_id=0, has_side_effects=True, vmem_limit_bytes=48 * 2**20),
    )(tracers.reshape(2 * NZ * X, G * YB), velocity, sea_mask, coupling, mixing)
    return out.reshape(tracers.shape)


def solution(mesh):
    placed = (
        P("group", None, "region", None),
        P(None, None, "region", "group"),
        P(None, "region", None),
        P(),
        P(),
    )
    return jax.shard_map(
        shards,
        mesh=mesh,
        in_specs=placed,
        out_specs=P("group", None, "region", None),
        check_vma=False,
    )
```

```python
import jax
import jax.numpy as jnp
from jax import lax
from jax.experimental import pallas as pl
from jax.experimental.pallas import tpu as pltpu
from jax.sharding import PartitionSpec as P

MESH = pl.DeviceIdType.MESH
STEPS = 2
NZ, NT, X, YB, G, R = 32, 32, 8, 32, 16, 8
XE, YE = X + 4, YB + 4
QUADS = ((0, 1, 6, 7), (2, 3, 4, 5))
RANGES = (((0, 2), (6, 8)), ((2, 6),))
NC = 5
CX, CY, CZ, SEA, OZ = range(NC)


def minmod(a, b):
    return jnp.maximum(jnp.minimum(a, b), jnp.minimum(jnp.maximum(a, b), 0.0))


def face(cell, following, slope, slope_following, c):
    forward = c > 0
    q = jnp.where(forward, 0.5, -0.5) - 0.5 * c
    return c * (jnp.where(forward, cell, following) + q * jnp.where(forward, slope, slope_following))


def halves(value):
    high = value.astype(jnp.bfloat16)
    return high, (value - high.astype(jnp.float32)).astype(jnp.bfloat16)


def block_swap(v, lane):
    low, even = lane < 64, (lane // 32) % 2 == 0
    axis = v[0].ndim - 1
    a = [None] * 4
    for n in (0, 1):
        a[n] = jnp.where(low, v[n], pltpu.roll(v[n + 2], 64, axis))
        a[n + 2] = jnp.where(low, pltpu.roll(v[n], 64, axis), v[n + 2])
    b = [None] * 4
    for n in (0, 2):
        b[n] = jnp.where(even, a[n], pltpu.roll(a[n + 1], 32, axis))
        b[n + 1] = jnp.where(even, pltpu.roll(a[n], 96, axis), a[n + 1])
    return b


def kernel(tr, velocity, mask, coupling_in, mixing_in, out,
           coupling, mixing, spread, stacked, own_mat, past_mat, mix, wmat, vel, sea3, q, dc, pack_up, pack_down, pack_y, got_low, got_high, got_y,
           tin, tout, sb, rb, fa, fb, fc, adv, edge, coef, so, ro,
           statics_in, send_static, recv_static,
           tiles_in, tiles_out, send_in, recv_in, send_halo, recv_x, send_y, recv_y, send_out, recv_out, local_sem):
    r, g = lax.axis_index("region"), lax.axis_index("group")
    lane = lax.broadcasted_iota(jnp.int32, (8, 128), 1)
    row = lax.broadcasted_iota(jnp.int32, (8, 128), 0)
    fa2, fb2 = fa.reshape(XE * YE * 8, 128), fb.reshape(XE * YE * 8, 128)
    rb2, so2 = rb.reshape(2 * 4 * NT * 8, 128), so.reshape(2 * 4 * NT * 8, 128)

    def fetch(j):
        return pltpu.make_async_copy(tr.at[:, pl.ds(j * 128, 128)], tin.at[j], tiles_in.at[j])

    def put(j):
        return pltpu.make_async_copy(tout.at[j], out.at[:, pl.ds(j * 128, 128)], tiles_out.at[j])

    at = lax.div(g, 4)
    spots = (at, jnp.maximum(at - 1, 0), jnp.minimum(at + 1, 3))
    fetches = [pltpu.make_async_copy(velocity, vel, statics_in.at[0]),
               pltpu.make_async_copy(coupling_in, coupling, statics_in.at[4]),
               pltpu.make_async_copy(mixing_in, mixing, statics_in.at[5])]
    for n, spot in enumerate(spots):
        fetches.append(pltpu.make_async_copy(
            mask.at[:, :, pl.ds(pl.multiple_of(spot * 128, 128), 128)], sea3.at[n], statics_in.at[n + 1]))
    for copy in fetches:
        copy.start()
    for j in range(4):
        fetch(j).start()

    for f in (fa, fb):
        f[0:2, 2:34] = jnp.zeros((2, 32, 8, 128), jnp.float32)
        f[10:12, 2:34] = jnp.zeros((2, 32, 8, 128), jnp.float32)
        f[2:10, 0:2] = jnp.zeros((8, 2, 8, 128), jnp.float32)
        f[2:10, 34:36] = jnp.zeros((8, 2, 8, 128), jnp.float32)

    barrier = pltpu.get_barrier_semaphore()

    def greet(d, carry):
        pl.semaphore_signal(barrier, inc=1, device_id=(r, lax.rem(g + d, G)), device_id_type=MESH)
        return carry

    lax.fori_loop(1, G, greet, 0)

    @pl.when(r > 0)
    def _():
        pl.semaphore_signal(barrier, inc=1, device_id=(r - 1, g), device_id_type=MESH)

    @pl.when(r < R - 1)
    def _():
        pl.semaphore_signal(barrier, inc=1, device_id=(r + 1, g), device_id_type=MESH)

    for j in range(4):
        fetch(j).wait()

    def begin(copy):
        copy.start()

    def static_halo(do):
        @pl.when(r < R - 1)
        def _():
            do(pltpu.make_async_remote_copy(
                src_ref=pack_up, dst_ref=got_low, send_sem=send_static.at[0], recv_sem=recv_static.at[0],
                device_id=(r + 1, g), device_id_type=MESH))

        @pl.when(r > 0)
        def _():
            do(pltpu.make_async_remote_copy(
                src_ref=pack_down, dst_ref=got_high, send_sem=send_static.at[1], recv_sem=recv_static.at[1],
                device_id=(r - 1, g), device_id_type=MESH))

        @pl.when(g < G - 1)
        def _():
            do(pltpu.make_async_remote_copy(
                src_ref=pack_y, dst_ref=got_y, send_sem=send_static.at[2], recv_sem=recv_static.at[2],
                device_id=(r, g + 1), device_id_type=MESH))

    for h, quad in enumerate(QUADS):
        def regroup(n, carry, h=h, quad=quad):
            t, zq = n // 4, n % 4
            for j in range(4):
                v = [tin[j, pl.ds((t * NZ + zq * 8) * X + x, 8, stride=8), :] for x in quad]
                for i, b in enumerate(block_swap(v, lane)):
                    sb[4 * j + i, h, zq, t] = b
            return carry

        lax.fori_loop(0, 8, regroup, 0, unroll=4)
        if h == 0:
            pl.semaphore_wait(barrier, G - 1 + jnp.minimum(r, 1) + jnp.minimum(R - 1 - r, 1))

        def send(d, carry, h=h):
            to = lax.rem(g + d, G)
            pltpu.make_async_remote_copy(
                src_ref=sb.at[to, h], dst_ref=rb.at[h, :, pl.ds(2 * g, 2)],
                send_sem=send_in.at[h], recv_sem=recv_in.at[h],
                device_id=(r, to), device_id_type=MESH).start()
            return carry

        lax.fori_loop(1, G, send, 0)
        pltpu.make_async_copy(sb.at[g, h], rb.at[h, :, pl.ds(2 * g, 2)], local_sem.at[h]).start()

    q[...] = jnp.zeros(q.shape, jnp.float32)
    for copy in fetches:
        copy.wait()
    for k in range(3):
        q[k, :, 2:10, 2:34] = vel[k]
    place = lax.rem(g, 4)
    has_left = jnp.minimum(at, 1).astype(jnp.float32)
    has_right = jnp.minimum(3 - at, 1).astype(jnp.float32)
    centre = sea3[0].astype(jnp.float32)
    left = sea3[1].astype(jnp.float32) * has_left
    right = sea3[2].astype(jnp.float32) * has_right
    centre = jnp.where(jnp.logical_and(lane >= 126, place == 0), left, centre)
    centre = jnp.where(jnp.logical_and(lane < 2, place == 3), right, centre)
    q[3, :, 2:10, :] = pltpu.roll(centre, lax.rem(130 - 32 * place, 128), 2)

    def level_rows(k, e):
        return q.at[k].reshape(NZ * 16, 128)[pl.ds(e, NZ, stride=16), :]

    def put_rows(k, e, value):
        q.at[k].reshape(NZ * 16, 128)[pl.ds(e, NZ, stride=16), :] = value

    pack_up[0], pack_up[1], pack_up[2] = level_rows(3, 8), level_rows(3, 9), level_rows(0, 9)
    pack_down[0], pack_down[1] = level_rows(3, 2), level_rows(3, 3)

    def pack_level(z, p):
        return jnp.where(lane == z, pltpu.roll(q[1, z, 2:10, :], lax.rem(z + 95, 128), 1), p)

    pack_y[...] = lax.fori_loop(0, NZ, pack_level, jnp.zeros((8, 128), jnp.float32), unroll=8)

    static_halo(begin)

    def iota(shape, axis):
        return lax.broadcasted_iota(jnp.int32, shape, axis)

    square = (128, 128)
    block_in, block_out = iota(square, 0) // 32, iota(square, 1) // 32
    for level in range(4):
        for k in range(NC):
            base = 32 * level + (24 + 4 * (k - 3) if k >= 3 else 4 * k)
            place_k = iota(square, 0) - (base + block_out)
            hit = place_k == 0 if k >= 3 else jnp.logical_or(place_k == 0, place_k == 12)
            spread[level, k] = jnp.where(hit, 1.0, 0.0).astype(jnp.bfloat16)
    first = iota(square, 0) % 32 == 0
    own = jnp.where(jnp.logical_and(first, block_in == block_out), 1.0, 0.0).astype(jnp.bfloat16)
    past = jnp.where(jnp.logical_and(first, block_in < block_out), 1.0, 0.0).astype(jnp.bfloat16)
    own_mat[...] = jnp.concatenate([own, own], 0)
    past_mat[...] = jnp.concatenate([past, past], 0)
    across = jnp.concatenate([coupling[...].T] * 4, 1)
    weights = jnp.where(block_in == block_out, jnp.concatenate([across] * 4, 0), 0.0)
    high, low = halves(weights)
    wmat[...] = jnp.concatenate([jnp.concatenate([high, low], 1), jnp.concatenate([high, jnp.zeros_like(low)], 1)], 0)
    tile = jnp.zeros((8, 128), jnp.float32)
    for z in range(NZ):
        tile = jnp.where(jnp.logical_and(row == z % 8, lane // 32 == z // 8), mixing[z], tile)
    mix[...] = tile

    @pl.when(r > 0)
    def _():
        pltpu.make_async_copy(got_low, got_low, recv_static.at[0]).wait()
        put_rows(3, 0, got_low[0])
        put_rows(3, 1, got_low[1])
        put_rows(0, 1, got_low[2])

    @pl.when(r < R - 1)
    def _():
        pltpu.make_async_copy(got_high, got_high, recv_static.at[1]).wait()
        put_rows(3, 10, got_high[0])
        put_rows(3, 11, got_high[1])

    @pl.when(g > 0)
    def _():
        pltpu.make_async_copy(got_y, got_y, recv_static.at[2]).wait()

        def unpack_level(z, carry):
            q[1, z, 2:10, :] = jnp.where(
                lane == 1, pltpu.roll(got_y[...], lax.rem(129 - z, 128), 1), q[1, z, 2:10, :])
            return carry

        lax.fori_loop(0, NZ, unpack_level, 0, unroll=8)

    sea = q[3]
    follow = (pltpu.roll(sea, 15, 1), pltpu.roll(sea, 127, 2),
              jnp.concatenate([sea[1:], jnp.zeros((1, 16, 128), jnp.float32)], 0))
    for k in range(3):
        opened = sea * follow[k]
        c = q[k] * opened
        high = c.astype(jnp.bfloat16).astype(jnp.float32)
        dc[k] = high
        dc[3 + k] = c - high
    dc[6] = sea
    dc[7] = opened

    def stack_one(e, carry):
        for half in range(2):
            rows = [dc.reshape(8 * NZ * 16, 128)[pl.ds((half * 4 + n) * 16 + e, 32, stride=128), :] for n in range(4)]
            stacked[half, pl.ds(pl.multiple_of(e * 48, 16), 48), :] = (
                jnp.concatenate(rows, axis=0).T[:48].astype(jnp.bfloat16))
        return carry

    lax.fori_loop(0, XE, stack_one, 0)

    def spread_one(zr, carry):
        for k in range(NC):
            wide = jnp.dot(stacked[zr // 4], spread[zr % 4, k], preferred_element_type=jnp.float32)
            for e in range(XE):
                coef.at[k].reshape(XE * YE * 8, 128)[pl.ds(e * YE * 8 + zr, YE, stride=8), :] = wide[e * 48:e * 48 + YE]
        return carry

    lax.fori_loop(0, 8, spread_one, 0)

    def x_halo(f, s, do):
        @pl.when(r > 0)
        def _():
            do(pltpu.make_async_remote_copy(
                src_ref=f.at[2:4, 2:34], dst_ref=f.at[10:12, 2:34],
                send_sem=send_halo.at[s, 0], recv_sem=recv_x.at[s, 1],
                device_id=(r - 1, g), device_id_type=MESH))

        @pl.when(r < R - 1)
        def _():
            do(pltpu.make_async_remote_copy(
                src_ref=f.at[8:10, 2:34], dst_ref=f.at[0:2, 2:34],
                send_sem=send_halo.at[s, 1], recv_sem=recv_x.at[s, 0],
                device_id=(r + 1, g), device_id_type=MESH))

    def y_halo(f, s, h):
        @pl.when(g > 0)
        def _():
            for x0, x1 in RANGES[h]:
                pltpu.make_async_remote_copy(
                    src_ref=f.at[x0 + 2:x1 + 2, 2:4], dst_ref=f.at[x0 + 2:x1 + 2, 34:36],
                    send_sem=send_y.at[s, h, 1], recv_sem=recv_y.at[s, h, 1],
                    device_id=(r, g - 1), device_id_type=MESH).start()

        @pl.when(g < G - 1)
        def _():
            for x0, x1 in RANGES[h]:
                pltpu.make_async_remote_copy(
                    src_ref=f.at[x0 + 2:x1 + 2, 32:34], dst_ref=f.at[x0 + 2:x1 + 2, 0:2],
                    send_sem=send_y.at[s, h, 0], recv_sem=recv_y.at[s, h, 0],
                    device_id=(r, g + 1), device_id_type=MESH).start()

    def landed(ref, sem):
        pltpu.make_async_copy(ref, ref, sem).wait()

    def arrive_x(f, s):
        @pl.when(r > 0)
        def _():
            landed(f.at[0:2, 2:34], recv_x.at[s, 0])

        @pl.when(r < R - 1)
        def _():
            landed(f.at[10:12, 2:34], recv_x.at[s, 1])

    def arrive_y(f, s, h):
        @pl.when(g > 0)
        def _():
            landed(f.at[2:6, 0:2], recv_y.at[s, h, 0])

        @pl.when(g < G - 1)
        def _():
            landed(f.at[2:6, 34:36], recv_y.at[s, h, 1])

    def sent_y(f, s, h):
        @pl.when(g > 0)
        def _():
            landed(f.at[2:6, 2:4], send_y.at[s, h, 1])

        @pl.when(g < G - 1)
        def _():
            landed(f.at[2:6, 32:34], send_y.at[s, h, 0])

    for h, quad in enumerate(QUADS):
        some = rb.at[h, :, 0:2 * (G - 1)]
        pltpu.make_async_copy(some, some, recv_in.at[h]).wait()
        pltpu.make_async_copy(sb.at[g, h], rb.at[h, :, pl.ds(2 * g, 2)], local_sem.at[h]).wait()

        def turn(zr, carry, h=h, quad=quad):
            turned = rb2[pl.ds(h * 4 * NT * 8 + zr, 128, stride=8), :].T
            for n, x in enumerate(quad):
                fa2[pl.ds(((x + 2) * YE + 2) * 8 + zr, YB, stride=8), :] = turned[n * YB:(n + 1) * YB]
            return carry

        lax.fori_loop(0, 8, turn, 0, unroll=8)
        if h == 0:
            x_halo(fa, 0, begin)
        y_halo(fa, 0, h)

    def z_edges(f, x0, x1):
        def rows(ref, k):
            return ref.reshape(ref.shape[0] * ref.shape[1] * 8, 128)[pl.ds((x0 + 2) * YE * 8 + k, (x1 - x0) * YE, stride=8), :]

        def static(k, n):
            return rows(coef.at[k], n)

        next0 = pltpu.roll(rows(f, 0), 96, 1)
        next1 = pltpu.roll(rows(f, 1), 96, 1)
        last = rows(f, 7)
        jump = (next0 - last) * static(OZ, 7)
        slope = minmod((last - rows(f, 6)) * static(OZ, 6), jump)
        slope_next = minmod(jump, (next1 - next0) * pltpu.roll(static(OZ, 0), 96, 1))
        flux = face(last, next0, slope, slope_next, static(CZ, 7)) - mix[7:8, :] * jump
        for n, k, v in ((0, 7, next0), (0, 0, pltpu.roll(jump, 32, 1)), (1, 7, slope_next), (1, 0, pltpu.roll(flux, 32, 1))):
            edge.at[n].reshape(X * YE * 8, 128)[pl.ds(x0 * YE * 8 + k, (x1 - x0) * YE, stride=8), :] = v

    def advect(f, h):
        parts = [advect_part(f, x0, x1) for x0, x1 in RANGES[h]]

        def column(y, carry):
            return tuple(step(y, c) for (_, step), c in zip(parts, carry))

        lax.fori_loop(0, YB, column, tuple(start for start, _ in parts), unroll=2)

    def advect_part(f, x0, x1):
        z_edges(f, x0, x1)
        n = x1 - x0

        def cells(e):
            return f[x0 + 2:x1 + 2, e]

        def along(k, e):
            return coef[k, x0 + 2:x1 + 2, e]

        def open_y(e):
            return along(SEA, e) * along(SEA, e + 1)

        f1, f2 = cells(1), cells(2)
        j0 = (f1 - cells(0)) * open_y(0)
        j1 = (f2 - f1) * open_y(1)
        j2 = (cells(3) - f2) * open_y(2)
        s1, s2 = minmod(j0, j1), minmod(j1, j2)
        start = (j2, s2, face(f1, f2, s1, s2, along(CY, 1)))

        def column(y, carry):
            jump, slope, before = carry
            e = y + 2
            fx = f[x0:x1 + 4, e]
            inner, following = fx[2:n + 2], cells(e + 1)
            jump_next = (cells(e + 2) - following) * open_y(e + 1)
            slope_next = minmod(jump, jump_next)
            after = face(inner, following, slope, slope_next, along(CY, e))
            total = inner - (after - before)
            sea_x = coef[SEA, x0:x1 + 4, e]
            jx = (fx[1:] - fx[:-1]) * (sea_x[1:] * sea_x[:-1])
            sx = minmod(jx[:-1], jx[1:])
            flux = face(fx[1:n + 2], fx[2:n + 3], sx[:-1], sx[1:], coef[CX, x0 + 1:x1 + 2, e])
            total = total - (flux[1:] - flux[:-1])
            edge0, edge1 = edge[0, x0:x1, e], edge[1, x0:x1, e]
            below = jnp.where(row == 7, edge0, pltpu.roll(inner, 7, 1))
            jz = (below - inner) * along(OZ, e)
            sz = minmod(jnp.where(row == 0, edge0, pltpu.roll(jz, 1, 1)), jz)
            sz_next = jnp.where(row == 7, edge1, pltpu.roll(sz, 7, 1))
            down = face(inner, below, sz, sz_next, along(CZ, e)) - mix[...] * jz
            adv[x0:x1, y] = total - (down - jnp.where(row == 0, edge1, pltpu.roll(down, 1, 1)))
            return jump_next, slope_next, after

        return start, column

    def react(x, result):
        a = adv[x]
        att = 0.05 + 0.1 * a * a
        inc = att
        for step in (1, 2, 4):
            inc = inc + jnp.where(row >= step, pltpu.roll(inc, step, 1), 0.0)
        exc = (inc - att).reshape(256, 128)
        ahead = jnp.dot(jnp.concatenate(halves(exc), axis=1), own_mat[...], preferred_element_type=jnp.float32)
        past = jnp.dot(jnp.concatenate(halves(inc.reshape(256, 128)), axis=1), past_mat[...],
                       preferred_element_type=jnp.float32).reshape(YB, 8, 128)
        light = jnp.exp(-(ahead.reshape(YB, 8, 128) + past[:, 7:8, :]))
        both = jnp.dot(jnp.concatenate(halves(jnp.tanh(a).reshape(256, 128)), axis=1), wmat[...],
                       preferred_element_type=jnp.float32)
        response = (both[:, :128] + both[:, 128:]).reshape(YB, 8, 128)
        result[...] = a + coef[SEA, x + 2, 2:34] * ((0.5 + light) * response)

    fc2 = fc.reshape(X * YB * 8, 128)

    def give_back(h, quad):
        def turn_back(zr, carry):
            stack = [fc2[pl.ds(x * YB * 8 + zr, YB, stride=8), :] for x in quad]
            so2[pl.ds(h * 4 * NT * 8 + zr, 128, stride=8), :] = jnp.concatenate(stack, axis=0).T
            return carry

        lax.fori_loop(0, 8, turn_back, 0, unroll=8)

        def send_back(d, carry):
            to = lax.rem(g + d, G)
            pltpu.make_async_remote_copy(
                src_ref=so.at[h, :, pl.ds(2 * to, 2)], dst_ref=ro.at[h, g],
                send_sem=send_out.at[h], recv_sem=recv_out.at[h],
                device_id=(r, to), device_id_type=MESH).start()
            return carry

        lax.fori_loop(1, G, send_back, 0)
        pltpu.make_async_copy(so.at[h, :, pl.ds(2 * g, 2)], ro.at[h, g], local_sem.at[2 + h]).start()

    arrive_x(fa, 0)
    for h, quad in enumerate(QUADS):
        arrive_y(fa, 0, h)
        advect(fa, h)
        for x in quad:
            react(x, fb.at[x + 2, 2:34])
        if h == 0:
            x_halo(fb, 1, begin)
        y_halo(fb, 1, h)
    for h in (1, 0):
        if h == 0:
            arrive_x(fb, 1)
        arrive_y(fb, 1, h)
        advect(fb, h)
        for x in QUADS[h]:
            react(x, fc.at[x])
        give_back(h, QUADS[h])

    static_halo(lambda copy: copy.wait_send())
    for s, f in ((0, fa), (1, fb)):
        x_halo(f, s, lambda copy: copy.wait_send())
        for h in range(2):
            sent_y(f, s, h)

    for h in (1, 0):
        some = ro.at[h, 0:G - 1]
        pltpu.make_async_copy(some, some, recv_out.at[h]).wait()
        pltpu.make_async_copy(so.at[h, :, pl.ds(2 * g, 2)], ro.at[h, g], local_sem.at[2 + h]).wait()

        def restore(n, carry, h=h, quad=QUADS[h]):
            t, zq = n // 4, n % 4
            for j in range(4):
                v = block_swap([ro[h, 4 * j + i, zq, t] for i in range(4)], lane)
                for x, b in zip(quad, v):
                    tout[j, pl.ds((t * NZ + zq * 8) * X + x, 8, stride=8), :] = b
            return carry

        lax.fori_loop(0, 8, restore, 0, unroll=4)

    for j in range(4):
        put(j).start()
    for h in range(2):
        some = sb.at[0:G - 1, h]
        pltpu.make_async_copy(some, some, send_in.at[h]).wait()
        some = ro.at[h, 0:G - 1]
        pltpu.make_async_copy(some, some, send_out.at[h]).wait()
    for j in range(4):
        put(j).wait()


def shards(tracers, velocity, sea_mask, coupling, mixing):
    anywhere = pl.BlockSpec(memory_space=pl.ANY)
    vmem = pl.BlockSpec(memory_space=pltpu.VMEM)
    f32 = jnp.float32
    dma = pltpu.SemaphoreType.DMA
    out = pl.pallas_call(
        kernel,
        out_shape=jax.ShapeDtypeStruct((2 * NZ * X, G * YB), f32),
        in_specs=[anywhere] * 3 + [anywhere, anywhere],
        out_specs=anywhere,
        scratch_shapes=[
            pltpu.VMEM((NT, NT), f32),
            pltpu.SMEM((NZ,), f32),
            pltpu.VMEM((4, NC, 128, 128), jnp.bfloat16),
            pltpu.VMEM((2, XE * 48, 128), jnp.bfloat16),
            pltpu.VMEM((256, 128), jnp.bfloat16),
            pltpu.VMEM((256, 128), jnp.bfloat16),
            pltpu.VMEM((8, 128), f32),
            pltpu.VMEM((256, 256), jnp.bfloat16),
            pltpu.VMEM((3, NZ, X, YB), f32),
            pltpu.VMEM((3, NZ, X, 128), jnp.int32),
            pltpu.VMEM((4, NZ, 16, 128), f32),
            pltpu.VMEM((8, NZ, 16, 128), f32),
            pltpu.VMEM((3, NZ, 128), f32),
            pltpu.VMEM((2, NZ, 128), f32),
            pltpu.VMEM((8, 128), f32),
            pltpu.VMEM((3, NZ, 128), f32),
            pltpu.VMEM((2, NZ, 128), f32),
            pltpu.VMEM((8, 128), f32),
            pltpu.VMEM((4, 2 * NZ * X, 128), f32),
            pltpu.VMEM((4, 2 * NZ * X, 128), f32),
            pltpu.VMEM((G, 2, 4, 2, 8, 128), f32),
            pltpu.VMEM((2, 4, NT, 8, 128), f32),
            pltpu.VMEM((XE, YE, 8, 128), f32),
            pltpu.VMEM((XE, YE, 8, 128), f32),
            pltpu.VMEM((X, YB, 8, 128), f32),
            pltpu.VMEM((X, YB, 8, 128), f32),
            pltpu.VMEM((2, X, YE, 8, 128), f32),
            pltpu.VMEM((NC, XE, YE, 8, 128), f32),
            pltpu.VMEM((2, 4, NT, 8, 128), f32),
            pltpu.VMEM((2, G, 4, 2, 8, 128), f32),
            dma((6,)), dma((3,)), dma((3,)),
            dma((4,)), dma((4,)), dma((2,)), dma((2,)), dma((2, 2)), dma((2, 2)), dma((2, 2, 2)), dma((2, 2, 2)), dma((2,)), dma((2,)), dma((4,)),
        ],
        compiler_params=pltpu.CompilerParams(
            collective_id=0, has_side_effects=True, vmem_limit_bytes=60 * 2**20),
    )(tracers.reshape(2 * NZ * X, G * YB), velocity, sea_mask, coupling, mixing)
    return out.reshape(tracers.shape)


def solution(mesh):
    placed = (
        P("group", None, "region", None),
        P(None, None, "region", "group"),
        P(None, "region", None),
        P(),
        P(),
    )
    return jax.shard_map(
        shards,
        mesh=mesh,
        in_specs=placed,
        out_specs=P("group", None, "region", None),
        check_vma=False,
    )
```

```python
import jax
import jax.numpy as jnp
from jax import lax
from jax.experimental import pallas as pl
from jax.experimental.pallas import tpu as pltpu
from jax.sharding import PartitionSpec as P

MESH = pl.DeviceIdType.MESH
STEPS = 2
NZ, NT, X, YB, G, R = 32, 32, 8, 32, 16, 8
XE, YE = X + 4, YB + 4
QUADS = ((0, 1, 6, 7), (2, 3, 4, 5))
RANGES = (((0, 2), (6, 8)), ((2, 6),))
NC = 5
CX, CY, CZ, SEA, OZ = range(NC)


def minmod(a, b):
    return jnp.maximum(jnp.minimum(a, b), jnp.minimum(jnp.maximum(a, b), 0.0))


def face(cell, following, slope, slope_following, c):
    forward = c > 0
    q = jnp.where(forward, 0.5, -0.5) - 0.5 * c
    return c * (jnp.where(forward, cell, following) + q * jnp.where(forward, slope, slope_following))


def halves(value):
    high = value.astype(jnp.bfloat16)
    return high, (value - high.astype(jnp.float32)).astype(jnp.bfloat16)


def block_swap(v, lane):
    low, even = lane < 64, (lane // 32) % 2 == 0
    axis = v[0].ndim - 1
    a = [None] * 4
    for n in (0, 1):
        a[n] = jnp.where(low, v[n], pltpu.roll(v[n + 2], 64, axis))
        a[n + 2] = jnp.where(low, pltpu.roll(v[n], 64, axis), v[n + 2])
    b = [None] * 4
    for n in (0, 2):
        b[n] = jnp.where(even, a[n], pltpu.roll(a[n + 1], 32, axis))
        b[n + 1] = jnp.where(even, pltpu.roll(a[n], 96, axis), a[n + 1])
    return b


def kernel(tr, velocity, mask, coupling_in, mixing_in, out,
           coupling, mixing, spread, stacked, own_mat, past_mat, mix, wmat, vel, vel_pack, vel_got, sea3, q, dc, pack_up, pack_down, pack_x, pack_y, got_x, got_low, got_high, got_y,
           tin, tout, sb, rb, fa, fb, fc, adv, edge, coef, so, ro,
           statics_in, send_static, recv_static,
           tiles_in, tiles_out, send_in, recv_in, send_halo, recv_x, send_y, recv_y, send_out, recv_out, local_sem):
    r, g = lax.axis_index("region"), lax.axis_index("group")
    upper = lax.div(r, R // 2)

    def flip(n, upper=upper):
        return n + upper * (2 - 4 * lax.rem(lax.div(n, 2), 2))

    block = flip(g)
    other = g + 2 - 4 * lax.rem(lax.div(g, 2), 2)
    g_next = jnp.where(r == R // 2 - 1, other, g)
    g_last = jnp.where(r == R // 2, other, g)
    lane = lax.broadcasted_iota(jnp.int32, (8, 128), 1)
    row = lax.broadcasted_iota(jnp.int32, (8, 128), 0)
    fa2, fb2 = fa.reshape(XE * YE * 8, 128), fb.reshape(XE * YE * 8, 128)
    rb2, so2 = rb.reshape(2 * 4 * NT * 8, 128), so.reshape(2 * 4 * NT * 8, 128)

    def fetch(j):
        return pltpu.make_async_copy(tr.at[:, pl.ds(j * 128, 128)], tin.at[j], tiles_in.at[j])

    def put(j):
        return pltpu.make_async_copy(tout.at[j], out.at[:, pl.ds(j * 128, 128)], tiles_out.at[j])

    at = lax.div(block, 4)
    spots = (at, jnp.maximum(at - 1, 0), jnp.minimum(at + 1, 3))
    fetches = [pltpu.make_async_copy(velocity, vel, statics_in.at[0]),
               pltpu.make_async_copy(coupling_in, coupling, statics_in.at[4]),
               pltpu.make_async_copy(mixing_in, mixing, statics_in.at[5])]
    for n, spot in enumerate(spots):
        fetches.append(pltpu.make_async_copy(
            mask.at[:, :, pl.ds(pl.multiple_of(spot * 128, 128), 128)], sea3.at[n], statics_in.at[n + 1]))
    for copy in fetches:
        copy.start()
    for j in range(4):
        fetch(j).start()

    for f in (fa, fb):
        f[0:2, 2:34] = jnp.zeros((2, 32, 8, 128), jnp.float32)
        f[10:12, 2:34] = jnp.zeros((2, 32, 8, 128), jnp.float32)
        f[2:10, 0:2] = jnp.zeros((8, 2, 8, 128), jnp.float32)
        f[2:10, 34:36] = jnp.zeros((8, 2, 8, 128), jnp.float32)

    barrier = pltpu.get_barrier_semaphore()

    def greet(d, carry):
        pl.semaphore_signal(barrier, inc=1, device_id=(r, lax.rem(g + d, G)), device_id_type=MESH)
        return carry

    lax.fori_loop(1, G, greet, 0)

    @pl.when(r > 0)
    def _():
        pl.semaphore_signal(barrier, inc=1, device_id=(r - 1, g_last), device_id_type=MESH)

    @pl.when(r > R // 2)
    def _():
        pl.semaphore_signal(barrier, inc=1, device_id=(r - 1, other), device_id_type=MESH)

    extra = jnp.where(jnp.logical_and(r >= R // 2, r < R - 1), 1, 0)

    @pl.when(r < R - 1)
    def _():
        pl.semaphore_signal(barrier, inc=1, device_id=(r + 1, g_next), device_id_type=MESH)

    for j in range(4):
        fetch(j).wait()

    def begin(copy):
        copy.start()

    def static_halo(do):
        @pl.when(r < R - 1)
        def _():
            do(pltpu.make_async_remote_copy(
                src_ref=pack_up, dst_ref=got_low, send_sem=send_static.at[0], recv_sem=recv_static.at[0],
                device_id=(r + 1, g_next), device_id_type=MESH))

        @pl.when(r > 0)
        def _():
            do(pltpu.make_async_remote_copy(
                src_ref=pack_down, dst_ref=got_high, send_sem=send_static.at[1], recv_sem=recv_static.at[1],
                device_id=(r - 1, g_last), device_id_type=MESH))

    def edges_over(do):
        @pl.when(r < R - 1)
        def _():
            to = flip(g, lax.div(r + 1, R // 2))
            do(pltpu.make_async_remote_copy(
                src_ref=pack_x, dst_ref=got_x, send_sem=send_static.at[4], recv_sem=recv_static.at[4],
                device_id=(r + 1, to), device_id_type=MESH))

        @pl.when(g < G - 1)
        def _():
            do(pltpu.make_async_remote_copy(
                src_ref=pack_y, dst_ref=got_y, send_sem=send_static.at[2], recv_sem=recv_static.at[2],
                device_id=(r, flip(g + 1)), device_id_type=MESH))

    def velocity_over(do, do_here):
        @pl.when(upper > 0)
        def _():
            do(pltpu.make_async_remote_copy(
                src_ref=vel_pack, dst_ref=vel_got, send_sem=send_static.at[3], recv_sem=recv_static.at[3],
                device_id=(r, block), device_id_type=MESH))

        @pl.when(upper == 0)
        def _():
            do_here(pltpu.make_async_copy(vel_pack, vel_got, recv_static.at[3]))

    fetches[0].wait()
    for k in range(3):
        for m in range(8):
            vel_pack[8 * k + m] = jnp.concatenate([vel[k, 4 * m + n] for n in range(4)], axis=1)
    pack_x[...] = vel_pack.reshape(24 * X, 128)[pl.ds(7, 8, stride=8), :]
    column = jnp.zeros((8, 128), jnp.float32)
    for m in range(8):
        column = jnp.where(lane % 32 == m, pltpu.roll(vel_pack[8 + m], m + 97, 1), column)
    pack_y[...] = column

    for h, quad in enumerate(QUADS):
        def regroup(n, carry, h=h, quad=quad):
            t, zq = n // 4, n % 4
            for j in range(4):
                v = [tin[j, pl.ds((t * NZ + zq * 8) * X + x, 8, stride=8), :] for x in quad]
                for i, b in enumerate(block_swap(v, lane)):
                    sb[4 * j + i, h, zq, t] = b
            return carry

        lax.fori_loop(0, 8, regroup, 0, unroll=4)
        if h == 0:
            pl.semaphore_wait(barrier, G - 1 + jnp.minimum(r, 1) + jnp.minimum(R - 1 - r, 1) + extra)
            velocity_over(begin, begin)
            edges_over(begin)

        def send(d, carry, h=h):
            to = lax.rem(g + d, G)
            pltpu.make_async_remote_copy(
                src_ref=sb.at[flip(to), h], dst_ref=rb.at[h, :, pl.ds(2 * g, 2)],
                send_sem=send_in.at[h], recv_sem=recv_in.at[h],
                device_id=(r, to), device_id_type=MESH).start()
            return carry

        lax.fori_loop(1, G, send, 0)
        pltpu.make_async_copy(sb.at[block, h], rb.at[h, :, pl.ds(2 * g, 2)], local_sem.at[h]).start()

    q[...] = jnp.zeros(q.shape, jnp.float32)
    for copy in fetches[1:]:
        copy.wait()
    velocity_over(lambda copy: copy.wait_recv(), lambda copy: copy.wait())
    for n in range(4):
        shifted = pltpu.roll(vel_got[...], (130 - 32 * n) % 128, 2)
        shifted = jnp.where(jnp.logical_and(lane >= 2, lane < 34), shifted, 0.0)
        for k in range(3):
            for m in range(8):
                q[k, 4 * m + n, 2:10, :] = shifted[8 * k + m]
    place = lax.rem(block, 4)
    has_left = jnp.minimum(at, 1).astype(jnp.float32)
    has_right = jnp.minimum(3 - at, 1).astype(jnp.float32)
    centre = sea3[0].astype(jnp.float32)
    left = sea3[1].astype(jnp.float32) * has_left
    right = sea3[2].astype(jnp.float32) * has_right
    centre = jnp.where(jnp.logical_and(lane >= 126, place == 0), left, centre)
    centre = jnp.where(jnp.logical_and(lane < 2, place == 3), right, centre)
    q[3, :, 2:10, :] = pltpu.roll(centre, lax.rem(130 - 32 * place, 128), 2)

    def level_rows(k, e):
        return q.at[k].reshape(NZ * 16, 128)[pl.ds(e, NZ, stride=16), :]

    def put_rows(k, e, value):
        q.at[k].reshape(NZ * 16, 128)[pl.ds(e, NZ, stride=16), :] = value

    pack_up[0], pack_up[1] = level_rows(3, 8), level_rows(3, 9)
    pack_down[0], pack_down[1] = level_rows(3, 2), level_rows(3, 3)

    static_halo(begin)

    def iota(shape, axis):
        return lax.broadcasted_iota(jnp.int32, shape, axis)

    square = (128, 128)
    block_in, block_out = iota(square, 0) // 32, iota(square, 1) // 32
    for level in range(4):
        for k in range(NC):
            base = 32 * level + (24 + 4 * (k - 3) if k >= 3 else 4 * k)
            place_k = iota(square, 0) - (base + block_out)
            hit = place_k == 0 if k >= 3 else jnp.logical_or(place_k == 0, place_k == 12)
            spread[level, k] = jnp.where(hit, 1.0, 0.0).astype(jnp.bfloat16)
    first = iota(square, 0) % 32 == 0
    own = jnp.where(jnp.logical_and(first, block_in == block_out), 1.0, 0.0).astype(jnp.bfloat16)
    past = jnp.where(jnp.logical_and(first, block_in < block_out), 1.0, 0.0).astype(jnp.bfloat16)
    own_mat[...] = jnp.concatenate([own, own], 0)
    past_mat[...] = jnp.concatenate([past, past], 0)
    across = jnp.concatenate([coupling[...].T] * 4, 1)
    weights = jnp.where(block_in == block_out, jnp.concatenate([across] * 4, 0), 0.0)
    high, low = halves(weights)
    wmat[...] = jnp.concatenate([jnp.concatenate([high, low], 1), jnp.concatenate([high, jnp.zeros_like(low)], 1)], 0)
    tile = jnp.zeros((8, 128), jnp.float32)
    for z in range(NZ):
        tile = jnp.where(jnp.logical_and(row == z % 8, lane // 32 == z // 8), mixing[z], tile)
    mix[...] = tile

    @pl.when(r > 0)
    def _():
        pltpu.make_async_copy(got_low, got_low, recv_static.at[0]).wait()
        put_rows(3, 0, got_low[0])
        put_rows(3, 1, got_low[1])
        pltpu.make_async_copy(got_x, got_x, recv_static.at[4]).wait()
        for n in range(4):
            q.at[0].reshape(NZ * 16, 128)[pl.ds(n * 16 + 1, 8, stride=64), :] = jnp.where(
                jnp.logical_and(lane >= 2, lane < 34), pltpu.roll(got_x[...], (130 - 32 * n) % 128, 1), 0.0)

    @pl.when(r < R - 1)
    def _():
        pltpu.make_async_copy(got_high, got_high, recv_static.at[1]).wait()
        put_rows(3, 10, got_high[0])
        put_rows(3, 11, got_high[1])

    @pl.when(block > 0)
    def _():
        pltpu.make_async_copy(got_y, got_y, recv_static.at[2]).wait()

        def unpack_level(z, carry):
            q[1, z, 2:10, :] = jnp.where(
                lane == 1, pltpu.roll(got_y[...], lax.rem(129 - lax.div(z, 4) - 32 * lax.rem(z, 4) + 128, 128), 1), q[1, z, 2:10, :])
            return carry

        lax.fori_loop(0, NZ, unpack_level, 0, unroll=8)

    sea = q[3]
    follow = (pltpu.roll(sea, 15, 1), pltpu.roll(sea, 127, 2),
              jnp.concatenate([sea[1:], jnp.zeros((1, 16, 128), jnp.float32)], 0))
    for k in range(3):
        opened = sea * follow[k]
        c = q[k] * opened
        high = c.astype(jnp.bfloat16).astype(jnp.float32)
        dc[k] = high
        dc[3 + k] = c - high
    dc[6] = sea
    dc[7] = opened

    def stack_one(e, carry):
        for half in range(2):
            rows = [dc.reshape(8 * NZ * 16, 128)[pl.ds((half * 4 + n) * 16 + e, 32, stride=128), :] for n in range(4)]
            stacked[half, pl.ds(pl.multiple_of(e * 48, 16), 48), :] = (
                jnp.concatenate(rows, axis=0).T[:48].astype(jnp.bfloat16))
        return carry

    def spread_one(zr, carry):
        for k in range(NC):
            wide = jnp.dot(stacked[zr // 4], spread[zr % 4, k], preferred_element_type=jnp.float32)
            for e in range(XE):
                coef.at[k].reshape(XE * YE * 8, 128)[pl.ds(e * YE * 8 + zr, YE, stride=8), :] = wide[e * 48:e * 48 + YE]
        return carry

    def x_halo(f, s, do):
        @pl.when(r > 0)
        def _():
            do(pltpu.make_async_remote_copy(
                src_ref=f.at[2:4, 2:34], dst_ref=f.at[10:12, 2:34],
                send_sem=send_halo.at[s, 0], recv_sem=recv_x.at[s, 1],
                device_id=(r - 1, g_last), device_id_type=MESH))

        @pl.when(r < R - 1)
        def _():
            do(pltpu.make_async_remote_copy(
                src_ref=f.at[8:10, 2:34], dst_ref=f.at[0:2, 2:34],
                send_sem=send_halo.at[s, 1], recv_sem=recv_x.at[s, 0],
                device_id=(r + 1, g_next), device_id_type=MESH))

    def y_halo(f, s, h):
        @pl.when(block > 0)
        def _():
            for x0, x1 in RANGES[h]:
                pltpu.make_async_remote_copy(
                    src_ref=f.at[x0 + 2:x1 + 2, 2:4], dst_ref=f.at[x0 + 2:x1 + 2, 34:36],
                    send_sem=send_y.at[s, h, 1], recv_sem=recv_y.at[s, h, 1],
                    device_id=(r, flip(block - 1)), device_id_type=MESH).start()

        @pl.when(block < G - 1)
        def _():
            for x0, x1 in RANGES[h]:
                pltpu.make_async_remote_copy(
                    src_ref=f.at[x0 + 2:x1 + 2, 32:34], dst_ref=f.at[x0 + 2:x1 + 2, 0:2],
                    send_sem=send_y.at[s, h, 0], recv_sem=recv_y.at[s, h, 0],
                    device_id=(r, flip(block + 1)), device_id_type=MESH).start()

    def landed(ref, sem):
        pltpu.make_async_copy(ref, ref, sem).wait()

    def arrive_x(f, s):
        @pl.when(r > 0)
        def _():
            landed(f.at[0:2, 2:34], recv_x.at[s, 0])

        @pl.when(r < R - 1)
        def _():
            landed(f.at[10:12, 2:34], recv_x.at[s, 1])

    def arrive_y(f, s, h):
        @pl.when(block > 0)
        def _():
            landed(f.at[2:6, 0:2], recv_y.at[s, h, 0])

        @pl.when(block < G - 1)
        def _():
            landed(f.at[2:6, 34:36], recv_y.at[s, h, 1])

    def sent_y(f, s, h):
        @pl.when(block > 0)
        def _():
            landed(f.at[2:6, 2:4], send_y.at[s, h, 1])

        @pl.when(block < G - 1)
        def _():
            landed(f.at[2:6, 32:34], send_y.at[s, h, 0])

    for h, quad in enumerate(QUADS):
        some = rb.at[h, :, 0:2 * (G - 1)]
        pltpu.make_async_copy(some, some, recv_in.at[h]).wait()
        pltpu.make_async_copy(sb.at[block, h], rb.at[h, :, pl.ds(2 * g, 2)], local_sem.at[h]).wait()

        def turn(zr, carry, h=h, quad=quad):
            turned = rb2[pl.ds(h * 4 * NT * 8 + zr, 128, stride=8), :].T
            for n, x in enumerate(quad):
                fa2[pl.ds(((x + 2) * YE + 2) * 8 + zr, YB, stride=8), :] = turned[n * YB:(n + 1) * YB]
            return carry

        lax.fori_loop(0, 8, turn, 0, unroll=8)
        if h == 0:
            x_halo(fa, 0, begin)
        y_halo(fa, 0, h)
        if h == 0:
            lax.fori_loop(0, XE, stack_one, 0)
            lax.fori_loop(0, 8, spread_one, 0)

    def z_edges(f, x0, x1):
        def rows(ref, k):
            return ref.reshape(ref.shape[0] * ref.shape[1] * 8, 128)[pl.ds((x0 + 2) * YE * 8 + k, (x1 - x0) * YE, stride=8), :]

        def static(k, n):
            return rows(coef.at[k], n)

        next0 = pltpu.roll(rows(f, 0), 96, 1)
        next1 = pltpu.roll(rows(f, 1), 96, 1)
        last = rows(f, 7)
        jump = (next0 - last) * static(OZ, 7)
        slope = minmod((last - rows(f, 6)) * static(OZ, 6), jump)
        slope_next = minmod(jump, (next1 - next0) * pltpu.roll(static(OZ, 0), 96, 1))
        flux = face(last, next0, slope, slope_next, static(CZ, 7)) - mix[7:8, :] * jump
        for n, k, v in ((0, 7, next0), (0, 0, pltpu.roll(jump, 32, 1)), (1, 7, slope_next), (1, 0, pltpu.roll(flux, 32, 1))):
            edge.at[n].reshape(X * YE * 8, 128)[pl.ds(x0 * YE * 8 + k, (x1 - x0) * YE, stride=8), :] = v

    def advect(f, h):
        parts = [advect_part(f, x0, x1) for x0, x1 in RANGES[h]]

        def column(y, carry):
            return tuple(step(y, c) for (_, step), c in zip(parts, carry))

        lax.fori_loop(0, YB, column, tuple(start for start, _ in parts), unroll=2)

    def advect_part(f, x0, x1):
        z_edges(f, x0, x1)
        n = x1 - x0

        def cells(e):
            return f[x0 + 2:x1 + 2, e]

        def along(k, e):
            return coef[k, x0 + 2:x1 + 2, e]

        def open_y(e):
            return along(SEA, e) * along(SEA, e + 1)

        f1, f2 = cells(1), cells(2)
        j0 = (f1 - cells(0)) * open_y(0)
        j1 = (f2 - f1) * open_y(1)
        j2 = (cells(3) - f2) * open_y(2)
        s1, s2 = minmod(j0, j1), minmod(j1, j2)
        start = (j2, s2, face(f1, f2, s1, s2, along(CY, 1)))

        def column(y, carry):
            jump, slope, before = carry
            e = y + 2
            fx = f[x0:x1 + 4, e]
            inner, following = fx[2:n + 2], cells(e + 1)
            jump_next = (cells(e + 2) - following) * open_y(e + 1)
            slope_next = minmod(jump, jump_next)
            after = face(inner, following, slope, slope_next, along(CY, e))
            total = inner - (after - before)
            sea_x = coef[SEA, x0:x1 + 4, e]
            jx = (fx[1:] - fx[:-1]) * (sea_x[1:] * sea_x[:-1])
            sx = minmod(jx[:-1], jx[1:])
            flux = face(fx[1:n + 2], fx[2:n + 3], sx[:-1], sx[1:], coef[CX, x0 + 1:x1 + 2, e])
            total = total - (flux[1:] - flux[:-1])
            edge0, edge1 = edge[0, x0:x1, e], edge[1, x0:x1, e]
            below = jnp.where(row == 7, edge0, pltpu.roll(inner, 7, 1))
            jz = (below - inner) * along(OZ, e)
            sz = minmod(jnp.where(row == 0, edge0, pltpu.roll(jz, 1, 1)), jz)
            sz_next = jnp.where(row == 7, edge1, pltpu.roll(sz, 7, 1))
            down = face(inner, below, sz, sz_next, along(CZ, e)) - mix[...] * jz
            adv[x0:x1, y] = total - (down - jnp.where(row == 0, edge1, pltpu.roll(down, 1, 1)))
            return jump_next, slope_next, after

        return start, column

    def react(x, result):
        a = adv[x]
        att = 0.05 + 0.1 * a * a
        inc = att
        for step in (1, 2, 4):
            inc = inc + jnp.where(row >= step, pltpu.roll(inc, step, 1), 0.0)
        exc = (inc - att).reshape(256, 128)
        ahead = jnp.dot(jnp.concatenate(halves(exc), axis=1), own_mat[...], preferred_element_type=jnp.float32)
        past = jnp.dot(jnp.concatenate(halves(inc.reshape(256, 128)), axis=1), past_mat[...],
                       preferred_element_type=jnp.float32).reshape(YB, 8, 128)
        light = jnp.exp(-(ahead.reshape(YB, 8, 128) + past[:, 7:8, :]))
        both = jnp.dot(jnp.concatenate(halves(jnp.tanh(a).reshape(256, 128)), axis=1), wmat[...],
                       preferred_element_type=jnp.float32)
        response = (both[:, :128] + both[:, 128:]).reshape(YB, 8, 128)
        result[...] = a + coef[SEA, x + 2, 2:34] * ((0.5 + light) * response)

    fc2 = fc.reshape(X * YB * 8, 128)

    def give_back(h, quad):
        def turn_back(zr, carry):
            stack = [fc2[pl.ds(x * YB * 8 + zr, YB, stride=8), :] for x in quad]
            so2[pl.ds(h * 4 * NT * 8 + zr, 128, stride=8), :] = jnp.concatenate(stack, axis=0).T
            return carry

        lax.fori_loop(0, 8, turn_back, 0, unroll=8)

        def send_back(d, carry):
            to = lax.rem(g + d, G)
            pltpu.make_async_remote_copy(
                src_ref=so.at[h, :, pl.ds(2 * to, 2)], dst_ref=ro.at[h, block],
                send_sem=send_out.at[h], recv_sem=recv_out.at[h],
                device_id=(r, to), device_id_type=MESH).start()
            return carry

        lax.fori_loop(1, G, send_back, 0)
        pltpu.make_async_copy(so.at[h, :, pl.ds(2 * g, 2)], ro.at[h, block], local_sem.at[2 + h]).start()

    arrive_x(fa, 0)
    for h, quad in enumerate(QUADS):
        arrive_y(fa, 0, h)
        advect(fa, h)
        for x in quad:
            react(x, fb.at[x + 2, 2:34])
        if h == 0:
            x_halo(fb, 1, begin)
        y_halo(fb, 1, h)
    for h in (1, 0):
        if h == 0:
            arrive_x(fb, 1)
        arrive_y(fb, 1, h)
        advect(fb, h)
        for x in QUADS[h]:
            react(x, fc.at[x])
        give_back(h, QUADS[h])

    static_halo(lambda copy: copy.wait_send())
    edges_over(lambda copy: copy.wait_send())

    @pl.when(upper > 0)
    def _():
        landed(vel_pack, send_static.at[3])

    for s, f in ((0, fa), (1, fb)):
        x_halo(f, s, lambda copy: copy.wait_send())
        for h in range(2):
            sent_y(f, s, h)

    for h in (1, 0):
        some = ro.at[h, 0:G - 1]
        pltpu.make_async_copy(some, some, recv_out.at[h]).wait()
        pltpu.make_async_copy(so.at[h, :, pl.ds(2 * g, 2)], ro.at[h, block], local_sem.at[2 + h]).wait()

        def restore(n, carry, h=h, quad=QUADS[h]):
            t, zq = n // 4, n % 4
            for j in range(4):
                v = block_swap([ro[h, 4 * j + i, zq, t] for i in range(4)], lane)
                for x, b in zip(quad, v):
                    tout[j, pl.ds((t * NZ + zq * 8) * X + x, 8, stride=8), :] = b
            return carry

        lax.fori_loop(0, 8, restore, 0, unroll=4)

    for j in range(4):
        put(j).start()
    for h in range(2):
        some = sb.at[0:G - 1, h]
        pltpu.make_async_copy(some, some, send_in.at[h]).wait()
        some = ro.at[h, 0:G - 1]
        pltpu.make_async_copy(some, some, send_out.at[h]).wait()
    for j in range(4):
        put(j).wait()


def shards(tracers, velocity, sea_mask, coupling, mixing):
    anywhere = pl.BlockSpec(memory_space=pl.ANY)
    vmem = pl.BlockSpec(memory_space=pltpu.VMEM)
    f32 = jnp.float32
    dma = pltpu.SemaphoreType.DMA
    out = pl.pallas_call(
        kernel,
        out_shape=jax.ShapeDtypeStruct((2 * NZ * X, G * YB), f32),
        in_specs=[anywhere] * 3 + [anywhere, anywhere],
        out_specs=anywhere,
        scratch_shapes=[
            pltpu.VMEM((NT, NT), f32),
            pltpu.SMEM((NZ,), f32),
            pltpu.VMEM((4, NC, 128, 128), jnp.bfloat16),
            pltpu.VMEM((2, XE * 48, 128), jnp.bfloat16),
            pltpu.VMEM((256, 128), jnp.bfloat16),
            pltpu.VMEM((256, 128), jnp.bfloat16),
            pltpu.VMEM((8, 128), f32),
            pltpu.VMEM((256, 256), jnp.bfloat16),
            pltpu.VMEM((3, NZ, X, YB), f32),
            pltpu.VMEM((24, X, 128), f32),
            pltpu.VMEM((24, X, 128), f32),
            pltpu.VMEM((3, NZ, X, 128), jnp.int32),
            pltpu.VMEM((4, NZ, 16, 128), f32),
            pltpu.VMEM((8, NZ, 16, 128), f32),
            pltpu.VMEM((2, NZ, 128), f32),
            pltpu.VMEM((2, NZ, 128), f32),
            pltpu.VMEM((8, 128), f32),
            pltpu.VMEM((8, 128), f32),
            pltpu.VMEM((8, 128), f32),
            pltpu.VMEM((2, NZ, 128), f32),
            pltpu.VMEM((2, NZ, 128), f32),
            pltpu.VMEM((8, 128), f32),
            pltpu.VMEM((4, 2 * NZ * X, 128), f32),
            pltpu.VMEM((4, 2 * NZ * X, 128), f32),
            pltpu.VMEM((G, 2, 4, 2, 8, 128), f32),
            pltpu.VMEM((2, 4, NT, 8, 128), f32),
            pltpu.VMEM((XE, YE, 8, 128), f32),
            pltpu.VMEM((XE, YE, 8, 128), f32),
            pltpu.VMEM((X, YB, 8, 128), f32),
            pltpu.VMEM((X, YB, 8, 128), f32),
            pltpu.VMEM((2, X, YE, 8, 128), f32),
            pltpu.VMEM((NC, XE, YE, 8, 128), f32),
            pltpu.VMEM((2, 4, NT, 8, 128), f32),
            pltpu.VMEM((2, G, 4, 2, 8, 128), f32),
            dma((6,)), dma((5,)), dma((5,)),
            dma((4,)), dma((4,)), dma((2,)), dma((2,)), dma((2, 2)), dma((2, 2)), dma((2, 2, 2)), dma((2, 2, 2)), dma((2,)), dma((2,)), dma((4,)),
        ],
        compiler_params=pltpu.CompilerParams(
            collective_id=0, has_side_effects=True, vmem_limit_bytes=60 * 2**20),
    )(tracers.reshape(2 * NZ * X, G * YB), velocity, sea_mask, coupling, mixing)
    return out.reshape(tracers.shape)


def solution(mesh):
    placed = (
        P("group", None, "region", None),
        P(None, None, "region", "group"),
        P(None, "region", None),
        P(),
        P(),
    )
    return jax.shard_map(
        shards,
        mesh=mesh,
        in_specs=placed,
        out_specs=P("group", None, "region", None),
        check_vma=False,
    )
```

```python
import jax
import jax.numpy as jnp
from jax import lax
from jax.experimental import pallas as pl
from jax.experimental.pallas import tpu as pltpu
from jax.sharding import PartitionSpec as P

MESH = pl.DeviceIdType.MESH
STEPS = 2
NZ, NT, X, YB, G, R = 32, 32, 8, 32, 16, 8
XE, YE = X + 4, YB + 4
QUADS = ((0, 1, 6, 7), (2, 3, 4, 5))
RANGES = (((0, 2), (6, 8)), ((2, 6),))
NC = 5
CX, CY, CZ, SEA, OZ = range(NC)


def minmod(a, b):
    return jnp.maximum(jnp.minimum(a, b), jnp.minimum(jnp.maximum(a, b), 0.0))


def face(cell, following, slope, slope_following, c):
    forward = c > 0
    q = jnp.where(forward, 0.5, -0.5) - 0.5 * c
    return c * (jnp.where(forward, cell, following) + q * jnp.where(forward, slope, slope_following))


def halves(value):
    high = value.astype(jnp.bfloat16)
    return high, (value - high.astype(jnp.float32)).astype(jnp.bfloat16)


def block_swap(v, lane):
    low, even = lane < 64, (lane // 32) % 2 == 0
    axis = v[0].ndim - 1
    a = [None] * 4
    for n in (0, 1):
        a[n] = jnp.where(low, v[n], pltpu.roll(v[n + 2], 64, axis))
        a[n + 2] = jnp.where(low, pltpu.roll(v[n], 64, axis), v[n + 2])
    b = [None] * 4
    for n in (0, 2):
        b[n] = jnp.where(even, a[n], pltpu.roll(a[n + 1], 32, axis))
        b[n + 1] = jnp.where(even, pltpu.roll(a[n], 96, axis), a[n + 1])
    return b


def kernel(tr, velocity, mask, coupling_in, mixing_in, out,
           coupling, mixing, spread, stacked, own_mat, past_mat, mix, wmat, vel, vel_pack, vel_got, sea3, q, dc, pack_up, pack_down, pack_x, pack_y, got_x, got_low, got_high, got_y,
           tin, tout, sb, rb, fa, fb, fc, adv, edge, coef, so, ro,
           statics_in, send_static, recv_static,
           tiles_in, tiles_out, send_in, recv_in, send_halo, recv_x, send_y, recv_y, send_out, recv_out, local_sem):
    r, g = lax.axis_index("region"), lax.axis_index("group")
    upper = lax.div(r, R // 2)

    def flip(n, upper=upper):
        return n + upper * (2 - 4 * lax.rem(lax.div(n, 2), 2))

    block = flip(g)
    other = g + 2 - 4 * lax.rem(lax.div(g, 2), 2)
    g_next = jnp.where(r == R // 2 - 1, other, g)
    g_last = jnp.where(r == R // 2, other, g)
    lane = lax.broadcasted_iota(jnp.int32, (8, 128), 1)
    row = lax.broadcasted_iota(jnp.int32, (8, 128), 0)
    fa2, fb2 = fa.reshape(XE * YE * 8, 128), fb.reshape(XE * YE * 8, 128)
    rb2, so2 = rb.reshape(2 * 4 * NT * 8, 128), so.reshape(2 * 4 * NT * 8, 128)

    def fetch(j):
        return pltpu.make_async_copy(tr.at[:, pl.ds(j * 128, 128)], tin.at[j], tiles_in.at[j])

    def put(j):
        return pltpu.make_async_copy(tout.at[j], out.at[:, pl.ds(j * 128, 128)], tiles_out.at[j])

    at = lax.div(block, 4)
    spots = (at, jnp.maximum(at - 1, 0), jnp.minimum(at + 1, 3))
    fetches = [pltpu.make_async_copy(velocity, vel, statics_in.at[0]),
               pltpu.make_async_copy(coupling_in, coupling, statics_in.at[4]),
               pltpu.make_async_copy(mixing_in, mixing, statics_in.at[5])]
    for n, spot in enumerate(spots):
        fetches.append(pltpu.make_async_copy(
            mask.at[:, :, pl.ds(pl.multiple_of(spot * 128, 128), 128)], sea3.at[n], statics_in.at[n + 1]))
    for copy in fetches:
        copy.start()
    for j in range(4):
        fetch(j).start()

    for f in (fa, fb):
        f[0:2, 2:34] = jnp.zeros((2, 32, 8, 128), jnp.float32)
        f[10:12, 2:34] = jnp.zeros((2, 32, 8, 128), jnp.float32)
        f[2:10, 0:2] = jnp.zeros((8, 2, 8, 128), jnp.float32)
        f[2:10, 34:36] = jnp.zeros((8, 2, 8, 128), jnp.float32)

    barrier = pltpu.get_barrier_semaphore()

    def greet(d, carry):
        pl.semaphore_signal(barrier, inc=1, device_id=(r, lax.rem(g + d, G)), device_id_type=MESH)
        return carry

    lax.fori_loop(1, G, greet, 0)

    @pl.when(r > 0)
    def _():
        pl.semaphore_signal(barrier, inc=1, device_id=(r - 1, g_last), device_id_type=MESH)

    @pl.when(r > R // 2)
    def _():
        pl.semaphore_signal(barrier, inc=1, device_id=(r - 1, other), device_id_type=MESH)

    extra = jnp.where(jnp.logical_and(r >= R // 2, r < R - 1), 1, 0)

    @pl.when(r < R - 1)
    def _():
        pl.semaphore_signal(barrier, inc=1, device_id=(r + 1, g_next), device_id_type=MESH)

    for j in range(4):
        fetch(j).wait()

    def begin(copy):
        copy.start()

    def static_halo(do):
        @pl.when(r < R - 1)
        def _():
            do(pltpu.make_async_remote_copy(
                src_ref=pack_up, dst_ref=got_low, send_sem=send_static.at[0], recv_sem=recv_static.at[0],
                device_id=(r + 1, g_next), device_id_type=MESH))

        @pl.when(r > 0)
        def _():
            do(pltpu.make_async_remote_copy(
                src_ref=pack_down, dst_ref=got_high, send_sem=send_static.at[1], recv_sem=recv_static.at[1],
                device_id=(r - 1, g_last), device_id_type=MESH))

    def edges_over(do):
        @pl.when(r < R - 1)
        def _():
            to = flip(g, lax.div(r + 1, R // 2))
            do(pltpu.make_async_remote_copy(
                src_ref=pack_x, dst_ref=got_x, send_sem=send_static.at[4], recv_sem=recv_static.at[4],
                device_id=(r + 1, to), device_id_type=MESH))

        @pl.when(g < G - 1)
        def _():
            do(pltpu.make_async_remote_copy(
                src_ref=pack_y, dst_ref=got_y, send_sem=send_static.at[2], recv_sem=recv_static.at[2],
                device_id=(r, flip(g + 1)), device_id_type=MESH))

    def velocity_over(do, do_here):
        @pl.when(upper > 0)
        def _():
            do(pltpu.make_async_remote_copy(
                src_ref=vel_pack, dst_ref=vel_got, send_sem=send_static.at[3], recv_sem=recv_static.at[3],
                device_id=(r, block), device_id_type=MESH))

        @pl.when(upper == 0)
        def _():
            do_here(pltpu.make_async_copy(vel_pack, vel_got, recv_static.at[3]))

    fetches[0].wait()
    for k in range(3):
        for m in range(8):
            vel_pack[8 * k + m] = jnp.concatenate([vel[k, 4 * m + n] for n in range(4)], axis=1)
    pack_x[...] = vel_pack.reshape(24 * X, 128)[pl.ds(7, 8, stride=8), :]
    column = jnp.zeros((8, 128), jnp.float32)
    for m in range(8):
        column = jnp.where(lane % 32 == m, pltpu.roll(vel_pack[8 + m], m + 97, 1), column)
    pack_y[...] = column

    for h, quad in enumerate(QUADS):
        def regroup(n, carry, h=h, quad=quad):
            t, zq = n // 4, n % 4
            for j in range(4):
                v = [tin[j, pl.ds((t * NZ + zq * 8) * X + x, 8, stride=8), :] for x in quad]
                for i, b in enumerate(block_swap(v, lane)):
                    sb[4 * j + i, h, zq, t] = b
            return carry

        lax.fori_loop(0, 8, regroup, 0, unroll=4)
        if h == 0:
            pl.semaphore_wait(barrier, G - 1 + jnp.minimum(r, 1) + jnp.minimum(R - 1 - r, 1) + extra)
            velocity_over(begin, begin)
            edges_over(begin)

        def send(d, carry, h=h):
            to = lax.rem(g + d, G)
            pltpu.make_async_remote_copy(
                src_ref=sb.at[flip(to), h], dst_ref=rb.at[h, :, pl.ds(2 * g, 2)],
                send_sem=send_in.at[h], recv_sem=recv_in.at[h],
                device_id=(r, to), device_id_type=MESH).start()
            return carry

        lax.fori_loop(1, G, send, 0)
        pltpu.make_async_copy(sb.at[block, h], rb.at[h, :, pl.ds(2 * g, 2)], local_sem.at[h]).start()

    q[...] = jnp.zeros(q.shape, jnp.float32)
    for copy in fetches[1:]:
        copy.wait()
    velocity_over(lambda copy: copy.wait_recv(), lambda copy: copy.wait())
    for n in range(4):
        shifted = pltpu.roll(vel_got[...], (130 - 32 * n) % 128, 2)
        shifted = jnp.where(jnp.logical_and(lane >= 2, lane < 34), shifted, 0.0)
        for k in range(3):
            for m in range(8):
                q[k, 4 * m + n, 2:10, :] = shifted[8 * k + m]
    place = lax.rem(block, 4)
    has_left = jnp.minimum(at, 1).astype(jnp.float32)
    has_right = jnp.minimum(3 - at, 1).astype(jnp.float32)
    centre = sea3[0].astype(jnp.float32)
    left = sea3[1].astype(jnp.float32) * has_left
    right = sea3[2].astype(jnp.float32) * has_right
    centre = jnp.where(jnp.logical_and(lane >= 126, place == 0), left, centre)
    centre = jnp.where(jnp.logical_and(lane < 2, place == 3), right, centre)
    q[3, :, 2:10, :] = pltpu.roll(centre, lax.rem(130 - 32 * place, 128), 2)

    def level_rows(k, e):
        return q.at[k].reshape(NZ * 16, 128)[pl.ds(e, NZ, stride=16), :]

    def put_rows(k, e, value):
        q.at[k].reshape(NZ * 16, 128)[pl.ds(e, NZ, stride=16), :] = value

    pack_up[0], pack_up[1] = level_rows(3, 8), level_rows(3, 9)
    pack_down[0], pack_down[1] = level_rows(3, 2), level_rows(3, 3)

    static_halo(begin)

    def iota(shape, axis):
        return lax.broadcasted_iota(jnp.int32, shape, axis)

    square = (128, 128)
    block_in, block_out = iota(square, 0) // 32, iota(square, 1) // 32
    tall = (256, 128)
    part_at, block_at = iota(tall, 0) % 32, iota(tall, 1) // 32
    for k in range(NC):
        place_k = part_at - (block_at + (24 + 4 * (k - 3) if k >= 3 else 4 * k))
        hit = place_k == 0 if k >= 3 else jnp.logical_or(place_k == 0, place_k == 12)
        spread[:, k * 128:(k + 1) * 128] = jnp.where(hit, 1.0, 0.0).astype(jnp.bfloat16)
    first = iota(square, 0) % 32 == 0
    own = jnp.where(jnp.logical_and(first, block_in == block_out), 1.0, 0.0).astype(jnp.bfloat16)
    past = jnp.where(jnp.logical_and(first, block_in < block_out), 1.0, 0.0).astype(jnp.bfloat16)
    own_mat[...] = jnp.concatenate([own, own], 0)
    past_mat[...] = jnp.concatenate([past, past], 0)
    across = jnp.concatenate([coupling[...].T] * 4, 1)
    weights = jnp.where(block_in == block_out, jnp.concatenate([across] * 4, 0), 0.0)
    high, low = halves(weights)
    wmat[...] = jnp.concatenate([jnp.concatenate([high, low], 1), jnp.concatenate([high, jnp.zeros_like(low)], 1)], 0)
    tile = jnp.zeros((8, 128), jnp.float32)
    for z in range(NZ):
        tile = jnp.where(jnp.logical_and(row == z % 8, lane // 32 == z // 8), mixing[z], tile)
    mix[...] = tile

    @pl.when(r > 0)
    def _():
        pltpu.make_async_copy(got_low, got_low, recv_static.at[0]).wait()
        put_rows(3, 0, got_low[0])
        put_rows(3, 1, got_low[1])
        pltpu.make_async_copy(got_x, got_x, recv_static.at[4]).wait()
        for n in range(4):
            q.at[0].reshape(NZ * 16, 128)[pl.ds(n * 16 + 1, 8, stride=64), :] = jnp.where(
                jnp.logical_and(lane >= 2, lane < 34), pltpu.roll(got_x[...], (130 - 32 * n) % 128, 1), 0.0)

    @pl.when(r < R - 1)
    def _():
        pltpu.make_async_copy(got_high, got_high, recv_static.at[1]).wait()
        put_rows(3, 10, got_high[0])
        put_rows(3, 11, got_high[1])

    @pl.when(block > 0)
    def _():
        pltpu.make_async_copy(got_y, got_y, recv_static.at[2]).wait()

        def unpack_level(z, carry):
            q[1, z, 2:10, :] = jnp.where(
                lane == 1, pltpu.roll(got_y[...], lax.rem(129 - lax.div(z, 4) - 32 * lax.rem(z, 4) + 128, 128), 1), q[1, z, 2:10, :])
            return carry

        lax.fori_loop(0, NZ, unpack_level, 0, unroll=8)

    sea = q[3]
    follow = (pltpu.roll(sea, 15, 1), pltpu.roll(sea, 127, 2),
              jnp.concatenate([sea[1:], jnp.zeros((1, 16, 128), jnp.float32)], 0))
    for k in range(3):
        opened = sea * follow[k]
        c = q[k] * opened
        high = c.astype(jnp.bfloat16).astype(jnp.float32)
        dc[k] = high
        dc[3 + k] = c - high
    dc[6] = sea
    dc[7] = opened

    def stack_one(e, carry):
        for half in range(2):
            rows = [dc.reshape(8 * NZ * 16, 128)[pl.ds((half * 4 + n) * 16 + e, 32, stride=128), :] for n in range(4)]
            stacked[pl.ds(pl.multiple_of(e * 40, 8), 40), half * 128:(half + 1) * 128] = (
                jnp.concatenate(rows, axis=0).T[:40])
        return carry

    own_lanes = iota((8, 256), 0) == iota((8, 256), 1) // 32

    def spread_some(n, carry):
        value = stacked[pl.ds(pl.multiple_of(n * 160, 8), 160), :]
        value = jnp.where(own_lanes, jnp.broadcast_to(value[:, None, :], (160, 8, 256)), 0.0)
        wide = jnp.dot(value.reshape(1280, 256).astype(jnp.bfloat16), spread[...], preferred_element_type=jnp.float32)
        for m in range(4):
            for k in range(NC):
                coef[k, 4 * n + m] = wide[m * 320:m * 320 + YE * 8, k * 128:(k + 1) * 128].reshape(YE, 8, 128)
        return carry

    def x_halo(f, s, do):
        @pl.when(r > 0)
        def _():
            do(pltpu.make_async_remote_copy(
                src_ref=f.at[2:4, 2:34], dst_ref=f.at[10:12, 2:34],
                send_sem=send_halo.at[s, 0], recv_sem=recv_x.at[s, 1],
                device_id=(r - 1, g_last), device_id_type=MESH))

        @pl.when(r < R - 1)
        def _():
            do(pltpu.make_async_remote_copy(
                src_ref=f.at[8:10, 2:34], dst_ref=f.at[0:2, 2:34],
                send_sem=send_halo.at[s, 1], recv_sem=recv_x.at[s, 0],
                device_id=(r + 1, g_next), device_id_type=MESH))

    def y_halo(f, s, h):
        @pl.when(block > 0)
        def _():
            for x0, x1 in RANGES[h]:
                pltpu.make_async_remote_copy(
                    src_ref=f.at[x0 + 2:x1 + 2, 2:4], dst_ref=f.at[x0 + 2:x1 + 2, 34:36],
                    send_sem=send_y.at[s, h, 1], recv_sem=recv_y.at[s, h, 1],
                    device_id=(r, flip(block - 1)), device_id_type=MESH).start()

        @pl.when(block < G - 1)
        def _():
            for x0, x1 in RANGES[h]:
                pltpu.make_async_remote_copy(
                    src_ref=f.at[x0 + 2:x1 + 2, 32:34], dst_ref=f.at[x0 + 2:x1 + 2, 0:2],
                    send_sem=send_y.at[s, h, 0], recv_sem=recv_y.at[s, h, 0],
                    device_id=(r, flip(block + 1)), device_id_type=MESH).start()

    def landed(ref, sem):
        pltpu.make_async_copy(ref, ref, sem).wait()

    def arrive_x(f, s):
        @pl.when(r > 0)
        def _():
            landed(f.at[0:2, 2:34], recv_x.at[s, 0])

        @pl.when(r < R - 1)
        def _():
            landed(f.at[10:12, 2:34], recv_x.at[s, 1])

    def arrive_y(f, s, h):
        @pl.when(block > 0)
        def _():
            landed(f.at[2:6, 0:2], recv_y.at[s, h, 0])

        @pl.when(block < G - 1)
        def _():
            landed(f.at[2:6, 34:36], recv_y.at[s, h, 1])

    def sent_y(f, s, h):
        @pl.when(block > 0)
        def _():
            landed(f.at[2:6, 2:4], send_y.at[s, h, 1])

        @pl.when(block < G - 1)
        def _():
            landed(f.at[2:6, 32:34], send_y.at[s, h, 0])

    for h, quad in enumerate(QUADS):
        some = rb.at[h, :, 0:2 * (G - 1)]
        pltpu.make_async_copy(some, some, recv_in.at[h]).wait()
        pltpu.make_async_copy(sb.at[block, h], rb.at[h, :, pl.ds(2 * g, 2)], local_sem.at[h]).wait()

        def turn(zr, carry, h=h, quad=quad):
            turned = rb2[pl.ds(h * 4 * NT * 8 + zr, 128, stride=8), :].T
            for n, x in enumerate(quad):
                fa2[pl.ds(((x + 2) * YE + 2) * 8 + zr, YB, stride=8), :] = turned[n * YB:(n + 1) * YB]
            return carry

        lax.fori_loop(0, 8, turn, 0, unroll=8)
        if h == 0:
            x_halo(fa, 0, begin)
        y_halo(fa, 0, h)
        if h == 0:
            lax.fori_loop(0, XE, stack_one, 0, unroll=2)
            lax.fori_loop(0, XE // 4, spread_some, 0)

    def z_edges(f, x0, x1):
        def rows(ref, k):
            return ref.reshape(ref.shape[0] * ref.shape[1] * 8, 128)[pl.ds((x0 + 2) * YE * 8 + k, (x1 - x0) * YE, stride=8), :]

        def static(k, n):
            return rows(coef.at[k], n)

        next0 = pltpu.roll(rows(f, 0), 96, 1)
        next1 = pltpu.roll(rows(f, 1), 96, 1)
        last = rows(f, 7)
        jump = (next0 - last) * static(OZ, 7)
        slope = minmod((last - rows(f, 6)) * static(OZ, 6), jump)
        slope_next = minmod(jump, (next1 - next0) * pltpu.roll(static(OZ, 0), 96, 1))
        flux = face(last, next0, slope, slope_next, static(CZ, 7)) - mix[7:8, :] * jump
        for n, k, v in ((0, 7, next0), (0, 0, pltpu.roll(jump, 32, 1)), (1, 7, slope_next), (1, 0, pltpu.roll(flux, 32, 1))):
            edge.at[n].reshape(X * YE * 8, 128)[pl.ds(x0 * YE * 8 + k, (x1 - x0) * YE, stride=8), :] = v

    def advect(f, h):
        parts = [advect_part(f, x0, x1) for x0, x1 in RANGES[h]]

        def column(y, carry):
            return tuple(step(y, c) for (_, step), c in zip(parts, carry))

        lax.fori_loop(0, YB, column, tuple(start for start, _ in parts), unroll=2)

    def advect_part(f, x0, x1):
        z_edges(f, x0, x1)
        n = x1 - x0

        def cells(e):
            return f[x0 + 2:x1 + 2, e]

        def along(k, e):
            return coef[k, x0 + 2:x1 + 2, e]

        def open_y(e):
            return along(SEA, e) * along(SEA, e + 1)

        f1, f2 = cells(1), cells(2)
        j0 = (f1 - cells(0)) * open_y(0)
        j1 = (f2 - f1) * open_y(1)
        j2 = (cells(3) - f2) * open_y(2)
        s1, s2 = minmod(j0, j1), minmod(j1, j2)
        start = (j2, s2, face(f1, f2, s1, s2, along(CY, 1)))

        def column(y, carry):
            jump, slope, before = carry
            e = y + 2
            fx = f[x0:x1 + 4, e]
            inner, following = fx[2:n + 2], cells(e + 1)
            jump_next = (cells(e + 2) - following) * open_y(e + 1)
            slope_next = minmod(jump, jump_next)
            after = face(inner, following, slope, slope_next, along(CY, e))
            total = inner - (after - before)
            sea_x = coef[SEA, x0:x1 + 4, e]
            jx = (fx[1:] - fx[:-1]) * (sea_x[1:] * sea_x[:-1])
            sx = minmod(jx[:-1], jx[1:])
            flux = face(fx[1:n + 2], fx[2:n + 3], sx[:-1], sx[1:], coef[CX, x0 + 1:x1 + 2, e])
            total = total - (flux[1:] - flux[:-1])
            edge0, edge1 = edge[0, x0:x1, e], edge[1, x0:x1, e]
            below = jnp.where(row == 7, edge0, pltpu.roll(inner, 7, 1))
            jz = (below - inner) * along(OZ, e)
            sz = minmod(jnp.where(row == 0, edge0, pltpu.roll(jz, 1, 1)), jz)
            sz_next = jnp.where(row == 7, edge1, pltpu.roll(sz, 7, 1))
            down = face(inner, below, sz, sz_next, along(CZ, e)) - mix[...] * jz
            adv[x0:x1, y] = total - (down - jnp.where(row == 0, edge1, pltpu.roll(down, 1, 1)))
            return jump_next, slope_next, after

        return start, column

    def react(h, results):
        count = 4 * YB
        a = jnp.concatenate([adv[x0:x1].reshape((x1 - x0) * YB, 8, 128) for x0, x1 in RANGES[h]], axis=0)
        att = 0.05 + 0.1 * a * a
        inc = att
        for step in (1, 2, 4):
            inc = inc + jnp.where(row >= step, pltpu.roll(inc, step, 1), 0.0)

        def spread_over(value, matrix):
            parts = jnp.concatenate(halves(value.reshape(count * 8, 128)), axis=1)
            return jnp.dot(parts, matrix[...], preferred_element_type=jnp.float32)

        both = spread_over(jnp.tanh(a), wmat)
        ahead = spread_over(inc - att, own_mat).reshape(count, 8, 128)
        past = spread_over(inc, past_mat).reshape(count, 8, 128)
        light = jnp.exp(-(ahead + past[:, 7:8, :]))
        response = (both[:, :128] + both[:, 128:]).reshape(count, 8, 128)
        change = (0.5 + light) * response
        for n, (x, result) in enumerate(zip(QUADS[h], results)):
            part = slice(n * YB, (n + 1) * YB)
            result[...] = a[part] + coef[SEA, x + 2, 2:34] * change[part]

    fc2 = fc.reshape(X * YB * 8, 128)

    def give_back(h, quad):
        def turn_back(zr, carry):
            stack = [fc2[pl.ds(x * YB * 8 + zr, YB, stride=8), :] for x in quad]
            so2[pl.ds(h * 4 * NT * 8 + zr, 128, stride=8), :] = jnp.concatenate(stack, axis=0).T
            return carry

        lax.fori_loop(0, 8, turn_back, 0, unroll=8)

        def send_back(d, carry):
            to = lax.rem(g + d, G)
            pltpu.make_async_remote_copy(
                src_ref=so.at[h, :, pl.ds(2 * to, 2)], dst_ref=ro.at[h, block],
                send_sem=send_out.at[h], recv_sem=recv_out.at[h],
                device_id=(r, to), device_id_type=MESH).start()
            return carry

        lax.fori_loop(1, G, send_back, 0)
        pltpu.make_async_copy(so.at[h, :, pl.ds(2 * g, 2)], ro.at[h, block], local_sem.at[2 + h]).start()

    for h in (1, 0):
        if h == 0:
            arrive_x(fa, 0)
        arrive_y(fa, 0, h)
        advect(fa, h)
        react(h, [fb.at[x + 2, 2:34] for x in QUADS[h]])
        if h == 0:
            x_halo(fb, 1, begin)
        y_halo(fb, 1, h)
    for h in (1, 0):
        if h == 0:
            arrive_x(fb, 1)
        arrive_y(fb, 1, h)
        advect(fb, h)
        react(h, [fc.at[x] for x in QUADS[h]])
        give_back(h, QUADS[h])

    static_halo(lambda copy: copy.wait_send())
    edges_over(lambda copy: copy.wait_send())

    @pl.when(upper > 0)
    def _():
        landed(vel_pack, send_static.at[3])

    for s, f in ((0, fa), (1, fb)):
        x_halo(f, s, lambda copy: copy.wait_send())
        for h in range(2):
            sent_y(f, s, h)

    for h in (1, 0):
        some = ro.at[h, 0:G - 1]
        pltpu.make_async_copy(some, some, recv_out.at[h]).wait()
        pltpu.make_async_copy(so.at[h, :, pl.ds(2 * g, 2)], ro.at[h, block], local_sem.at[2 + h]).wait()

        def restore(n, carry, h=h, quad=QUADS[h]):
            t, zq = n // 4, n % 4
            for j in range(4):
                v = block_swap([ro[h, 4 * j + i, zq, t] for i in range(4)], lane)
                for x, b in zip(quad, v):
                    tout[j, pl.ds((t * NZ + zq * 8) * X + x, 8, stride=8), :] = b
            return carry

        lax.fori_loop(0, 8, restore, 0, unroll=4)

    for j in range(4):
        put(j).start()
    for h in range(2):
        some = sb.at[0:G - 1, h]
        pltpu.make_async_copy(some, some, send_in.at[h]).wait()
        some = ro.at[h, 0:G - 1]
        pltpu.make_async_copy(some, some, send_out.at[h]).wait()
    for j in range(4):
        put(j).wait()


def shards(tracers, velocity, sea_mask, coupling, mixing):
    anywhere = pl.BlockSpec(memory_space=pl.ANY)
    vmem = pl.BlockSpec(memory_space=pltpu.VMEM)
    f32 = jnp.float32
    dma = pltpu.SemaphoreType.DMA
    out = pl.pallas_call(
        kernel,
        out_shape=jax.ShapeDtypeStruct((2 * NZ * X, G * YB), f32),
        in_specs=[anywhere] * 3 + [anywhere, anywhere],
        out_specs=anywhere,
        scratch_shapes=[
            pltpu.VMEM((NT, NT), f32),
            pltpu.SMEM((NZ,), f32),
            pltpu.VMEM((256, NC * 128), jnp.bfloat16),
            pltpu.VMEM((XE * 40, 256), f32),
            pltpu.VMEM((256, 128), jnp.bfloat16),
            pltpu.VMEM((256, 128), jnp.bfloat16),
            pltpu.VMEM((8, 128), f32),
            pltpu.VMEM((256, 256), jnp.bfloat16),
            pltpu.VMEM((3, NZ, X, YB), f32),
            pltpu.VMEM((24, X, 128), f32),
            pltpu.VMEM((24, X, 128), f32),
            pltpu.VMEM((3, NZ, X, 128), jnp.int32),
            pltpu.VMEM((4, NZ, 16, 128), f32),
            pltpu.VMEM((8, NZ, 16, 128), f32),
            pltpu.VMEM((2, NZ, 128), f32),
            pltpu.VMEM((2, NZ, 128), f32),
            pltpu.VMEM((8, 128), f32),
            pltpu.VMEM((8, 128), f32),
            pltpu.VMEM((8, 128), f32),
            pltpu.VMEM((2, NZ, 128), f32),
            pltpu.VMEM((2, NZ, 128), f32),
            pltpu.VMEM((8, 128), f32),
            pltpu.VMEM((4, 2 * NZ * X, 128), f32),
            pltpu.VMEM((4, 2 * NZ * X, 128), f32),
            pltpu.VMEM((G, 2, 4, 2, 8, 128), f32),
            pltpu.VMEM((2, 4, NT, 8, 128), f32),
            pltpu.VMEM((XE, YE, 8, 128), f32),
            pltpu.VMEM((XE, YE, 8, 128), f32),
            pltpu.VMEM((X, YB, 8, 128), f32),
            pltpu.VMEM((X, YB, 8, 128), f32),
            pltpu.VMEM((2, X, YE, 8, 128), f32),
            pltpu.VMEM((NC, XE, YE, 8, 128), f32),
            pltpu.VMEM((2, 4, NT, 8, 128), f32),
            pltpu.VMEM((2, G, 4, 2, 8, 128), f32),
            dma((6,)), dma((5,)), dma((5,)),
            dma((4,)), dma((4,)), dma((2,)), dma((2,)), dma((2, 2)), dma((2, 2)), dma((2, 2, 2)), dma((2, 2, 2)), dma((2,)), dma((2,)), dma((4,)),
        ],
        compiler_params=pltpu.CompilerParams(
            collective_id=0, has_side_effects=True, vmem_limit_bytes=60 * 2**20),
    )(tracers.reshape(2 * NZ * X, G * YB), velocity, sea_mask, coupling, mixing)
    return out.reshape(tracers.shape)


def solution(mesh):
    placed = (
        P("group", None, "region", None),
        P(None, None, "region", "group"),
        P(None, "region", None),
        P(),
        P(),
    )
    return jax.shard_map(
        shards,
        mesh=mesh,
        in_specs=placed,
        out_specs=P("group", None, "region", None),
        check_vma=False,
    )
```

```python
import jax
import jax.numpy as jnp
from jax import lax
from jax.experimental import pallas as pl
from jax.experimental.pallas import tpu as pltpu
from jax.sharding import PartitionSpec as P

MESH = pl.DeviceIdType.MESH
STEPS = 2
NZ, NT, X, YB, G, R = 32, 32, 8, 32, 16, 8
XE, YE = X + 4, YB + 4
QUADS = ((0, 1, 6, 7), (2, 3, 4, 5))
RANGES = (((0, 2), (6, 8)), ((2, 6),))
NC = 5
CX, CY, CZ, SEA, OZ = range(NC)


def minmod(a, b):
    return jnp.maximum(jnp.minimum(a, b), jnp.minimum(jnp.maximum(a, b), 0.0))


def face(cell, following, slope, slope_following, c):
    forward = c > 0
    q = jnp.where(forward, 0.5, -0.5) - 0.5 * c
    return c * (jnp.where(forward, cell, following) + q * jnp.where(forward, slope, slope_following))


def halves(value):
    high = value.astype(jnp.bfloat16)
    return high, (value - high.astype(jnp.float32)).astype(jnp.bfloat16)


def block_swap(v, lane):
    low, even = lane < 64, (lane // 32) % 2 == 0
    axis = v[0].ndim - 1
    a = [None] * 4
    for n in (0, 1):
        a[n] = jnp.where(low, v[n], pltpu.roll(v[n + 2], 64, axis))
        a[n + 2] = jnp.where(low, pltpu.roll(v[n], 64, axis), v[n + 2])
    b = [None] * 4
    for n in (0, 2):
        b[n] = jnp.where(even, a[n], pltpu.roll(a[n + 1], 32, axis))
        b[n + 1] = jnp.where(even, pltpu.roll(a[n], 96, axis), a[n + 1])
    return b


def kernel(tr, velocity, mask, coupling_in, mixing_in, out,
           coupling, mixing, spread, stacked, own_mat, past_mat, mix, wmat, vel, vel_pack, vel_got, sea3, q, dc, pack_up, pack_down, pack_x, pack_y, got_x, got_low, got_high, got_y,
           tin, tout, sb, rb, fa, fb, fc, adv, edge, coef, so, ro,
           statics_in, send_static, recv_static,
           tiles_in, tiles_out, send_in, recv_in, send_halo, recv_x, send_y, recv_y, send_out, recv_out, local_sem):
    r, g = lax.axis_index("region"), lax.axis_index("group")
    upper = lax.div(r, R // 2)

    def flip(n, upper=upper):
        return n + upper * (2 - 4 * lax.rem(lax.div(n, 2), 2))

    block = flip(g)
    other = g + 2 - 4 * lax.rem(lax.div(g, 2), 2)
    g_next = jnp.where(r == R // 2 - 1, other, g)
    g_last = jnp.where(r == R // 2, other, g)
    lane = lax.broadcasted_iota(jnp.int32, (8, 128), 1)
    row = lax.broadcasted_iota(jnp.int32, (8, 128), 0)
    fa2, fb2 = fa.reshape(XE * YE * 8, 128), fb.reshape(XE * YE * 8, 128)
    rb2, so2 = rb.reshape(2 * 4 * NT * 8, 128), so.reshape(2 * 4 * NT * 8, 128)

    def fetch(j):
        return pltpu.make_async_copy(tr.at[:, pl.ds(j * 128, 128)], tin.at[j], tiles_in.at[j])

    def put(j):
        return pltpu.make_async_copy(tout.at[j], out.at[:, pl.ds(j * 128, 128)], tiles_out.at[j])

    at = lax.div(block, 4)
    spots = (at, jnp.maximum(at - 1, 0), jnp.minimum(at + 1, 3))
    fetches = [pltpu.make_async_copy(velocity, vel, statics_in.at[0]),
               pltpu.make_async_copy(coupling_in, coupling, statics_in.at[4]),
               pltpu.make_async_copy(mixing_in, mixing, statics_in.at[5])]
    for n, spot in enumerate(spots):
        fetches.append(pltpu.make_async_copy(
            mask.at[:, :, pl.ds(pl.multiple_of(spot * 128, 128), 128)], sea3.at[n], statics_in.at[n + 1]))
    for copy in fetches:
        copy.start()
    for j in range(4):
        fetch(j).start()

    for f in (fa, fb):
        f[0:2, 2:34] = jnp.zeros((2, 32, 8, 128), jnp.float32)
        f[10:12, 2:34] = jnp.zeros((2, 32, 8, 128), jnp.float32)
        f[2:10, 0:2] = jnp.zeros((8, 2, 8, 128), jnp.float32)
        f[2:10, 34:36] = jnp.zeros((8, 2, 8, 128), jnp.float32)

    barrier = pltpu.get_barrier_semaphore()

    def greet(d, carry):
        pl.semaphore_signal(barrier, inc=1, device_id=(r, lax.rem(g + d, G)), device_id_type=MESH)
        return carry

    lax.fori_loop(1, G, greet, 0)

    @pl.when(r > 0)
    def _():
        pl.semaphore_signal(barrier, inc=1, device_id=(r - 1, g_last), device_id_type=MESH)

    @pl.when(r > R // 2)
    def _():
        pl.semaphore_signal(barrier, inc=1, device_id=(r - 1, other), device_id_type=MESH)

    extra = jnp.where(jnp.logical_and(r >= R // 2, r < R - 1), 1, 0)

    @pl.when(r < R - 1)
    def _():
        pl.semaphore_signal(barrier, inc=1, device_id=(r + 1, g_next), device_id_type=MESH)

    for j in range(4):
        fetch(j).wait()

    def begin(copy):
        copy.start()

    def static_halo(do):
        @pl.when(r < R - 1)
        def _():
            do(pltpu.make_async_remote_copy(
                src_ref=pack_up, dst_ref=got_low, send_sem=send_static.at[0], recv_sem=recv_static.at[0],
                device_id=(r + 1, g_next), device_id_type=MESH))

        @pl.when(r > 0)
        def _():
            do(pltpu.make_async_remote_copy(
                src_ref=pack_down, dst_ref=got_high, send_sem=send_static.at[1], recv_sem=recv_static.at[1],
                device_id=(r - 1, g_last), device_id_type=MESH))

    def edges_over(do):
        @pl.when(r < R - 1)
        def _():
            to = flip(g, lax.div(r + 1, R // 2))
            do(pltpu.make_async_remote_copy(
                src_ref=pack_x, dst_ref=got_x, send_sem=send_static.at[4], recv_sem=recv_static.at[4],
                device_id=(r + 1, to), device_id_type=MESH))

        @pl.when(g < G - 1)
        def _():
            do(pltpu.make_async_remote_copy(
                src_ref=pack_y, dst_ref=got_y, send_sem=send_static.at[2], recv_sem=recv_static.at[2],
                device_id=(r, flip(g + 1)), device_id_type=MESH))

    def velocity_over(do, do_here):
        @pl.when(upper > 0)
        def _():
            do(pltpu.make_async_remote_copy(
                src_ref=vel_pack, dst_ref=vel_got, send_sem=send_static.at[3], recv_sem=recv_static.at[3],
                device_id=(r, block), device_id_type=MESH))

        @pl.when(upper == 0)
        def _():
            do_here(pltpu.make_async_copy(vel_pack, vel_got, recv_static.at[3]))

    fetches[0].wait()
    for k in range(3):
        for m in range(8):
            vel_pack[8 * k + m] = jnp.concatenate([vel[k, 4 * m + n] for n in range(4)], axis=1)
    pack_x[...] = vel_pack.reshape(24 * X, 128)[pl.ds(7, 8, stride=8), :]
    column = jnp.zeros((8, 128), jnp.float32)
    for m in range(8):
        column = jnp.where(lane % 32 == m, pltpu.roll(vel_pack[8 + m], m + 97, 1), column)
    pack_y[...] = column

    for h, quad in enumerate(QUADS):
        def regroup(n, carry, h=h, quad=quad):
            t, zq = n // 4, n % 4
            for j in range(4):
                v = [tin[j, pl.ds((t * NZ + zq * 8) * X + x, 8, stride=8), :] for x in quad]
                for i, b in enumerate(block_swap(v, lane)):
                    sb[4 * j + i, h, zq, t] = b
            return carry

        lax.fori_loop(0, 8, regroup, 0, unroll=4)
        if h == 0:
            pl.semaphore_wait(barrier, G - 1 + jnp.minimum(r, 1) + jnp.minimum(R - 1 - r, 1) + extra)
            velocity_over(begin, begin)
            edges_over(begin)

        def send(d, carry, h=h):
            to = lax.rem(g + d, G)
            pltpu.make_async_remote_copy(
                src_ref=sb.at[flip(to), h], dst_ref=rb.at[h, :, pl.ds(2 * g, 2)],
                send_sem=send_in.at[h], recv_sem=recv_in.at[h],
                device_id=(r, to), device_id_type=MESH).start()
            return carry

        lax.fori_loop(1, G, send, 0)
        pltpu.make_async_copy(sb.at[block, h], rb.at[h, :, pl.ds(2 * g, 2)], local_sem.at[h]).start()

    q[...] = jnp.zeros(q.shape, jnp.float32)
    for copy in fetches[1:]:
        copy.wait()
    velocity_over(lambda copy: copy.wait_recv(), lambda copy: copy.wait())
    for n in range(4):
        shifted = pltpu.roll(vel_got[...], (130 - 32 * n) % 128, 2)
        shifted = jnp.where(jnp.logical_and(lane >= 2, lane < 34), shifted, 0.0)
        for k in range(3):
            for m in range(8):
                q[k, 4 * m + n, 2:10, :] = shifted[8 * k + m]
    place = lax.rem(block, 4)
    has_left = jnp.minimum(at, 1).astype(jnp.float32)
    has_right = jnp.minimum(3 - at, 1).astype(jnp.float32)
    centre = sea3[0].astype(jnp.float32)
    left = sea3[1].astype(jnp.float32) * has_left
    right = sea3[2].astype(jnp.float32) * has_right
    centre = jnp.where(jnp.logical_and(lane >= 126, place == 0), left, centre)
    centre = jnp.where(jnp.logical_and(lane < 2, place == 3), right, centre)
    q[3, :, 2:10, :] = pltpu.roll(centre, lax.rem(130 - 32 * place, 128), 2)

    def level_rows(k, e):
        return q.at[k].reshape(NZ * 16, 128)[pl.ds(e, NZ, stride=16), :]

    def put_rows(k, e, value):
        q.at[k].reshape(NZ * 16, 128)[pl.ds(e, NZ, stride=16), :] = value

    pack_up[0], pack_up[1] = level_rows(3, 8), level_rows(3, 9)
    pack_down[0], pack_down[1] = level_rows(3, 2), level_rows(3, 3)

    static_halo(begin)

    def iota(shape, axis):
        return lax.broadcasted_iota(jnp.int32, shape, axis)

    square = (128, 128)
    block_in, block_out = iota(square, 0) // 32, iota(square, 1) // 32
    tall = (256, 128)
    part_at, block_at = iota(tall, 0) % 32, iota(tall, 1) // 32
    for k in range(NC):
        place_k = part_at - (block_at + (24 + 4 * (k - 3) if k >= 3 else 4 * k))
        hit = place_k == 0 if k >= 3 else jnp.logical_or(place_k == 0, place_k == 12)
        spread[:, k * 128:(k + 1) * 128] = jnp.where(hit, 1.0, 0.0).astype(jnp.bfloat16)
    first = iota(square, 0) % 32 == 0
    own = jnp.where(jnp.logical_and(first, block_in == block_out), 1.0, 0.0).astype(jnp.bfloat16)
    past = jnp.where(jnp.logical_and(first, block_in < block_out), 1.0, 0.0).astype(jnp.bfloat16)
    own_mat[...] = jnp.concatenate([own, own], 0)
    past_mat[...] = jnp.concatenate([past, past], 0)
    across = jnp.concatenate([coupling[...].T] * 4, 1)
    weights = jnp.where(block_in == block_out, jnp.concatenate([across] * 4, 0), 0.0)
    high, low = halves(weights)
    wmat[...] = jnp.concatenate([jnp.concatenate([high, low], 1), jnp.concatenate([high, jnp.zeros_like(low)], 1)], 0)
    tile = jnp.zeros((8, 128), jnp.float32)
    for z in range(NZ):
        tile = jnp.where(jnp.logical_and(row == z % 8, lane // 32 == z // 8), mixing[z], tile)
    mix[...] = tile

    @pl.when(r > 0)
    def _():
        pltpu.make_async_copy(got_low, got_low, recv_static.at[0]).wait()
        put_rows(3, 0, got_low[0])
        put_rows(3, 1, got_low[1])
        pltpu.make_async_copy(got_x, got_x, recv_static.at[4]).wait()
        for n in range(4):
            q.at[0].reshape(NZ * 16, 128)[pl.ds(n * 16 + 1, 8, stride=64), :] = jnp.where(
                jnp.logical_and(lane >= 2, lane < 34), pltpu.roll(got_x[...], (130 - 32 * n) % 128, 1), 0.0)

    @pl.when(r < R - 1)
    def _():
        pltpu.make_async_copy(got_high, got_high, recv_static.at[1]).wait()
        put_rows(3, 10, got_high[0])
        put_rows(3, 11, got_high[1])

    @pl.when(block > 0)
    def _():
        pltpu.make_async_copy(got_y, got_y, recv_static.at[2]).wait()

        def unpack_level(z, carry):
            q[1, z, 2:10, :] = jnp.where(
                lane == 1, pltpu.roll(got_y[...], lax.rem(129 - lax.div(z, 4) - 32 * lax.rem(z, 4) + 128, 128), 1), q[1, z, 2:10, :])
            return carry

        lax.fori_loop(0, NZ, unpack_level, 0, unroll=8)

    sea = q[3]
    follow = (pltpu.roll(sea, 15, 1), pltpu.roll(sea, 127, 2),
              jnp.concatenate([sea[1:], jnp.zeros((1, 16, 128), jnp.float32)], 0))
    for k in range(3):
        opened = sea * follow[k]
        c = q[k] * opened
        high = c.astype(jnp.bfloat16).astype(jnp.float32)
        dc[k] = high
        dc[3 + k] = c - high
    dc[6] = sea
    dc[7] = opened

    def stack_one(e, carry):
        for half in range(2):
            rows = [dc.reshape(8 * NZ * 16, 128)[pl.ds((half * 4 + n) * 16 + e, 32, stride=128), :] for n in range(4)]
            stacked[pl.ds(pl.multiple_of(e * 40, 8), 40), half * 128:(half + 1) * 128] = (
                jnp.concatenate(rows, axis=0).T[:40])
        return carry

    own_lanes = iota((8, 256), 0) == iota((8, 256), 1) // 32

    def spread_some(n, carry):
        value = stacked[pl.ds(pl.multiple_of(n * 160, 8), 160), :]
        value = jnp.where(own_lanes, jnp.broadcast_to(value[:, None, :], (160, 8, 256)), 0.0)
        wide = jnp.dot(value.reshape(1280, 256).astype(jnp.bfloat16), spread[...], preferred_element_type=jnp.float32)
        for m in range(4):
            for k in range(NC):
                coef[k, 4 * n + m] = wide[m * 320:m * 320 + YE * 8, k * 128:(k + 1) * 128].reshape(YE, 8, 128)
        return carry

    def x_halo(f, s, y0, y1):
        @pl.when(r > 0)
        def _():
            pltpu.make_async_remote_copy(
                src_ref=f.at[2:4, y0 + 2:y1 + 2], dst_ref=f.at[10:12, y0 + 2:y1 + 2],
                send_sem=send_halo.at[s, 0], recv_sem=recv_x.at[s, 1],
                device_id=(r - 1, g_last), device_id_type=MESH).start()

        @pl.when(r < R - 1)
        def _():
            pltpu.make_async_remote_copy(
                src_ref=f.at[8:10, y0 + 2:y1 + 2], dst_ref=f.at[0:2, y0 + 2:y1 + 2],
                send_sem=send_halo.at[s, 1], recv_sem=recv_x.at[s, 0],
                device_id=(r + 1, g_next), device_id_type=MESH).start()

    def y_halo(f, s, h):
        @pl.when(block > 0)
        def _():
            for x0, x1 in RANGES[h]:
                pltpu.make_async_remote_copy(
                    src_ref=f.at[x0 + 2:x1 + 2, 2:4], dst_ref=f.at[x0 + 2:x1 + 2, 34:36],
                    send_sem=send_y.at[s, h, 1], recv_sem=recv_y.at[s, h, 1],
                    device_id=(r, flip(block - 1)), device_id_type=MESH).start()

        @pl.when(block < G - 1)
        def _():
            for x0, x1 in RANGES[h]:
                pltpu.make_async_remote_copy(
                    src_ref=f.at[x0 + 2:x1 + 2, 32:34], dst_ref=f.at[x0 + 2:x1 + 2, 0:2],
                    send_sem=send_y.at[s, h, 0], recv_sem=recv_y.at[s, h, 0],
                    device_id=(r, flip(block + 1)), device_id_type=MESH).start()

    def landed(ref, sem):
        pltpu.make_async_copy(ref, ref, sem).wait()

    def sent_x(f, s):
        @pl.when(r > 0)
        def _():
            landed(f.at[2:4, 2:34], send_halo.at[s, 0])

        @pl.when(r < R - 1)
        def _():
            landed(f.at[8:10, 2:34], send_halo.at[s, 1])

    def arrive_x(f, s):
        @pl.when(r > 0)
        def _():
            landed(f.at[0:2, 2:34], recv_x.at[s, 0])

        @pl.when(r < R - 1)
        def _():
            landed(f.at[10:12, 2:34], recv_x.at[s, 1])

    def arrive_y(f, s, h):
        @pl.when(block > 0)
        def _():
            landed(f.at[2:6, 0:2], recv_y.at[s, h, 0])

        @pl.when(block < G - 1)
        def _():
            landed(f.at[2:6, 34:36], recv_y.at[s, h, 1])

    def sent_y(f, s, h):
        @pl.when(block > 0)
        def _():
            landed(f.at[2:6, 2:4], send_y.at[s, h, 1])

        @pl.when(block < G - 1)
        def _():
            landed(f.at[2:6, 32:34], send_y.at[s, h, 0])

    for h, quad in enumerate(QUADS):
        some = rb.at[h, :, 0:2 * (G - 1)]
        pltpu.make_async_copy(some, some, recv_in.at[h]).wait()
        pltpu.make_async_copy(sb.at[block, h], rb.at[h, :, pl.ds(2 * g, 2)], local_sem.at[h]).wait()

        def turn(zr, carry, h=h, quad=quad):
            turned = rb2[pl.ds(h * 4 * NT * 8 + zr, 128, stride=8), :].T
            for n, x in enumerate(quad):
                fa2[pl.ds(((x + 2) * YE + 2) * 8 + zr, YB, stride=8), :] = turned[n * YB:(n + 1) * YB]
            return carry

        lax.fori_loop(0, 8, turn, 0, unroll=8)
        if h == 0:
            x_halo(fa, 0, 0, YB)
        y_halo(fa, 0, h)
        if h == 0:
            lax.fori_loop(0, XE, stack_one, 0, unroll=2)

    def z_edges(f, x0, x1):
        def rows(ref, k):
            return ref.reshape(ref.shape[0] * ref.shape[1] * 8, 128)[pl.ds((x0 + 2) * YE * 8 + k, (x1 - x0) * YE, stride=8), :]

        def static(k, n):
            return rows(coef.at[k], n)

        next0 = pltpu.roll(rows(f, 0), 96, 1)
        next1 = pltpu.roll(rows(f, 1), 96, 1)
        last = rows(f, 7)
        jump = (next0 - last) * static(OZ, 7)
        slope = minmod((last - rows(f, 6)) * static(OZ, 6), jump)
        slope_next = minmod(jump, (next1 - next0) * pltpu.roll(static(OZ, 0), 96, 1))
        flux = face(last, next0, slope, slope_next, static(CZ, 7)) - mix[7:8, :] * jump
        for n, k, v in ((0, 7, next0), (0, 0, pltpu.roll(jump, 32, 1)), (1, 7, slope_next), (1, 0, pltpu.roll(flux, 32, 1))):
            edge.at[n].reshape(X * YE * 8, 128)[pl.ds(x0 * YE * 8 + k, (x1 - x0) * YE, stride=8), :] = v

    def advect(f, h, then):
        parts = [advect_part(f, x0, x1) for x0, x1 in RANGES[h]]

        def column(y, carry):
            return tuple(step(y, c) for (_, step), c in zip(parts, carry))

        carry = tuple(start for start, _ in parts)
        for y0, y1 in ((0, YB // 2), (YB // 2, YB)):
            carry = lax.fori_loop(y0, y1, column, carry, unroll=4)
            then(y0, y1)

    def advect_part(f, x0, x1):
        z_edges(f, x0, x1)
        n = x1 - x0

        def cells(e):
            return f[x0 + 2:x1 + 2, e]

        def along(k, e):
            return coef[k, x0 + 2:x1 + 2, e]

        def open_y(e):
            return along(SEA, e) * along(SEA, e + 1)

        f1, f2 = cells(1), cells(2)
        j0 = (f1 - cells(0)) * open_y(0)
        j1 = (f2 - f1) * open_y(1)
        j2 = (cells(3) - f2) * open_y(2)
        s1, s2 = minmod(j0, j1), minmod(j1, j2)
        start = (j2, s2, face(f1, f2, s1, s2, along(CY, 1)))

        def column(y, carry):
            jump, slope, before = carry
            e = y + 2
            fx = f[x0:x1 + 4, e]
            inner, following = fx[2:n + 2], cells(e + 1)
            jump_next = (cells(e + 2) - following) * open_y(e + 1)
            slope_next = minmod(jump, jump_next)
            after = face(inner, following, slope, slope_next, along(CY, e))
            total = inner - (after - before)
            sea_x = coef[SEA, x0:x1 + 4, e]
            jx = (fx[1:] - fx[:-1]) * (sea_x[1:] * sea_x[:-1])
            sx = minmod(jx[:-1], jx[1:])
            flux = face(fx[1:n + 2], fx[2:n + 3], sx[:-1], sx[1:], coef[CX, x0 + 1:x1 + 2, e])
            total = total - (flux[1:] - flux[:-1])
            edge0, edge1 = edge[0, x0:x1, e], edge[1, x0:x1, e]
            below = jnp.where(row == 7, edge0, pltpu.roll(inner, 7, 1))
            jz = (below - inner) * along(OZ, e)
            sz = minmod(jnp.where(row == 0, edge0, pltpu.roll(jz, 1, 1)), jz)
            sz_next = jnp.where(row == 7, edge1, pltpu.roll(sz, 7, 1))
            down = face(inner, below, sz, sz_next, along(CZ, e)) - mix[...] * jz
            adv[x0:x1, y] = total - (down - jnp.where(row == 0, edge1, pltpu.roll(down, 1, 1)))
            return jump_next, slope_next, after

        return start, column

    def react(h, results, y0, y1):
        length = y1 - y0
        count = 4 * length
        a = jnp.concatenate([adv[x0:x1, y0:y1].reshape((x1 - x0) * length, 8, 128) for x0, x1 in RANGES[h]], axis=0)
        att = 0.05 + 0.1 * a * a
        inc = att
        for step in (1, 2, 4):
            inc = inc + jnp.where(row >= step, pltpu.roll(inc, step, 1), 0.0)

        def spread_over(value, matrix):
            parts = jnp.concatenate(halves(value.reshape(count * 8, 128)), axis=1)
            return jnp.dot(parts, matrix[...], preferred_element_type=jnp.float32)

        both = spread_over(jnp.tanh(a), wmat)
        ahead = spread_over(inc - att, own_mat).reshape(count, 8, 128)
        past = spread_over(inc, past_mat).reshape(count, 8, 128)
        light = jnp.exp(-(ahead + past[:, 7:8, :]))
        response = (both[:, :128] + both[:, 128:]).reshape(count, 8, 128)
        change = (0.5 + light) * response
        for n, (x, result) in enumerate(zip(QUADS[h], results)):
            part = slice(n * length, (n + 1) * length)
            result[...] = a[part] + coef[SEA, x + 2, y0 + 2:y1 + 2] * change[part]

    fc2 = fc.reshape(X * YB * 8, 128)

    def give_back(h, quad):
        def turn_back(zr, carry):
            stack = [fc2[pl.ds(x * YB * 8 + zr, YB, stride=8), :] for x in quad]
            so2[pl.ds(h * 4 * NT * 8 + zr, 128, stride=8), :] = jnp.concatenate(stack, axis=0).T
            return carry

        lax.fori_loop(0, 8, turn_back, 0, unroll=8)

        def send_back(d, carry):
            to = lax.rem(g + d, G)
            pltpu.make_async_remote_copy(
                src_ref=so.at[h, :, pl.ds(2 * to, 2)], dst_ref=ro.at[h, block],
                send_sem=send_out.at[h], recv_sem=recv_out.at[h],
                device_id=(r, to), device_id_type=MESH).start()
            return carry

        lax.fori_loop(1, G, send_back, 0)
        pltpu.make_async_copy(so.at[h, :, pl.ds(2 * g, 2)], ro.at[h, block], local_sem.at[2 + h]).start()

    lax.fori_loop(0, XE // 4, spread_some, 0)

    for h in (1, 0):
        if h == 0:
            arrive_x(fa, 0)
        arrive_y(fa, 0, h)

        def step_1(y0, y1, h=h):
            if h == 1:
                if y1 == YB:
                    react(h, [fb.at[x + 2, 2:34] for x in QUADS[h]], 0, YB)
            else:
                react(h, [fb.at[x + 2, y0 + 2:y1 + 2] for x in QUADS[h]], y0, y1)
                x_halo(fb, 1, y0, y1)

        advect(fa, h, step_1)
        y_halo(fb, 1, h)
    for h in (1, 0):
        if h == 0:
            arrive_x(fb, 1)
        arrive_y(fb, 1, h)
        advect(fb, h, lambda y0, y1: None)
        react(h, [fc.at[x] for x in QUADS[h]], 0, YB)
        give_back(h, QUADS[h])

    static_halo(lambda copy: copy.wait_send())
    edges_over(lambda copy: copy.wait_send())

    @pl.when(upper > 0)
    def _():
        landed(vel_pack, send_static.at[3])

    for s, f in ((0, fa), (1, fb)):
        sent_x(f, s)
        for h in range(2):
            sent_y(f, s, h)

    for h in (1, 0):
        some = ro.at[h, 0:G - 1]
        pltpu.make_async_copy(some, some, recv_out.at[h]).wait()
        pltpu.make_async_copy(so.at[h, :, pl.ds(2 * g, 2)], ro.at[h, block], local_sem.at[2 + h]).wait()

        def restore(n, carry, h=h, quad=QUADS[h]):
            t, zq = n // 4, n % 4
            for j in range(4):
                v = block_swap([ro[h, 4 * j + i, zq, t] for i in range(4)], lane)
                for x, b in zip(quad, v):
                    tout[j, pl.ds((t * NZ + zq * 8) * X + x, 8, stride=8), :] = b
            return carry

        lax.fori_loop(0, 8, restore, 0, unroll=4)

    for j in range(4):
        put(j).start()
    for h in range(2):
        some = sb.at[0:G - 1, h]
        pltpu.make_async_copy(some, some, send_in.at[h]).wait()
        some = ro.at[h, 0:G - 1]
        pltpu.make_async_copy(some, some, send_out.at[h]).wait()
    for j in range(4):
        put(j).wait()


def shards(tracers, velocity, sea_mask, coupling, mixing):
    anywhere = pl.BlockSpec(memory_space=pl.ANY)
    vmem = pl.BlockSpec(memory_space=pltpu.VMEM)
    f32 = jnp.float32
    dma = pltpu.SemaphoreType.DMA
    out = pl.pallas_call(
        kernel,
        out_shape=jax.ShapeDtypeStruct((2 * NZ * X, G * YB), f32),
        in_specs=[anywhere] * 3 + [anywhere, anywhere],
        out_specs=anywhere,
        scratch_shapes=[
            pltpu.VMEM((NT, NT), f32),
            pltpu.SMEM((NZ,), f32),
            pltpu.VMEM((256, NC * 128), jnp.bfloat16),
            pltpu.VMEM((XE * 40, 256), f32),
            pltpu.VMEM((256, 128), jnp.bfloat16),
            pltpu.VMEM((256, 128), jnp.bfloat16),
            pltpu.VMEM((8, 128), f32),
            pltpu.VMEM((256, 256), jnp.bfloat16),
            pltpu.VMEM((3, NZ, X, YB), f32),
            pltpu.VMEM((24, X, 128), f32),
            pltpu.VMEM((24, X, 128), f32),
            pltpu.VMEM((3, NZ, X, 128), jnp.int32),
            pltpu.VMEM((4, NZ, 16, 128), f32),
            pltpu.VMEM((8, NZ, 16, 128), f32),
            pltpu.VMEM((2, NZ, 128), f32),
            pltpu.VMEM((2, NZ, 128), f32),
            pltpu.VMEM((8, 128), f32),
            pltpu.VMEM((8, 128), f32),
            pltpu.VMEM((8, 128), f32),
            pltpu.VMEM((2, NZ, 128), f32),
            pltpu.VMEM((2, NZ, 128), f32),
            pltpu.VMEM((8, 128), f32),
            pltpu.VMEM((4, 2 * NZ * X, 128), f32),
            pltpu.VMEM((4, 2 * NZ * X, 128), f32),
            pltpu.VMEM((G, 2, 4, 2, 8, 128), f32),
            pltpu.VMEM((2, 4, NT, 8, 128), f32),
            pltpu.VMEM((XE, YE, 8, 128), f32),
            pltpu.VMEM((XE, YE, 8, 128), f32),
            pltpu.VMEM((X, YB, 8, 128), f32),
            pltpu.VMEM((X, YB, 8, 128), f32),
            pltpu.VMEM((2, X, YE, 8, 128), f32),
            pltpu.VMEM((NC, XE, YE, 8, 128), f32),
            pltpu.VMEM((2, 4, NT, 8, 128), f32),
            pltpu.VMEM((2, G, 4, 2, 8, 128), f32),
            dma((6,)), dma((5,)), dma((5,)),
            dma((4,)), dma((4,)), dma((2,)), dma((2,)), dma((2, 2)), dma((2, 2)), dma((2, 2, 2)), dma((2, 2, 2)), dma((2,)), dma((2,)), dma((4,)),
        ],
        compiler_params=pltpu.CompilerParams(
            collective_id=0, has_side_effects=True, vmem_limit_bytes=60 * 2**20),
    )(tracers.reshape(2 * NZ * X, G * YB), velocity, sea_mask, coupling, mixing)
    return out.reshape(tracers.shape)


def solution(mesh):
    placed = (
        P("group", None, "region", None),
        P(None, None, "region", "group"),
        P(None, "region", None),
        P(),
        P(),
    )
    return jax.shard_map(
        shards,
        mesh=mesh,
        in_specs=placed,
        out_specs=P("group", None, "region", None),
        check_vma=False,
    )
```

```python
import jax
import jax.numpy as jnp
from jax import lax
from jax.experimental import pallas as pl
from jax.experimental.pallas import tpu as pltpu
from jax.sharding import PartitionSpec as P

MESH = pl.DeviceIdType.MESH
STEPS = 2
NZ, NT, X, YB, G, R = 32, 32, 8, 32, 16, 8
XE, YE = X + 4, YB + 4
QUADS = ((0, 1, 6, 7), (2, 3, 4, 5))
RANGES = (((0, 2), (6, 8)), ((2, 6),))
NC = 5
CX, CY, CZ, SEA, OZ = range(NC)


def minmod(a, b):
    return jnp.maximum(jnp.minimum(a, b), jnp.minimum(jnp.maximum(a, b), 0.0))


def face(cell, following, slope, slope_following, c):
    forward = c > 0
    q = jnp.where(forward, 0.5, -0.5) - 0.5 * c
    return c * (jnp.where(forward, cell, following) + q * jnp.where(forward, slope, slope_following))


def halves(value):
    high = value.astype(jnp.bfloat16)
    return high, (value - high.astype(jnp.float32)).astype(jnp.bfloat16)


def block_swap(v, lane):
    low, even = lane < 64, (lane // 32) % 2 == 0
    axis = v[0].ndim - 1
    a = [None] * 4
    for n in (0, 1):
        a[n] = jnp.where(low, v[n], pltpu.roll(v[n + 2], 64, axis))
        a[n + 2] = jnp.where(low, pltpu.roll(v[n], 64, axis), v[n + 2])
    b = [None] * 4
    for n in (0, 2):
        b[n] = jnp.where(even, a[n], pltpu.roll(a[n + 1], 32, axis))
        b[n + 1] = jnp.where(even, pltpu.roll(a[n], 96, axis), a[n + 1])
    return b


def kernel(tr, velocity, mask, coupling_in, mixing_in, out,
           coupling, mixing, spread, stacked, own_mat, past_mat, mix, wmat, vel, vel_pack, vel_got, sea3, q, dc, pack_up, pack_down, pack_x, pack_y, got_x, got_low, got_high, got_y,
           tin, tout, sb, rb, fa, fb, fc, adv, edge, coef, so, ro,
           statics_in, send_static, recv_static,
           tiles_in, tiles_out, send_in, recv_in, send_halo, recv_x, send_y, recv_y, send_out, recv_out, local_sem):
    r, g = lax.axis_index("region"), lax.axis_index("group")
    upper = lax.div(r, R // 2)

    def flip(n, upper=upper):
        return n + upper * (2 - 4 * lax.rem(lax.div(n, 2), 2))

    block = flip(g)
    other = g + 2 - 4 * lax.rem(lax.div(g, 2), 2)
    g_next = jnp.where(r == R // 2 - 1, other, g)
    g_last = jnp.where(r == R // 2, other, g)
    lane = lax.broadcasted_iota(jnp.int32, (8, 128), 1)
    row = lax.broadcasted_iota(jnp.int32, (8, 128), 0)
    fa2, fb2 = fa.reshape(XE * YE * 8, 128), fb.reshape(XE * YE * 8, 128)
    rb2, so2 = rb.reshape(2 * 4 * NT * 8, 128), so.reshape(2 * 4 * NT * 8, 128)

    def fetch(j):
        return pltpu.make_async_copy(tr.at[:, pl.ds(j * 128, 128)], tin.at[j], tiles_in.at[j])

    def put(j):
        return pltpu.make_async_copy(tout.at[j], out.at[:, pl.ds(j * 128, 128)], tiles_out.at[j])

    at = lax.div(block, 4)
    spots = (at, jnp.maximum(at - 1, 0), jnp.minimum(at + 1, 3))
    fetches = [pltpu.make_async_copy(velocity, vel, statics_in.at[0]),
               pltpu.make_async_copy(coupling_in, coupling, statics_in.at[4]),
               pltpu.make_async_copy(mixing_in, mixing, statics_in.at[5])]
    for n, spot in enumerate(spots):
        fetches.append(pltpu.make_async_copy(
            mask.at[:, :, pl.ds(pl.multiple_of(spot * 128, 128), 128)], sea3.at[n], statics_in.at[n + 1]))
    for copy in fetches:
        copy.start()
    for j in range(4):
        fetch(j).start()

    for f in (fa, fb):
        f[0:2, 2:34] = jnp.zeros((2, 32, 8, 128), jnp.float32)
        f[10:12, 2:34] = jnp.zeros((2, 32, 8, 128), jnp.float32)
        f[2:10, 0:2] = jnp.zeros((8, 2, 8, 128), jnp.float32)
        f[2:10, 34:36] = jnp.zeros((8, 2, 8, 128), jnp.float32)

    barrier = pltpu.get_barrier_semaphore()

    def greet(d, carry):
        pl.semaphore_signal(barrier, inc=1, device_id=(r, lax.rem(g + d, G)), device_id_type=MESH)
        return carry

    lax.fori_loop(1, G, greet, 0)

    @pl.when(r > 0)
    def _():
        pl.semaphore_signal(barrier, inc=1, device_id=(r - 1, g_last), device_id_type=MESH)

    @pl.when(r > R // 2)
    def _():
        pl.semaphore_signal(barrier, inc=1, device_id=(r - 1, other), device_id_type=MESH)

    extra = jnp.where(jnp.logical_and(r >= R // 2, r < R - 1), 1, 0)

    @pl.when(r < R - 1)
    def _():
        pl.semaphore_signal(barrier, inc=1, device_id=(r + 1, g_next), device_id_type=MESH)

    for j in range(4):
        fetch(j).wait()

    def begin(copy):
        copy.start()

    def static_halo(do):
        @pl.when(r < R - 1)
        def _():
            do(pltpu.make_async_remote_copy(
                src_ref=pack_up, dst_ref=got_low, send_sem=send_static.at[0], recv_sem=recv_static.at[0],
                device_id=(r + 1, g_next), device_id_type=MESH))

        @pl.when(r > 0)
        def _():
            do(pltpu.make_async_remote_copy(
                src_ref=pack_down, dst_ref=got_high, send_sem=send_static.at[1], recv_sem=recv_static.at[1],
                device_id=(r - 1, g_last), device_id_type=MESH))

    def edges_over(do):
        @pl.when(r < R - 1)
        def _():
            to = flip(g, lax.div(r + 1, R // 2))
            do(pltpu.make_async_remote_copy(
                src_ref=pack_x, dst_ref=got_x, send_sem=send_static.at[4], recv_sem=recv_static.at[4],
                device_id=(r + 1, to), device_id_type=MESH))

        @pl.when(g < G - 1)
        def _():
            do(pltpu.make_async_remote_copy(
                src_ref=pack_y, dst_ref=got_y, send_sem=send_static.at[2], recv_sem=recv_static.at[2],
                device_id=(r, flip(g + 1)), device_id_type=MESH))

    def velocity_over(do, do_here):
        @pl.when(upper > 0)
        def _():
            do(pltpu.make_async_remote_copy(
                src_ref=vel_pack, dst_ref=vel_got, send_sem=send_static.at[3], recv_sem=recv_static.at[3],
                device_id=(r, block), device_id_type=MESH))

        @pl.when(upper == 0)
        def _():
            do_here(pltpu.make_async_copy(vel_pack, vel_got, recv_static.at[3]))

    fetches[0].wait()
    for k in range(3):
        for m in range(8):
            vel_pack[8 * k + m] = jnp.concatenate([vel[k, 4 * m + n] for n in range(4)], axis=1)
    pack_x[...] = vel_pack.reshape(24 * X, 128)[pl.ds(7, 8, stride=8), :]
    column = jnp.zeros((8, 128), jnp.float32)
    for m in range(8):
        column = jnp.where(lane % 32 == m, pltpu.roll(vel_pack[8 + m], m + 97, 1), column)
    pack_y[...] = column

    for h, quad in enumerate(QUADS):
        def regroup(n, carry, h=h, quad=quad):
            t, zq = n // 4, n % 4
            for j in range(4):
                v = [tin[j, pl.ds((t * NZ + zq * 8) * X + x, 8, stride=8), :] for x in quad]
                for i, b in enumerate(block_swap(v, lane)):
                    sb[4 * j + i, h, zq, t] = b
            return carry

        lax.fori_loop(0, 8, regroup, 0, unroll=4)
        if h == 0:
            pl.semaphore_wait(barrier, G - 1 + jnp.minimum(r, 1) + jnp.minimum(R - 1 - r, 1) + extra)
            velocity_over(begin, begin)
            edges_over(begin)

        def send(d, carry, h=h):
            to = lax.rem(g + d, G)
            pltpu.make_async_remote_copy(
                src_ref=sb.at[flip(to), h], dst_ref=rb.at[h, :, pl.ds(2 * g, 2)],
                send_sem=send_in.at[h], recv_sem=recv_in.at[h],
                device_id=(r, to), device_id_type=MESH).start()
            return carry

        lax.fori_loop(1, G, send, 0)
        pltpu.make_async_copy(sb.at[block, h], rb.at[h, :, pl.ds(2 * g, 2)], local_sem.at[h]).start()

    q[...] = jnp.zeros(q.shape, jnp.float32)
    for copy in fetches[1:]:
        copy.wait()
    velocity_over(lambda copy: copy.wait_recv(), lambda copy: copy.wait())
    for n in range(4):
        shifted = pltpu.roll(vel_got[...], (130 - 32 * n) % 128, 2)
        shifted = jnp.where(jnp.logical_and(lane >= 2, lane < 34), shifted, 0.0)
        for k in range(3):
            for m in range(8):
                q[k, 4 * m + n, 2:10, :] = shifted[8 * k + m]
    place = lax.rem(block, 4)
    has_left = jnp.minimum(at, 1).astype(jnp.float32)
    has_right = jnp.minimum(3 - at, 1).astype(jnp.float32)
    centre = sea3[0].astype(jnp.float32)
    left = sea3[1].astype(jnp.float32) * has_left
    right = sea3[2].astype(jnp.float32) * has_right
    centre = jnp.where(jnp.logical_and(lane >= 126, place == 0), left, centre)
    centre = jnp.where(jnp.logical_and(lane < 2, place == 3), right, centre)
    q[3, :, 2:10, :] = pltpu.roll(centre, lax.rem(130 - 32 * place, 128), 2)

    def level_rows(k, e):
        return q.at[k].reshape(NZ * 16, 128)[pl.ds(e, NZ, stride=16), :]

    def put_rows(k, e, value):
        q.at[k].reshape(NZ * 16, 128)[pl.ds(e, NZ, stride=16), :] = value

    pack_up[0], pack_up[1] = level_rows(3, 8), level_rows(3, 9)
    pack_down[0], pack_down[1] = level_rows(3, 2), level_rows(3, 3)

    static_halo(begin)

    def iota(shape, axis):
        return lax.broadcasted_iota(jnp.int32, shape, axis)

    square = (128, 128)
    block_in, block_out = iota(square, 0) // 32, iota(square, 1) // 32
    tall = (256, 128)
    part_at, block_at = iota(tall, 0) % 32, iota(tall, 1) // 32
    for k in range(NC):
        place_k = part_at - (block_at + (24 + 4 * (k - 3) if k >= 3 else 4 * k))
        hit = place_k == 0 if k >= 3 else jnp.logical_or(place_k == 0, place_k == 12)
        spread[:, k * 128:(k + 1) * 128] = jnp.where(hit, 1.0, 0.0).astype(jnp.bfloat16)
    first = iota(square, 0) % 32 == 0
    own = jnp.where(jnp.logical_and(first, block_in == block_out), 1.0, 0.0).astype(jnp.bfloat16)
    past = jnp.where(jnp.logical_and(first, block_in < block_out), 1.0, 0.0).astype(jnp.bfloat16)
    own_mat[...] = jnp.concatenate([own, own], 0)
    past_mat[...] = jnp.concatenate([past, past], 0)
    across = jnp.concatenate([coupling[...].T] * 4, 1)
    weights = jnp.where(block_in == block_out, jnp.concatenate([across] * 4, 0), 0.0)
    high, low = halves(weights)
    wmat[...] = jnp.concatenate([jnp.concatenate([high, low], 1), jnp.concatenate([high, jnp.zeros_like(low)], 1)], 0)
    tile = jnp.zeros((8, 128), jnp.float32)
    for z in range(NZ):
        tile = jnp.where(jnp.logical_and(row == z % 8, lane // 32 == z // 8), mixing[z], tile)
    mix[...] = tile

    @pl.when(r > 0)
    def _():
        pltpu.make_async_copy(got_low, got_low, recv_static.at[0]).wait()
        put_rows(3, 0, got_low[0])
        put_rows(3, 1, got_low[1])
        pltpu.make_async_copy(got_x, got_x, recv_static.at[4]).wait()
        for n in range(4):
            q.at[0].reshape(NZ * 16, 128)[pl.ds(n * 16 + 1, 8, stride=64), :] = jnp.where(
                jnp.logical_and(lane >= 2, lane < 34), pltpu.roll(got_x[...], (130 - 32 * n) % 128, 1), 0.0)

    @pl.when(r < R - 1)
    def _():
        pltpu.make_async_copy(got_high, got_high, recv_static.at[1]).wait()
        put_rows(3, 10, got_high[0])
        put_rows(3, 11, got_high[1])

    @pl.when(block > 0)
    def _():
        pltpu.make_async_copy(got_y, got_y, recv_static.at[2]).wait()

        def unpack_level(z, carry):
            q[1, z, 2:10, :] = jnp.where(
                lane == 1, pltpu.roll(got_y[...], lax.rem(129 - lax.div(z, 4) - 32 * lax.rem(z, 4) + 128, 128), 1), q[1, z, 2:10, :])
            return carry

        lax.fori_loop(0, NZ, unpack_level, 0, unroll=8)

    sea = q[3]
    follow = (pltpu.roll(sea, 15, 1), pltpu.roll(sea, 127, 2),
              jnp.concatenate([sea[1:], jnp.zeros((1, 16, 128), jnp.float32)], 0))
    for k in range(3):
        opened = sea * follow[k]
        c = q[k] * opened
        high = c.astype(jnp.bfloat16).astype(jnp.float32)
        dc[k] = high
        dc[3 + k] = c - high
    dc[6] = sea
    dc[7] = opened

    def stack_one(e, carry):
        for half in range(2):
            rows = [dc.reshape(8 * NZ * 16, 128)[pl.ds((half * 4 + n) * 16 + e, 32, stride=128), :] for n in range(4)]
            stacked[pl.ds(pl.multiple_of(e * 40, 8), 40), half * 128:(half + 1) * 128] = (
                jnp.concatenate(rows, axis=0).T[:40])
        return carry

    own_lanes = iota((8, 256), 0) == iota((8, 256), 1) // 32

    def spread_some(n, carry):
        value = stacked[pl.ds(pl.multiple_of(n * 160, 8), 160), :]
        value = jnp.where(own_lanes, jnp.broadcast_to(value[:, None, :], (160, 8, 256)), 0.0)
        wide = jnp.dot(value.reshape(1280, 256).astype(jnp.bfloat16), spread[...], preferred_element_type=jnp.float32)
        for m in range(4):
            for k in range(NC):
                coef[k, 4 * n + m] = wide[m * 320:m * 320 + YE * 8, k * 128:(k + 1) * 128].reshape(YE, 8, 128)
        return carry

    def x_halo(f, s, y0, y1):
        slot = s + y0 // (YB // 2)

        @pl.when(r > 0)
        def _():
            pltpu.make_async_remote_copy(
                src_ref=f.at[2:4, y0 + 2:y1 + 2], dst_ref=f.at[10:12, y0 + 2:y1 + 2],
                send_sem=send_halo.at[s, 0], recv_sem=recv_x.at[slot, 1],
                device_id=(r - 1, g_last), device_id_type=MESH).start()

        @pl.when(r < R - 1)
        def _():
            pltpu.make_async_remote_copy(
                src_ref=f.at[8:10, y0 + 2:y1 + 2], dst_ref=f.at[0:2, y0 + 2:y1 + 2],
                send_sem=send_halo.at[s, 1], recv_sem=recv_x.at[slot, 0],
                device_id=(r + 1, g_next), device_id_type=MESH).start()

    def y_halo(f, s, h):
        @pl.when(block > 0)
        def _():
            for x0, x1 in RANGES[h]:
                pltpu.make_async_remote_copy(
                    src_ref=f.at[x0 + 2:x1 + 2, 2:4], dst_ref=f.at[x0 + 2:x1 + 2, 34:36],
                    send_sem=send_y.at[s, h, 1], recv_sem=recv_y.at[s, h, 1],
                    device_id=(r, flip(block - 1)), device_id_type=MESH).start()

        @pl.when(block < G - 1)
        def _():
            for x0, x1 in RANGES[h]:
                pltpu.make_async_remote_copy(
                    src_ref=f.at[x0 + 2:x1 + 2, 32:34], dst_ref=f.at[x0 + 2:x1 + 2, 0:2],
                    send_sem=send_y.at[s, h, 0], recv_sem=recv_y.at[s, h, 0],
                    device_id=(r, flip(block + 1)), device_id_type=MESH).start()

    def landed(ref, sem):
        pltpu.make_async_copy(ref, ref, sem).wait()

    def sent_x(f, s):
        @pl.when(r > 0)
        def _():
            landed(f.at[2:4, 2:34], send_halo.at[s, 0])

        @pl.when(r < R - 1)
        def _():
            landed(f.at[8:10, 2:34], send_halo.at[s, 1])

    def arrive_x(f, s, y0, y1):
        slot = s + y0 // (YB // 2)

        @pl.when(r > 0)
        def _():
            landed(f.at[0:2, y0 + 2:y1 + 2], recv_x.at[slot, 0])

        @pl.when(r < R - 1)
        def _():
            landed(f.at[10:12, y0 + 2:y1 + 2], recv_x.at[slot, 1])

    def arrive_y(f, s, h):
        @pl.when(block > 0)
        def _():
            landed(f.at[2:6, 0:2], recv_y.at[s, h, 0])

        @pl.when(block < G - 1)
        def _():
            landed(f.at[2:6, 34:36], recv_y.at[s, h, 1])

    def sent_y(f, s, h):
        @pl.when(block > 0)
        def _():
            landed(f.at[2:6, 2:4], send_y.at[s, h, 1])

        @pl.when(block < G - 1)
        def _():
            landed(f.at[2:6, 32:34], send_y.at[s, h, 0])

    for h, quad in enumerate(QUADS):
        some = rb.at[h, :, 0:2 * (G - 1)]
        pltpu.make_async_copy(some, some, recv_in.at[h]).wait()
        pltpu.make_async_copy(sb.at[block, h], rb.at[h, :, pl.ds(2 * g, 2)], local_sem.at[h]).wait()

        def turn(zr, carry, h=h, quad=quad):
            turned = rb2[pl.ds(h * 4 * NT * 8 + zr, 128, stride=8), :].T
            for n, x in enumerate(quad):
                fa2[pl.ds(((x + 2) * YE + 2) * 8 + zr, YB, stride=8), :] = turned[n * YB:(n + 1) * YB]
            return carry

        lax.fori_loop(0, 8, turn, 0, unroll=8)
        if h == 0:
            x_halo(fa, 0, 0, YB)
        y_halo(fa, 0, h)
        if h == 0:
            lax.fori_loop(0, XE, stack_one, 0, unroll=2)

    def z_edges(f, x0, x1):
        def rows(ref, k):
            return ref.reshape(ref.shape[0] * ref.shape[1] * 8, 128)[pl.ds((x0 + 2) * YE * 8 + k, (x1 - x0) * YE, stride=8), :]

        def static(k, n):
            return rows(coef.at[k], n)

        next0 = pltpu.roll(rows(f, 0), 96, 1)
        next1 = pltpu.roll(rows(f, 1), 96, 1)
        last = rows(f, 7)
        jump = (next0 - last) * static(OZ, 7)
        slope = minmod((last - rows(f, 6)) * static(OZ, 6), jump)
        slope_next = minmod(jump, (next1 - next0) * pltpu.roll(static(OZ, 0), 96, 1))
        flux = face(last, next0, slope, slope_next, static(CZ, 7)) - mix[7:8, :] * jump
        for n, k, v in ((0, 7, next0), (0, 0, pltpu.roll(jump, 32, 1)), (1, 7, slope_next), (1, 0, pltpu.roll(flux, 32, 1))):
            edge.at[n].reshape(X * YE * 8, 128)[pl.ds(x0 * YE * 8 + k, (x1 - x0) * YE, stride=8), :] = v

    def advect(f, h, then, ready):
        parts = [advect_part(f, x0, x1) for x0, x1 in RANGES[h]]

        def column(y, carry):
            return tuple(step(y, c) for (_, step), c in zip(parts, carry))

        carry = tuple(start for start, _ in parts)
        for y0, y1 in ((0, YB // 2), (YB // 2, YB)):
            ready(y0, y1)
            carry = lax.fori_loop(y0, y1, column, carry, unroll=4)
            then(y0, y1)

    def advect_part(f, x0, x1):
        z_edges(f, x0, x1)
        n = x1 - x0

        def cells(e):
            return f[x0 + 2:x1 + 2, e]

        def along(k, e):
            return coef[k, x0 + 2:x1 + 2, e]

        def open_y(e):
            return along(SEA, e) * along(SEA, e + 1)

        f1, f2 = cells(1), cells(2)
        j0 = (f1 - cells(0)) * open_y(0)
        j1 = (f2 - f1) * open_y(1)
        j2 = (cells(3) - f2) * open_y(2)
        s1, s2 = minmod(j0, j1), minmod(j1, j2)
        start = (j2, s2, face(f1, f2, s1, s2, along(CY, 1)))

        def column(y, carry):
            jump, slope, before = carry
            e = y + 2
            fx = f[x0:x1 + 4, e]
            inner, following = fx[2:n + 2], cells(e + 1)
            jump_next = (cells(e + 2) - following) * open_y(e + 1)
            slope_next = minmod(jump, jump_next)
            after = face(inner, following, slope, slope_next, along(CY, e))
            total = inner - (after - before)
            sea_x = coef[SEA, x0:x1 + 4, e]
            jx = (fx[1:] - fx[:-1]) * (sea_x[1:] * sea_x[:-1])
            sx = minmod(jx[:-1], jx[1:])
            flux = face(fx[1:n + 2], fx[2:n + 3], sx[:-1], sx[1:], coef[CX, x0 + 1:x1 + 2, e])
            total = total - (flux[1:] - flux[:-1])
            edge0, edge1 = edge[0, x0:x1, e], edge[1, x0:x1, e]
            below = jnp.where(row == 7, edge0, pltpu.roll(inner, 7, 1))
            jz = (below - inner) * along(OZ, e)
            sz = minmod(jnp.where(row == 0, edge0, pltpu.roll(jz, 1, 1)), jz)
            sz_next = jnp.where(row == 7, edge1, pltpu.roll(sz, 7, 1))
            down = face(inner, below, sz, sz_next, along(CZ, e)) - mix[...] * jz
            adv[x0:x1, y] = total - (down - jnp.where(row == 0, edge1, pltpu.roll(down, 1, 1)))
            return jump_next, slope_next, after

        return start, column

    def react(h, results, y0, y1):
        length = y1 - y0
        count = 4 * length
        a = jnp.concatenate([adv[x0:x1, y0:y1].reshape((x1 - x0) * length, 8, 128) for x0, x1 in RANGES[h]], axis=0)
        att = 0.05 + 0.1 * a * a
        inc = att
        for step in (1, 2, 4):
            inc = inc + jnp.where(row >= step, pltpu.roll(inc, step, 1), 0.0)

        def spread_over(value, matrix):
            parts = jnp.concatenate(halves(value.reshape(count * 8, 128)), axis=1)
            return jnp.dot(parts, matrix[...], preferred_element_type=jnp.float32)

        both = spread_over(jnp.tanh(a), wmat)
        ahead = spread_over(inc - att, own_mat).reshape(count, 8, 128)
        past = spread_over(inc, past_mat).reshape(count, 8, 128)
        light = jnp.exp(-(ahead + past[:, 7:8, :]))
        response = (both[:, :128] + both[:, 128:]).reshape(count, 8, 128)
        change = (0.5 + light) * response
        for n, (x, result) in enumerate(zip(QUADS[h], results)):
            part = slice(n * length, (n + 1) * length)
            result[...] = a[part] + coef[SEA, x + 2, y0 + 2:y1 + 2] * change[part]

    fc2 = fc.reshape(X * YB * 8, 128)

    def give_back(h, quad):
        def turn_back(zr, carry):
            stack = [fc2[pl.ds(x * YB * 8 + zr, YB, stride=8), :] for x in quad]
            so2[pl.ds(h * 4 * NT * 8 + zr, 128, stride=8), :] = jnp.concatenate(stack, axis=0).T
            return carry

        lax.fori_loop(0, 8, turn_back, 0, unroll=8)

        def send_back(d, carry):
            to = lax.rem(g + d, G)
            pltpu.make_async_remote_copy(
                src_ref=so.at[h, :, pl.ds(2 * to, 2)], dst_ref=ro.at[h, block],
                send_sem=send_out.at[h], recv_sem=recv_out.at[h],
                device_id=(r, to), device_id_type=MESH).start()
            return carry

        lax.fori_loop(1, G, send_back, 0)
        pltpu.make_async_copy(so.at[h, :, pl.ds(2 * g, 2)], ro.at[h, block], local_sem.at[2 + h]).start()

    lax.fori_loop(0, XE // 4, spread_some, 0)

    for h in (1, 0):
        if h == 0:
            arrive_x(fa, 0, 0, YB)
        arrive_y(fa, 0, h)

        def step_1(y0, y1, h=h):
            if h == 1:
                if y1 == YB:
                    react(h, [fb.at[x + 2, 2:34] for x in QUADS[h]], 0, YB)
            else:
                react(h, [fb.at[x + 2, y0 + 2:y1 + 2] for x in QUADS[h]], y0, y1)
                x_halo(fb, 1, y0, y1)

        advect(fa, h, step_1, lambda y0, y1: None)
        y_halo(fb, 1, h)
    for h in (1, 0):
        arrive_y(fb, 1, h)
        advect(fb, h, lambda y0, y1: None, lambda y0, y1, h=h: arrive_x(fb, 1, y0, y1) if h == 0 else None)
        react(h, [fc.at[x] for x in QUADS[h]], 0, YB)
        give_back(h, QUADS[h])

    static_halo(lambda copy: copy.wait_send())
    edges_over(lambda copy: copy.wait_send())

    @pl.when(upper > 0)
    def _():
        landed(vel_pack, send_static.at[3])

    for s, f in ((0, fa), (1, fb)):
        sent_x(f, s)
        for h in range(2):
            sent_y(f, s, h)

    for h in (1, 0):
        some = ro.at[h, 0:G - 1]
        pltpu.make_async_copy(some, some, recv_out.at[h]).wait()
        pltpu.make_async_copy(so.at[h, :, pl.ds(2 * g, 2)], ro.at[h, block], local_sem.at[2 + h]).wait()

        def restore(n, carry, h=h, quad=QUADS[h]):
            t, zq = n // 4, n % 4
            for j in range(4):
                v = block_swap([ro[h, 4 * j + i, zq, t] for i in range(4)], lane)
                for x, b in zip(quad, v):
                    tout[j, pl.ds((t * NZ + zq * 8) * X + x, 8, stride=8), :] = b
            return carry

        lax.fori_loop(0, 8, restore, 0, unroll=4)

    for j in range(4):
        put(j).start()
    for h in range(2):
        some = sb.at[0:G - 1, h]
        pltpu.make_async_copy(some, some, send_in.at[h]).wait()
        some = ro.at[h, 0:G - 1]
        pltpu.make_async_copy(some, some, send_out.at[h]).wait()
    for j in range(4):
        put(j).wait()


def shards(tracers, velocity, sea_mask, coupling, mixing):
    anywhere = pl.BlockSpec(memory_space=pl.ANY)
    vmem = pl.BlockSpec(memory_space=pltpu.VMEM)
    f32 = jnp.float32
    dma = pltpu.SemaphoreType.DMA
    out = pl.pallas_call(
        kernel,
        out_shape=jax.ShapeDtypeStruct((2 * NZ * X, G * YB), f32),
        in_specs=[anywhere] * 3 + [anywhere, anywhere],
        out_specs=anywhere,
        scratch_shapes=[
            pltpu.VMEM((NT, NT), f32),
            pltpu.SMEM((NZ,), f32),
            pltpu.VMEM((256, NC * 128), jnp.bfloat16),
            pltpu.VMEM((XE * 40, 256), f32),
            pltpu.VMEM((256, 128), jnp.bfloat16),
            pltpu.VMEM((256, 128), jnp.bfloat16),
            pltpu.VMEM((8, 128), f32),
            pltpu.VMEM((256, 256), jnp.bfloat16),
            pltpu.VMEM((3, NZ, X, YB), f32),
            pltpu.VMEM((24, X, 128), f32),
            pltpu.VMEM((24, X, 128), f32),
            pltpu.VMEM((3, NZ, X, 128), jnp.int32),
            pltpu.VMEM((4, NZ, 16, 128), f32),
            pltpu.VMEM((8, NZ, 16, 128), f32),
            pltpu.VMEM((2, NZ, 128), f32),
            pltpu.VMEM((2, NZ, 128), f32),
            pltpu.VMEM((8, 128), f32),
            pltpu.VMEM((8, 128), f32),
            pltpu.VMEM((8, 128), f32),
            pltpu.VMEM((2, NZ, 128), f32),
            pltpu.VMEM((2, NZ, 128), f32),
            pltpu.VMEM((8, 128), f32),
            pltpu.VMEM((4, 2 * NZ * X, 128), f32),
            pltpu.VMEM((4, 2 * NZ * X, 128), f32),
            pltpu.VMEM((G, 2, 4, 2, 8, 128), f32),
            pltpu.VMEM((2, 4, NT, 8, 128), f32),
            pltpu.VMEM((XE, YE, 8, 128), f32),
            pltpu.VMEM((XE, YE, 8, 128), f32),
            pltpu.VMEM((X, YB, 8, 128), f32),
            pltpu.VMEM((X, YB, 8, 128), f32),
            pltpu.VMEM((2, X, YE, 8, 128), f32),
            pltpu.VMEM((NC, XE, YE, 8, 128), f32),
            pltpu.VMEM((2, 4, NT, 8, 128), f32),
            pltpu.VMEM((2, G, 4, 2, 8, 128), f32),
            dma((6,)), dma((5,)), dma((5,)),
            dma((4,)), dma((4,)), dma((2,)), dma((2,)), dma((2, 2)), dma((3, 2)), dma((2, 2, 2)), dma((2, 2, 2)), dma((2,)), dma((2,)), dma((4,)),
        ],
        compiler_params=pltpu.CompilerParams(
            collective_id=0, has_side_effects=True, vmem_limit_bytes=60 * 2**20),
    )(tracers.reshape(2 * NZ * X, G * YB), velocity, sea_mask, coupling, mixing)
    return out.reshape(tracers.shape)


def solution(mesh):
    placed = (
        P("group", None, "region", None),
        P(None, None, "region", "group"),
        P(None, "region", None),
        P(),
        P(),
    )
    return jax.shard_map(
        shards,
        mesh=mesh,
        in_specs=placed,
        out_specs=P("group", None, "region", None),
        check_vma=False,
    )
```

```python
import jax
import jax.numpy as jnp
from jax import lax
from jax.experimental import pallas as pl
from jax.experimental.pallas import tpu as pltpu
from jax.sharding import PartitionSpec as P

MESH = pl.DeviceIdType.MESH
STEPS = 2
NZ, NT, X, YB, G, R = 32, 32, 8, 32, 16, 8
XE, YE = X + 4, YB + 4
QUADS = ((0, 1, 6, 7), (2, 3, 4, 5))
RANGES = (((0, 2), (6, 8)), ((2, 6),))
NC = 5
CX, CY, CZ, SEA, OZ = range(NC)


def minmod(a, b):
    return jnp.maximum(jnp.minimum(a, b), jnp.minimum(jnp.maximum(a, b), 0.0))


def face(cell, following, slope, slope_following, c):
    forward = c > 0
    q = jnp.where(forward, 0.5, -0.5) - 0.5 * c
    return c * (jnp.where(forward, cell, following) + q * jnp.where(forward, slope, slope_following))


def halves(value):
    high = value.astype(jnp.bfloat16)
    return high, (value - high.astype(jnp.float32)).astype(jnp.bfloat16)


def block_swap(v, lane):
    low, even = lane < 64, (lane // 32) % 2 == 0
    axis = v[0].ndim - 1
    a = [None] * 4
    for n in (0, 1):
        a[n] = jnp.where(low, v[n], pltpu.roll(v[n + 2], 64, axis))
        a[n + 2] = jnp.where(low, pltpu.roll(v[n], 64, axis), v[n + 2])
    b = [None] * 4
    for n in (0, 2):
        b[n] = jnp.where(even, a[n], pltpu.roll(a[n + 1], 32, axis))
        b[n + 1] = jnp.where(even, pltpu.roll(a[n], 96, axis), a[n + 1])
    return b


def kernel(tr, velocity, mask, coupling_in, mixing_in, out,
           coupling, mixing, spread, stacked, own_mat, past_mat, mix, wmat, vel, vel_pack, vel_got, sea3, q, dc, pack_up, pack_down, pack_x, pack_y, got_x, got_low, got_high, got_y,
           tin, tout, sb, rb, fa, fb, fc, adv, edge, coef, so, ro,
           statics_in, send_static, recv_static,
           tiles_in, tiles_out, send_in, recv_in, send_halo, recv_x, send_y, recv_y, send_out, recv_out, local_sem):
    r, g = lax.axis_index("region"), lax.axis_index("group")
    upper = lax.div(r, R // 2)

    def flip(n, upper=upper):
        return n + upper * (2 - 4 * lax.rem(lax.div(n, 2), 2))

    block = flip(g)
    other = g + 2 - 4 * lax.rem(lax.div(g, 2), 2)
    g_next = jnp.where(r == R // 2 - 1, other, g)
    g_last = jnp.where(r == R // 2, other, g)
    lane = lax.broadcasted_iota(jnp.int32, (8, 128), 1)
    row = lax.broadcasted_iota(jnp.int32, (8, 128), 0)
    fa2, fb2 = fa.reshape(XE * YE * 8, 128), fb.reshape(XE * YE * 8, 128)
    rb2, so2 = rb.reshape(2 * 4 * NT * 8, 128), so.reshape(2 * 4 * NT * 8, 128)

    def fetch(j):
        return pltpu.make_async_copy(tr.at[:, pl.ds(j * 128, 128)], tin.at[j], tiles_in.at[j])

    def put(j):
        return pltpu.make_async_copy(tout.at[j], out.at[:, pl.ds(j * 128, 128)], tiles_out.at[j])

    at = lax.div(block, 4)
    spots = (at, jnp.maximum(at - 1, 0), jnp.minimum(at + 1, 3))
    fetches = [pltpu.make_async_copy(velocity, vel, statics_in.at[0]),
               pltpu.make_async_copy(coupling_in, coupling, statics_in.at[4]),
               pltpu.make_async_copy(mixing_in, mixing, statics_in.at[5])]
    for n, spot in enumerate(spots):
        fetches.append(pltpu.make_async_copy(
            mask.at[:, :, pl.ds(pl.multiple_of(spot * 128, 128), 128)], sea3.at[n], statics_in.at[n + 1]))
    for copy in fetches:
        copy.start()
    for j in range(4):
        fetch(j).start()

    for f in (fa, fb):
        f[0:2, 2:34] = jnp.zeros((2, 32, 8, 128), jnp.float32)
        f[10:12, 2:34] = jnp.zeros((2, 32, 8, 128), jnp.float32)
        f[2:10, 0:2] = jnp.zeros((8, 2, 8, 128), jnp.float32)
        f[2:10, 34:36] = jnp.zeros((8, 2, 8, 128), jnp.float32)

    barrier = pltpu.get_barrier_semaphore()

    def greet(d, carry):
        pl.semaphore_signal(barrier, inc=1, device_id=(r, lax.rem(g + d, G)), device_id_type=MESH)
        return carry

    lax.fori_loop(1, G, greet, 0)

    @pl.when(r > 0)
    def _():
        pl.semaphore_signal(barrier, inc=1, device_id=(r - 1, g_last), device_id_type=MESH)

    @pl.when(r > R // 2)
    def _():
        pl.semaphore_signal(barrier, inc=1, device_id=(r - 1, other), device_id_type=MESH)

    extra = jnp.where(jnp.logical_and(r >= R // 2, r < R - 1), 1, 0)

    @pl.when(r < R - 1)
    def _():
        pl.semaphore_signal(barrier, inc=1, device_id=(r + 1, g_next), device_id_type=MESH)

    for j in range(4):
        fetch(j).wait()

    def begin(copy):
        copy.start()

    def static_halo(do):
        @pl.when(r < R - 1)
        def _():
            do(pltpu.make_async_remote_copy(
                src_ref=pack_up, dst_ref=got_low, send_sem=send_static.at[0], recv_sem=recv_static.at[0],
                device_id=(r + 1, g_next), device_id_type=MESH))

        @pl.when(r > 0)
        def _():
            do(pltpu.make_async_remote_copy(
                src_ref=pack_down, dst_ref=got_high, send_sem=send_static.at[1], recv_sem=recv_static.at[1],
                device_id=(r - 1, g_last), device_id_type=MESH))

    def edges_over(do):
        @pl.when(r < R - 1)
        def _():
            to = flip(g, lax.div(r + 1, R // 2))
            do(pltpu.make_async_remote_copy(
                src_ref=pack_x, dst_ref=got_x, send_sem=send_static.at[4], recv_sem=recv_static.at[4],
                device_id=(r + 1, to), device_id_type=MESH))

        @pl.when(g < G - 1)
        def _():
            do(pltpu.make_async_remote_copy(
                src_ref=pack_y, dst_ref=got_y, send_sem=send_static.at[2], recv_sem=recv_static.at[2],
                device_id=(r, flip(g + 1)), device_id_type=MESH))

    def velocity_over(do, do_here):
        @pl.when(upper > 0)
        def _():
            do(pltpu.make_async_remote_copy(
                src_ref=vel_pack, dst_ref=vel_got, send_sem=send_static.at[3], recv_sem=recv_static.at[3],
                device_id=(r, block), device_id_type=MESH))

        @pl.when(upper == 0)
        def _():
            do_here(pltpu.make_async_copy(vel_pack, vel_got, recv_static.at[3]))

    fetches[0].wait()
    for k in range(3):
        for m in range(8):
            vel_pack[8 * k + m] = jnp.concatenate([vel[k, 4 * m + n] for n in range(4)], axis=1)
    pack_x[...] = vel_pack.reshape(24 * X, 128)[pl.ds(7, 8, stride=8), :]
    column = jnp.zeros((8, 128), jnp.float32)
    for m in range(8):
        column = jnp.where(lane % 32 == m, pltpu.roll(vel_pack[8 + m], m + 97, 1), column)
    pack_y[...] = column

    for h, quad in enumerate(QUADS):
        def regroup(n, carry, h=h, quad=quad):
            t, zq = n // 4, n % 4
            for j in range(4):
                v = [tin[j, pl.ds((t * NZ + zq * 8) * X + x, 8, stride=8), :] for x in quad]
                for i, b in enumerate(block_swap(v, lane)):
                    sb[4 * j + i, h, zq, t] = b
            return carry

        lax.fori_loop(0, 8, regroup, 0, unroll=4)
        if h == 0:
            pl.semaphore_wait(barrier, G - 1 + jnp.minimum(r, 1) + jnp.minimum(R - 1 - r, 1) + extra)
            velocity_over(begin, begin)
            edges_over(begin)

        def send(d, carry, h=h):
            to = lax.rem(g + d, G)
            pltpu.make_async_remote_copy(
                src_ref=sb.at[flip(to), h], dst_ref=rb.at[h, :, pl.ds(2 * g, 2)],
                send_sem=send_in.at[h], recv_sem=recv_in.at[h],
                device_id=(r, to), device_id_type=MESH).start()
            return carry

        lax.fori_loop(1, G, send, 0)
        pltpu.make_async_copy(sb.at[block, h], rb.at[h, :, pl.ds(2 * g, 2)], local_sem.at[h]).start()

    q[...] = jnp.zeros(q.shape, jnp.float32)
    for copy in fetches[1:]:
        copy.wait()
    velocity_over(lambda copy: copy.wait_recv(), lambda copy: copy.wait())
    for n in range(4):
        shifted = pltpu.roll(vel_got[...], (130 - 32 * n) % 128, 2)
        shifted = jnp.where(jnp.logical_and(lane >= 2, lane < 34), shifted, 0.0)
        for k in range(3):
            for m in range(8):
                q[k, 4 * m + n, 2:10, :] = shifted[8 * k + m]
    place = lax.rem(block, 4)
    has_left = jnp.minimum(at, 1).astype(jnp.float32)
    has_right = jnp.minimum(3 - at, 1).astype(jnp.float32)
    centre = sea3[0].astype(jnp.float32)
    left = sea3[1].astype(jnp.float32) * has_left
    right = sea3[2].astype(jnp.float32) * has_right
    centre = jnp.where(jnp.logical_and(lane >= 126, place == 0), left, centre)
    centre = jnp.where(jnp.logical_and(lane < 2, place == 3), right, centre)
    q[3, :, 2:10, :] = pltpu.roll(centre, lax.rem(130 - 32 * place, 128), 2)

    def level_rows(k, e):
        return q.at[k].reshape(NZ * 16, 128)[pl.ds(e, NZ, stride=16), :]

    def put_rows(k, e, value):
        q.at[k].reshape(NZ * 16, 128)[pl.ds(e, NZ, stride=16), :] = value

    pack_up[0], pack_up[1] = level_rows(3, 8), level_rows(3, 9)
    pack_down[0], pack_down[1] = level_rows(3, 2), level_rows(3, 3)

    static_halo(begin)

    def iota(shape, axis):
        return lax.broadcasted_iota(jnp.int32, shape, axis)

    square = (128, 128)
    block_in, block_out = iota(square, 0) // 32, iota(square, 1) // 32
    tall = (256, 128)
    part_at, block_at = iota(tall, 0) % 32, iota(tall, 1) // 32
    for k in range(NC):
        place_k = part_at - (block_at + (24 + 4 * (k - 3) if k >= 3 else 4 * k))
        hit = place_k == 0 if k >= 3 else jnp.logical_or(place_k == 0, place_k == 12)
        spread[:, k * 128:(k + 1) * 128] = jnp.where(hit, 1.0, 0.0).astype(jnp.bfloat16)
    first = iota(square, 0) % 32 == 0
    own = jnp.where(jnp.logical_and(first, block_in == block_out), 1.0, 0.0).astype(jnp.bfloat16)
    past = jnp.where(jnp.logical_and(first, block_in < block_out), 1.0, 0.0).astype(jnp.bfloat16)
    own_mat[...] = jnp.concatenate([own, own], 0)
    past_mat[...] = jnp.concatenate([past, past], 0)
    across = jnp.concatenate([coupling[...].T] * 4, 1)
    weights = jnp.where(block_in == block_out, jnp.concatenate([across] * 4, 0), 0.0)
    high, low = halves(weights)
    wmat[...] = jnp.concatenate([jnp.concatenate([high, low], 1), jnp.concatenate([high, jnp.zeros_like(low)], 1)], 0)
    tile = jnp.zeros((8, 128), jnp.float32)
    for z in range(NZ):
        tile = jnp.where(jnp.logical_and(row == z % 8, lane // 32 == z // 8), mixing[z], tile)
    mix[...] = tile

    @pl.when(r > 0)
    def _():
        pltpu.make_async_copy(got_low, got_low, recv_static.at[0]).wait()
        put_rows(3, 0, got_low[0])
        put_rows(3, 1, got_low[1])
        pltpu.make_async_copy(got_x, got_x, recv_static.at[4]).wait()
        for n in range(4):
            q.at[0].reshape(NZ * 16, 128)[pl.ds(n * 16 + 1, 8, stride=64), :] = jnp.where(
                jnp.logical_and(lane >= 2, lane < 34), pltpu.roll(got_x[...], (130 - 32 * n) % 128, 1), 0.0)

    @pl.when(r < R - 1)
    def _():
        pltpu.make_async_copy(got_high, got_high, recv_static.at[1]).wait()
        put_rows(3, 10, got_high[0])
        put_rows(3, 11, got_high[1])

    @pl.when(block > 0)
    def _():
        pltpu.make_async_copy(got_y, got_y, recv_static.at[2]).wait()

        def unpack_level(z, carry):
            q[1, z, 2:10, :] = jnp.where(
                lane == 1, pltpu.roll(got_y[...], lax.rem(129 - lax.div(z, 4) - 32 * lax.rem(z, 4) + 128, 128), 1), q[1, z, 2:10, :])
            return carry

        lax.fori_loop(0, NZ, unpack_level, 0, unroll=8)

    sea = q[3]
    follow = (pltpu.roll(sea, 15, 1), pltpu.roll(sea, 127, 2),
              jnp.concatenate([sea[1:], jnp.zeros((1, 16, 128), jnp.float32)], 0))
    for k in range(3):
        opened = sea * follow[k]
        c = q[k] * opened
        high = c.astype(jnp.bfloat16).astype(jnp.float32)
        dc[k] = high
        dc[3 + k] = c - high
    dc[6] = sea
    dc[7] = opened

    def stack_one(e, carry):
        for half in range(2):
            rows = [dc.reshape(8 * NZ * 16, 128)[pl.ds((half * 4 + n) * 16 + e, 32, stride=128), :] for n in range(4)]
            stacked[pl.ds(pl.multiple_of(e * 40, 8), 40), half * 128:(half + 1) * 128] = (
                jnp.concatenate(rows, axis=0).T[:40])
        return carry

    own_lanes = iota((8, 256), 0) == iota((8, 256), 1) // 32

    def spread_some(n, carry):
        value = stacked[pl.ds(pl.multiple_of(n * 160, 8), 160), :]
        value = jnp.where(own_lanes, jnp.broadcast_to(value[:, None, :], (160, 8, 256)), 0.0)
        wide = jnp.dot(value.reshape(1280, 256).astype(jnp.bfloat16), spread[...], preferred_element_type=jnp.float32)
        for m in range(4):
            for k in range(NC):
                coef[k, 4 * n + m] = wide[m * 320:m * 320 + YE * 8, k * 128:(k + 1) * 128].reshape(YE, 8, 128)
        return carry

    def x_halo(f, s, y0, y1):
        slot = s + y0 // (YB // 2)

        @pl.when(r > 0)
        def _():
            pltpu.make_async_remote_copy(
                src_ref=f.at[2:4, y0 + 2:y1 + 2], dst_ref=f.at[10:12, y0 + 2:y1 + 2],
                send_sem=send_halo.at[s, 0], recv_sem=recv_x.at[slot, 1],
                device_id=(r - 1, g_last), device_id_type=MESH).start()

        @pl.when(r < R - 1)
        def _():
            pltpu.make_async_remote_copy(
                src_ref=f.at[8:10, y0 + 2:y1 + 2], dst_ref=f.at[0:2, y0 + 2:y1 + 2],
                send_sem=send_halo.at[s, 1], recv_sem=recv_x.at[slot, 0],
                device_id=(r + 1, g_next), device_id_type=MESH).start()

    def y_halo(f, s, h):
        @pl.when(block > 0)
        def _():
            for x0, x1 in RANGES[h]:
                pltpu.make_async_remote_copy(
                    src_ref=f.at[x0 + 2:x1 + 2, 2:4], dst_ref=f.at[x0 + 2:x1 + 2, 34:36],
                    send_sem=send_y.at[s, h, 1], recv_sem=recv_y.at[s, h, 1],
                    device_id=(r, flip(block - 1)), device_id_type=MESH).start()

        @pl.when(block < G - 1)
        def _():
            for x0, x1 in RANGES[h]:
                pltpu.make_async_remote_copy(
                    src_ref=f.at[x0 + 2:x1 + 2, 32:34], dst_ref=f.at[x0 + 2:x1 + 2, 0:2],
                    send_sem=send_y.at[s, h, 0], recv_sem=recv_y.at[s, h, 0],
                    device_id=(r, flip(block + 1)), device_id_type=MESH).start()

    def landed(ref, sem):
        pltpu.make_async_copy(ref, ref, sem).wait()

    def sent_x(f, s):
        @pl.when(r > 0)
        def _():
            landed(f.at[2:4, 2:34], send_halo.at[s, 0])

        @pl.when(r < R - 1)
        def _():
            landed(f.at[8:10, 2:34], send_halo.at[s, 1])

    def arrive_x(f, s, y0, y1):
        slot = s + y0 // (YB // 2)

        @pl.when(r > 0)
        def _():
            landed(f.at[0:2, y0 + 2:y1 + 2], recv_x.at[slot, 0])

        @pl.when(r < R - 1)
        def _():
            landed(f.at[10:12, y0 + 2:y1 + 2], recv_x.at[slot, 1])

    def arrive_y(f, s, h):
        @pl.when(block > 0)
        def _():
            landed(f.at[2:6, 0:2], recv_y.at[s, h, 0])

        @pl.when(block < G - 1)
        def _():
            landed(f.at[2:6, 34:36], recv_y.at[s, h, 1])

    def sent_y(f, s, h):
        @pl.when(block > 0)
        def _():
            landed(f.at[2:6, 2:4], send_y.at[s, h, 1])

        @pl.when(block < G - 1)
        def _():
            landed(f.at[2:6, 32:34], send_y.at[s, h, 0])

    for h, quad in enumerate(QUADS):
        some = rb.at[h, :, 0:2 * (G - 1)]
        pltpu.make_async_copy(some, some, recv_in.at[h]).wait()
        pltpu.make_async_copy(sb.at[block, h], rb.at[h, :, pl.ds(2 * g, 2)], local_sem.at[h]).wait()

        def turn(zr, carry, h=h, quad=quad):
            turned = rb2[pl.ds(h * 4 * NT * 8 + zr, 128, stride=8), :].T
            for n, x in enumerate(quad):
                fa2[pl.ds(((x + 2) * YE + 2) * 8 + zr, YB, stride=8), :] = turned[n * YB:(n + 1) * YB]
            return carry

        lax.fori_loop(0, 8, turn, 0, unroll=8)
        if h == 0:
            x_halo(fa, 0, 0, YB)
        y_halo(fa, 0, h)
        if h == 0:
            lax.fori_loop(0, XE, stack_one, 0, unroll=2)

    def z_edges(f, x0, x1):
        def rows(ref, k):
            return ref.reshape(ref.shape[0] * ref.shape[1] * 8, 128)[pl.ds((x0 + 2) * YE * 8 + k, (x1 - x0) * YE, stride=8), :]

        def static(k, n):
            return rows(coef.at[k], n)

        next0 = pltpu.roll(rows(f, 0), 96, 1)
        next1 = pltpu.roll(rows(f, 1), 96, 1)
        last = rows(f, 7)
        jump = (next0 - last) * static(OZ, 7)
        slope = minmod((last - rows(f, 6)) * static(OZ, 6), jump)
        slope_next = minmod(jump, (next1 - next0) * pltpu.roll(static(OZ, 0), 96, 1))
        flux = face(last, next0, slope, slope_next, static(CZ, 7)) - mix[7:8, :] * jump
        for n, k, v in ((0, 7, next0), (0, 0, pltpu.roll(jump, 32, 1)), (1, 7, slope_next), (1, 0, pltpu.roll(flux, 32, 1))):
            edge.at[n].reshape(X * YE * 8, 128)[pl.ds(x0 * YE * 8 + k, (x1 - x0) * YE, stride=8), :] = v

    def advect(f, h, then, ready):
        parts = [advect_part(f, x0, x1) for x0, x1 in RANGES[h]]

        def column(y, carry):
            return tuple(step(y, c) for (_, step), c in zip(parts, carry))

        carry = tuple(start for start, _ in parts)
        for y0, y1 in ((0, YB // 2), (YB // 2, YB)):
            ready(y0, y1)
            carry = lax.fori_loop(y0, y1, column, carry, unroll=4)
            then(y0, y1)

    def advect_part(f, x0, x1):
        z_edges(f, x0, x1)
        n = x1 - x0

        def cells(e):
            return f[x0 + 2:x1 + 2, e]

        def along(k, e):
            return coef[k, x0 + 2:x1 + 2, e]

        def open_y(e):
            return along(SEA, e) * along(SEA, e + 1)

        f1, f2 = cells(1), cells(2)
        j0 = (f1 - cells(0)) * open_y(0)
        j1 = (f2 - f1) * open_y(1)
        j2 = (cells(3) - f2) * open_y(2)
        s1, s2 = minmod(j0, j1), minmod(j1, j2)
        start = (j2, s2, face(f1, f2, s1, s2, along(CY, 1)))

        def column(y, carry):
            jump, slope, before = carry
            e = y + 2
            fx = f[x0:x1 + 4, e]
            inner, following = fx[2:n + 2], cells(e + 1)
            jump_next = (cells(e + 2) - following) * open_y(e + 1)
            slope_next = minmod(jump, jump_next)
            after = face(inner, following, slope, slope_next, along(CY, e))
            total = inner - (after - before)
            sea_x = coef[SEA, x0:x1 + 4, e]
            jx = (fx[1:] - fx[:-1]) * (sea_x[1:] * sea_x[:-1])
            sx = minmod(jx[:-1], jx[1:])
            flux = face(fx[1:n + 2], fx[2:n + 3], sx[:-1], sx[1:], coef[CX, x0 + 1:x1 + 2, e])
            total = total - (flux[1:] - flux[:-1])
            edge0, edge1 = edge[0, x0:x1, e], edge[1, x0:x1, e]
            below = jnp.where(row == 7, edge0, pltpu.roll(inner, 7, 1))
            jz = (below - inner) * along(OZ, e)
            sz = minmod(jnp.where(row == 0, edge0, pltpu.roll(jz, 1, 1)), jz)
            sz_next = jnp.where(row == 7, edge1, pltpu.roll(sz, 7, 1))
            down = face(inner, below, sz, sz_next, along(CZ, e)) - mix[...] * jz
            adv[x0:x1, y] = total - (down - jnp.where(row == 0, edge1, pltpu.roll(down, 1, 1)))
            return jump_next, slope_next, after

        return start, column

    def react(h, results, y0, y1):
        length = y1 - y0
        count = 4 * length
        a = jnp.concatenate([adv[x0:x1, y0:y1].reshape((x1 - x0) * length, 8, 128) for x0, x1 in RANGES[h]], axis=0)
        att = 0.05 + 0.1 * a * a
        inc = att
        for step in (1, 2, 4):
            inc = inc + jnp.where(row >= step, pltpu.roll(inc, step, 1), 0.0)

        def spread_over(value, matrix):
            parts = jnp.concatenate(halves(value.reshape(count * 8, 128)), axis=1)
            return jnp.dot(parts, matrix[...], preferred_element_type=jnp.float32)

        both = spread_over(jnp.tanh(a), wmat)
        ahead = spread_over(inc - att, own_mat).reshape(count, 8, 128)
        past = spread_over(inc, past_mat).reshape(count, 8, 128)
        light = jnp.exp(-(ahead + past[:, 7:8, :]))
        response = (both[:, :128] + both[:, 128:]).reshape(count, 8, 128)
        change = (0.5 + light) * response
        for n, (x, result) in enumerate(zip(QUADS[h], results)):
            part = slice(n * length, (n + 1) * length)
            result[...] = a[part] + coef[SEA, x + 2, y0 + 2:y1 + 2] * change[part]

    fc2 = fc.reshape(X * YB * 8, 128)

    def give_back(h, quad):
        def turn_back(zr, carry):
            stack = [fc2[pl.ds(x * YB * 8 + zr, YB, stride=8), :] for x in quad]
            so2[pl.ds(h * 4 * NT * 8 + zr, 128, stride=8), :] = jnp.concatenate(stack, axis=0).T
            return carry

        lax.fori_loop(0, 8, turn_back, 0, unroll=8)

        def send_back(d, carry):
            to = lax.rem(g + d, G)
            pltpu.make_async_remote_copy(
                src_ref=so.at[h, :, pl.ds(2 * to, 2)], dst_ref=ro.at[h, block],
                send_sem=send_out.at[h], recv_sem=recv_out.at[h],
                device_id=(r, to), device_id_type=MESH).start()
            return carry

        lax.fori_loop(1, G, send_back, 0)
        pltpu.make_async_copy(so.at[h, :, pl.ds(2 * g, 2)], ro.at[h, block], local_sem.at[2 + h]).start()

    lax.fori_loop(0, XE // 4, spread_some, 0)

    for h in (1, 0):
        arrive_y(fa, 0, h)

        def step_1(y0, y1, h=h):
            if h == 1:
                if y1 == YB:
                    react(h, [fb.at[x + 2, 2:34] for x in QUADS[h]], 0, YB)
            else:
                react(h, [fb.at[x + 2, y0 + 2:y1 + 2] for x in QUADS[h]], y0, y1)
                x_halo(fb, 1, y0, y1)

        advect(fa, h, step_1, lambda y0, y1, h=h: arrive_x(fa, 0, 0, YB) if h == 0 and y0 == 0 else None)
        y_halo(fb, 1, h)
    for h in (1, 0):
        arrive_y(fb, 1, h)
        advect(fb, h, lambda y0, y1: None, lambda y0, y1, h=h: arrive_x(fb, 1, y0, y1) if h == 0 else None)
        react(h, [fc.at[x] for x in QUADS[h]], 0, YB)
        give_back(h, QUADS[h])

    static_halo(lambda copy: copy.wait_send())
    edges_over(lambda copy: copy.wait_send())

    @pl.when(upper > 0)
    def _():
        landed(vel_pack, send_static.at[3])

    for s, f in ((0, fa), (1, fb)):
        sent_x(f, s)
        for h in range(2):
            sent_y(f, s, h)

    for h in (1, 0):
        some = ro.at[h, 0:G - 1]
        pltpu.make_async_copy(some, some, recv_out.at[h]).wait()
        pltpu.make_async_copy(so.at[h, :, pl.ds(2 * g, 2)], ro.at[h, block], local_sem.at[2 + h]).wait()

        def restore(n, carry, h=h, quad=QUADS[h]):
            t, zq = n // 4, n % 4
            for j in range(4):
                v = block_swap([ro[h, 4 * j + i, zq, t] for i in range(4)], lane)
                for x, b in zip(quad, v):
                    tout[j, pl.ds((t * NZ + zq * 8) * X + x, 8, stride=8), :] = b
            return carry

        lax.fori_loop(0, 8, restore, 0, unroll=4)

    for j in range(4):
        put(j).start()
    for h in range(2):
        some = sb.at[0:G - 1, h]
        pltpu.make_async_copy(some, some, send_in.at[h]).wait()
        some = ro.at[h, 0:G - 1]
        pltpu.make_async_copy(some, some, send_out.at[h]).wait()
    for j in range(4):
        put(j).wait()


def shards(tracers, velocity, sea_mask, coupling, mixing):
    anywhere = pl.BlockSpec(memory_space=pl.ANY)
    vmem = pl.BlockSpec(memory_space=pltpu.VMEM)
    f32 = jnp.float32
    dma = pltpu.SemaphoreType.DMA
    out = pl.pallas_call(
        kernel,
        out_shape=jax.ShapeDtypeStruct((2 * NZ * X, G * YB), f32),
        in_specs=[anywhere] * 3 + [anywhere, anywhere],
        out_specs=anywhere,
        scratch_shapes=[
            pltpu.VMEM((NT, NT), f32),
            pltpu.SMEM((NZ,), f32),
            pltpu.VMEM((256, NC * 128), jnp.bfloat16),
            pltpu.VMEM((XE * 40, 256), f32),
            pltpu.VMEM((256, 128), jnp.bfloat16),
            pltpu.VMEM((256, 128), jnp.bfloat16),
            pltpu.VMEM((8, 128), f32),
            pltpu.VMEM((256, 256), jnp.bfloat16),
            pltpu.VMEM((3, NZ, X, YB), f32),
            pltpu.VMEM((24, X, 128), f32),
            pltpu.VMEM((24, X, 128), f32),
            pltpu.VMEM((3, NZ, X, 128), jnp.int32),
            pltpu.VMEM((4, NZ, 16, 128), f32),
            pltpu.VMEM((8, NZ, 16, 128), f32),
            pltpu.VMEM((2, NZ, 128), f32),
            pltpu.VMEM((2, NZ, 128), f32),
            pltpu.VMEM((8, 128), f32),
            pltpu.VMEM((8, 128), f32),
            pltpu.VMEM((8, 128), f32),
            pltpu.VMEM((2, NZ, 128), f32),
            pltpu.VMEM((2, NZ, 128), f32),
            pltpu.VMEM((8, 128), f32),
            pltpu.VMEM((4, 2 * NZ * X, 128), f32),
            pltpu.VMEM((4, 2 * NZ * X, 128), f32),
            pltpu.VMEM((G, 2, 4, 2, 8, 128), f32),
            pltpu.VMEM((2, 4, NT, 8, 128), f32),
            pltpu.VMEM((XE, YE, 8, 128), f32),
            pltpu.VMEM((XE, YE, 8, 128), f32),
            pltpu.VMEM((X, YB, 8, 128), f32),
            pltpu.VMEM((X, YB, 8, 128), f32),
            pltpu.VMEM((2, X, YE, 8, 128), f32),
            pltpu.VMEM((NC, XE, YE, 8, 128), f32),
            pltpu.VMEM((2, 4, NT, 8, 128), f32),
            pltpu.VMEM((2, G, 4, 2, 8, 128), f32),
            dma((6,)), dma((5,)), dma((5,)),
            dma((4,)), dma((4,)), dma((2,)), dma((2,)), dma((2, 2)), dma((3, 2)), dma((2, 2, 2)), dma((2, 2, 2)), dma((2,)), dma((2,)), dma((4,)),
        ],
        compiler_params=pltpu.CompilerParams(
            collective_id=0, has_side_effects=True, vmem_limit_bytes=60 * 2**20),
    )(tracers.reshape(2 * NZ * X, G * YB), velocity, sea_mask, coupling, mixing)
    return out.reshape(tracers.shape)


def solution(mesh):
    placed = (
        P("group", None, "region", None),
        P(None, None, "region", "group"),
        P(None, "region", None),
        P(),
        P(),
    )
    return jax.shard_map(
        shards,
        mesh=mesh,
        in_specs=placed,
        out_specs=P("group", None, "region", None),
        check_vma=False,
    )
```

```python
import jax
import jax.numpy as jnp
from jax import lax
from jax.experimental import pallas as pl
from jax.experimental.pallas import tpu as pltpu
from jax.sharding import PartitionSpec as P

MESH = pl.DeviceIdType.MESH
STEPS = 2
NZ, NT, X, YB, G, R = 32, 32, 8, 32, 16, 8
XE, YE = X + 4, YB + 4
QUADS = ((0, 1, 6, 7), (2, 3, 4, 5))
RANGES = (((0, 2), (6, 8)), ((2, 6),))
NC = 5
CX, CY, CZ, SEA, OZ = range(NC)


def minmod(a, b):
    return jnp.maximum(jnp.minimum(a, b), jnp.minimum(jnp.maximum(a, b), 0.0))


def face(cell, following, slope, slope_following, c):
    forward = c > 0
    q = jnp.where(forward, 0.5, -0.5) - 0.5 * c
    return c * (jnp.where(forward, cell, following) + q * jnp.where(forward, slope, slope_following))


def halves(value):
    high = value.astype(jnp.bfloat16)
    return high, (value - high.astype(jnp.float32)).astype(jnp.bfloat16)


def block_swap(v, lane):
    low, even = lane < 64, (lane // 32) % 2 == 0
    axis = v[0].ndim - 1
    a = [None] * 4
    for n in (0, 1):
        a[n] = jnp.where(low, v[n], pltpu.roll(v[n + 2], 64, axis))
        a[n + 2] = jnp.where(low, pltpu.roll(v[n], 64, axis), v[n + 2])
    b = [None] * 4
    for n in (0, 2):
        b[n] = jnp.where(even, a[n], pltpu.roll(a[n + 1], 32, axis))
        b[n + 1] = jnp.where(even, pltpu.roll(a[n], 96, axis), a[n + 1])
    return b


def kernel(tr, velocity, mask, coupling_in, mixing_in, out,
           coupling, mixing, spread, stacked, own_mat, past_mat, mix, wmat, vel, vel_pack, vel_got, sea3, q, dc, pack_up, pack_down, pack_x, pack_y, got_x, got_low, got_high, got_y,
           tin, tout, sb, rb, fa, fb, fc, adv, edge, coef, so, ro,
           statics_in, send_static, recv_static,
           tiles_in, tiles_out, send_in, recv_in, send_halo, recv_x, send_y, recv_y, send_out, recv_out, local_sem):
    r, g = lax.axis_index("region"), lax.axis_index("group")
    upper = lax.div(r, R // 2)

    def flip(n, upper=upper):
        return n + upper * (2 - 4 * lax.rem(lax.div(n, 2), 2))

    block = flip(g)
    other = g + 2 - 4 * lax.rem(lax.div(g, 2), 2)
    g_next = jnp.where(r == R // 2 - 1, other, g)
    g_last = jnp.where(r == R // 2, other, g)
    lane = lax.broadcasted_iota(jnp.int32, (8, 128), 1)
    row = lax.broadcasted_iota(jnp.int32, (8, 128), 0)
    fa2, fb2 = fa.reshape(XE * YE * 8, 128), fb.reshape(XE * YE * 8, 128)
    rb2, so2 = rb.reshape(2 * 4 * NT * 8, 128), so.reshape(2 * 4 * NT * 8, 128)

    def fetch(j):
        return pltpu.make_async_copy(tr.at[:, pl.ds(j * 128, 128)], tin.at[j], tiles_in.at[j])

    def put(j):
        return pltpu.make_async_copy(tout.at[j], out.at[:, pl.ds(j * 128, 128)], tiles_out.at[j])

    at = lax.div(block, 4)
    spots = (at, jnp.maximum(at - 1, 0), jnp.minimum(at + 1, 3))
    fetches = [pltpu.make_async_copy(velocity, vel, statics_in.at[0]),
               pltpu.make_async_copy(coupling_in, coupling, statics_in.at[4]),
               pltpu.make_async_copy(mixing_in, mixing, statics_in.at[5])]
    for n, spot in enumerate(spots):
        fetches.append(pltpu.make_async_copy(
            mask.at[:, :, pl.ds(pl.multiple_of(spot * 128, 128), 128)], sea3.at[n], statics_in.at[n + 1]))
    for copy in fetches:
        copy.start()
    for j in range(4):
        fetch(j).start()

    for f in (fa, fb):
        f[0:2, 2:34] = jnp.zeros((2, 32, 8, 128), jnp.float32)
        f[10:12, 2:34] = jnp.zeros((2, 32, 8, 128), jnp.float32)
        f[2:10, 0:2] = jnp.zeros((8, 2, 8, 128), jnp.float32)
        f[2:10, 34:36] = jnp.zeros((8, 2, 8, 128), jnp.float32)

    barrier = pltpu.get_barrier_semaphore()

    def greet(d, carry):
        pl.semaphore_signal(barrier, inc=1, device_id=(r, lax.rem(g + d, G)), device_id_type=MESH)
        return carry

    lax.fori_loop(1, G, greet, 0)

    @pl.when(r > 0)
    def _():
        pl.semaphore_signal(barrier, inc=1, device_id=(r - 1, g_last), device_id_type=MESH)

    @pl.when(r > R // 2)
    def _():
        pl.semaphore_signal(barrier, inc=1, device_id=(r - 1, other), device_id_type=MESH)

    extra = jnp.where(jnp.logical_and(r >= R // 2, r < R - 1), 1, 0)

    @pl.when(r < R - 1)
    def _():
        pl.semaphore_signal(barrier, inc=1, device_id=(r + 1, g_next), device_id_type=MESH)

    for j in range(4):
        fetch(j).wait()

    def begin(copy):
        copy.start()

    def static_halo(do):
        @pl.when(r < R - 1)
        def _():
            do(pltpu.make_async_remote_copy(
                src_ref=pack_up, dst_ref=got_low, send_sem=send_static.at[0], recv_sem=recv_static.at[0],
                device_id=(r + 1, g_next), device_id_type=MESH))

        @pl.when(r > 0)
        def _():
            do(pltpu.make_async_remote_copy(
                src_ref=pack_down, dst_ref=got_high, send_sem=send_static.at[1], recv_sem=recv_static.at[1],
                device_id=(r - 1, g_last), device_id_type=MESH))

    def edges_over(do):
        @pl.when(r < R - 1)
        def _():
            to = flip(g, lax.div(r + 1, R // 2))
            do(pltpu.make_async_remote_copy(
                src_ref=pack_x, dst_ref=got_x, send_sem=send_static.at[4], recv_sem=recv_static.at[4],
                device_id=(r + 1, to), device_id_type=MESH))

        @pl.when(g < G - 1)
        def _():
            do(pltpu.make_async_remote_copy(
                src_ref=pack_y, dst_ref=got_y, send_sem=send_static.at[2], recv_sem=recv_static.at[2],
                device_id=(r, flip(g + 1)), device_id_type=MESH))

    def velocity_over(do, do_here):
        @pl.when(upper > 0)
        def _():
            do(pltpu.make_async_remote_copy(
                src_ref=vel_pack, dst_ref=vel_got, send_sem=send_static.at[3], recv_sem=recv_static.at[3],
                device_id=(r, block), device_id_type=MESH))

        @pl.when(upper == 0)
        def _():
            do_here(pltpu.make_async_copy(vel_pack, vel_got, recv_static.at[3]))

    fetches[0].wait()
    for k in range(3):
        for m in range(8):
            vel_pack[8 * k + m] = jnp.concatenate([vel[k, 4 * m + n] for n in range(4)], axis=1)
    pack_x[...] = vel_pack.reshape(24 * X, 128)[pl.ds(7, 8, stride=8), :]
    column = jnp.zeros((8, 128), jnp.float32)
    for m in range(8):
        column = jnp.where(lane % 32 == m, pltpu.roll(vel_pack[8 + m], m + 97, 1), column)
    pack_y[...] = column

    for h, quad in enumerate(QUADS):
        def regroup(n, carry, h=h, quad=quad):
            t, zq = n // 4, n % 4
            for j in range(4):
                v = [tin[j, pl.ds((t * NZ + zq * 8) * X + x, 8, stride=8), :] for x in quad]
                for i, b in enumerate(block_swap(v, lane)):
                    sb[4 * j + i, h, zq, t] = b
            return carry

        lax.fori_loop(0, 8, regroup, 0, unroll=8)
        if h == 0:
            pl.semaphore_wait(barrier, G - 1 + jnp.minimum(r, 1) + jnp.minimum(R - 1 - r, 1) + extra)
            velocity_over(begin, begin)
            edges_over(begin)

        def send(d, carry, h=h):
            to = lax.rem(g + d, G)
            pltpu.make_async_remote_copy(
                src_ref=sb.at[flip(to), h], dst_ref=rb.at[h, :, pl.ds(2 * g, 2)],
                send_sem=send_in.at[h], recv_sem=recv_in.at[h],
                device_id=(r, to), device_id_type=MESH).start()
            return carry

        lax.fori_loop(1, G, send, 0)
        pltpu.make_async_copy(sb.at[block, h], rb.at[h, :, pl.ds(2 * g, 2)], local_sem.at[h]).start()

    q[...] = jnp.zeros(q.shape, jnp.float32)
    for copy in fetches[1:]:
        copy.wait()
    velocity_over(lambda copy: copy.wait_recv(), lambda copy: copy.wait())
    for n in range(4):
        shifted = pltpu.roll(vel_got[...], (130 - 32 * n) % 128, 2)
        shifted = jnp.where(jnp.logical_and(lane >= 2, lane < 34), shifted, 0.0)
        for k in range(3):
            for m in range(8):
                q[k, 4 * m + n, 2:10, :] = shifted[8 * k + m]
    place = lax.rem(block, 4)
    has_left = jnp.minimum(at, 1).astype(jnp.float32)
    has_right = jnp.minimum(3 - at, 1).astype(jnp.float32)
    centre = sea3[0].astype(jnp.float32)
    left = sea3[1].astype(jnp.float32) * has_left
    right = sea3[2].astype(jnp.float32) * has_right
    centre = jnp.where(jnp.logical_and(lane >= 126, place == 0), left, centre)
    centre = jnp.where(jnp.logical_and(lane < 2, place == 3), right, centre)
    q[3, :, 2:10, :] = pltpu.roll(centre, lax.rem(130 - 32 * place, 128), 2)

    def level_rows(k, e):
        return q.at[k].reshape(NZ * 16, 128)[pl.ds(e, NZ, stride=16), :]

    def put_rows(k, e, value):
        q.at[k].reshape(NZ * 16, 128)[pl.ds(e, NZ, stride=16), :] = value

    pack_up[0], pack_up[1] = level_rows(3, 8), level_rows(3, 9)
    pack_down[0], pack_down[1] = level_rows(3, 2), level_rows(3, 3)

    static_halo(begin)

    def iota(shape, axis):
        return lax.broadcasted_iota(jnp.int32, shape, axis)

    square = (128, 128)
    block_in, block_out = iota(square, 0) // 32, iota(square, 1) // 32
    tall = (256, 128)
    part_at, block_at = iota(tall, 0) % 32, iota(tall, 1) // 32
    for k in range(NC):
        place_k = part_at - (block_at + (24 + 4 * (k - 3) if k >= 3 else 4 * k))
        hit = place_k == 0 if k >= 3 else jnp.logical_or(place_k == 0, place_k == 12)
        spread[:, k * 128:(k + 1) * 128] = jnp.where(hit, 1.0, 0.0).astype(jnp.bfloat16)
    first = iota(square, 0) % 32 == 0
    own = jnp.where(jnp.logical_and(first, block_in == block_out), 1.0, 0.0).astype(jnp.bfloat16)
    past = jnp.where(jnp.logical_and(first, block_in < block_out), 1.0, 0.0).astype(jnp.bfloat16)
    own_mat[...] = jnp.concatenate([own, own], 0)
    past_mat[...] = jnp.concatenate([past, past], 0)
    across = jnp.concatenate([coupling[...].T] * 4, 1)
    weights = jnp.where(block_in == block_out, jnp.concatenate([across] * 4, 0), 0.0)
    high, low = halves(weights)
    wmat[...] = jnp.concatenate([jnp.concatenate([high, low], 1), jnp.concatenate([high, jnp.zeros_like(low)], 1)], 0)
    tile = jnp.zeros((8, 128), jnp.float32)
    for z in range(NZ):
        tile = jnp.where(jnp.logical_and(row == z % 8, lane // 32 == z // 8), mixing[z], tile)
    mix[...] = tile

    @pl.when(r > 0)
    def _():
        pltpu.make_async_copy(got_low, got_low, recv_static.at[0]).wait()
        put_rows(3, 0, got_low[0])
        put_rows(3, 1, got_low[1])
        pltpu.make_async_copy(got_x, got_x, recv_static.at[4]).wait()
        for n in range(4):
            q.at[0].reshape(NZ * 16, 128)[pl.ds(n * 16 + 1, 8, stride=64), :] = jnp.where(
                jnp.logical_and(lane >= 2, lane < 34), pltpu.roll(got_x[...], (130 - 32 * n) % 128, 1), 0.0)

    @pl.when(r < R - 1)
    def _():
        pltpu.make_async_copy(got_high, got_high, recv_static.at[1]).wait()
        put_rows(3, 10, got_high[0])
        put_rows(3, 11, got_high[1])

    @pl.when(block > 0)
    def _():
        pltpu.make_async_copy(got_y, got_y, recv_static.at[2]).wait()

        def unpack_level(z, carry):
            q[1, z, 2:10, :] = jnp.where(
                lane == 1, pltpu.roll(got_y[...], lax.rem(129 - lax.div(z, 4) - 32 * lax.rem(z, 4) + 128, 128), 1), q[1, z, 2:10, :])
            return carry

        lax.fori_loop(0, NZ, unpack_level, 0, unroll=8)

    sea = q[3]
    follow = (pltpu.roll(sea, 15, 1), pltpu.roll(sea, 127, 2),
              jnp.concatenate([sea[1:], jnp.zeros((1, 16, 128), jnp.float32)], 0))
    for k in range(3):
        opened = sea * follow[k]
        c = q[k] * opened
        high = c.astype(jnp.bfloat16).astype(jnp.float32)
        dc[k] = high
        dc[3 + k] = c - high
    dc[6] = sea
    dc[7] = opened

    def stack_one(e, carry):
        for half in range(2):
            rows = [dc.reshape(8 * NZ * 16, 128)[pl.ds((half * 4 + n) * 16 + e, 32, stride=128), :] for n in range(4)]
            stacked[pl.ds(pl.multiple_of(e * 40, 8), 40), half * 128:(half + 1) * 128] = (
                jnp.concatenate(rows, axis=0).T[:40])
        return carry

    own_lanes = iota((8, 256), 0) == iota((8, 256), 1) // 32

    def spread_some(n, carry):
        value = stacked[pl.ds(pl.multiple_of(n * 160, 8), 160), :]
        value = jnp.where(own_lanes, jnp.broadcast_to(value[:, None, :], (160, 8, 256)), 0.0)
        wide = jnp.dot(value.reshape(1280, 256).astype(jnp.bfloat16), spread[...], preferred_element_type=jnp.float32)
        for m in range(4):
            for k in range(NC):
                coef[k, 4 * n + m] = wide[m * 320:m * 320 + YE * 8, k * 128:(k + 1) * 128].reshape(YE, 8, 128)
        return carry

    def x_halo(f, s, y0, y1):
        slot = s + y0 // (YB // 2)

        @pl.when(r > 0)
        def _():
            pltpu.make_async_remote_copy(
                src_ref=f.at[2:4, y0 + 2:y1 + 2], dst_ref=f.at[10:12, y0 + 2:y1 + 2],
                send_sem=send_halo.at[s, 0], recv_sem=recv_x.at[slot, 1],
                device_id=(r - 1, g_last), device_id_type=MESH).start()

        @pl.when(r < R - 1)
        def _():
            pltpu.make_async_remote_copy(
                src_ref=f.at[8:10, y0 + 2:y1 + 2], dst_ref=f.at[0:2, y0 + 2:y1 + 2],
                send_sem=send_halo.at[s, 1], recv_sem=recv_x.at[slot, 0],
                device_id=(r + 1, g_next), device_id_type=MESH).start()

    def y_halo(f, s, h):
        @pl.when(block > 0)
        def _():
            for x0, x1 in RANGES[h]:
                pltpu.make_async_remote_copy(
                    src_ref=f.at[x0 + 2:x1 + 2, 2:4], dst_ref=f.at[x0 + 2:x1 + 2, 34:36],
                    send_sem=send_y.at[s, h, 1], recv_sem=recv_y.at[s, h, 1],
                    device_id=(r, flip(block - 1)), device_id_type=MESH).start()

        @pl.when(block < G - 1)
        def _():
            for x0, x1 in RANGES[h]:
                pltpu.make_async_remote_copy(
                    src_ref=f.at[x0 + 2:x1 + 2, 32:34], dst_ref=f.at[x0 + 2:x1 + 2, 0:2],
                    send_sem=send_y.at[s, h, 0], recv_sem=recv_y.at[s, h, 0],
                    device_id=(r, flip(block + 1)), device_id_type=MESH).start()

    def landed(ref, sem):
        pltpu.make_async_copy(ref, ref, sem).wait()

    def sent_x(f, s):
        @pl.when(r > 0)
        def _():
            landed(f.at[2:4, 2:34], send_halo.at[s, 0])

        @pl.when(r < R - 1)
        def _():
            landed(f.at[8:10, 2:34], send_halo.at[s, 1])

    def arrive_x(f, s, y0, y1):
        slot = s + y0 // (YB // 2)

        @pl.when(r > 0)
        def _():
            landed(f.at[0:2, y0 + 2:y1 + 2], recv_x.at[slot, 0])

        @pl.when(r < R - 1)
        def _():
            landed(f.at[10:12, y0 + 2:y1 + 2], recv_x.at[slot, 1])

    def arrive_y(f, s, h):
        @pl.when(block > 0)
        def _():
            landed(f.at[2:6, 0:2], recv_y.at[s, h, 0])

        @pl.when(block < G - 1)
        def _():
            landed(f.at[2:6, 34:36], recv_y.at[s, h, 1])

    def sent_y(f, s, h):
        @pl.when(block > 0)
        def _():
            landed(f.at[2:6, 2:4], send_y.at[s, h, 1])

        @pl.when(block < G - 1)
        def _():
            landed(f.at[2:6, 32:34], send_y.at[s, h, 0])

    for h, quad in enumerate(QUADS):
        some = rb.at[h, :, 0:2 * (G - 1)]
        pltpu.make_async_copy(some, some, recv_in.at[h]).wait()
        pltpu.make_async_copy(sb.at[block, h], rb.at[h, :, pl.ds(2 * g, 2)], local_sem.at[h]).wait()

        def turn(zr, carry, h=h, quad=quad):
            turned = rb2[pl.ds(h * 4 * NT * 8 + zr, 128, stride=8), :].T
            for n, x in enumerate(quad):
                fa2[pl.ds(((x + 2) * YE + 2) * 8 + zr, YB, stride=8), :] = turned[n * YB:(n + 1) * YB]
            return carry

        lax.fori_loop(0, 8, turn, 0, unroll=8)
        if h == 0:
            x_halo(fa, 0, 0, YB)
        y_halo(fa, 0, h)
        if h == 0:
            lax.fori_loop(0, XE, stack_one, 0, unroll=2)

    def z_edges(f, x0, x1):
        def rows(ref, k):
            return ref.reshape(ref.shape[0] * ref.shape[1] * 8, 128)[pl.ds((x0 + 2) * YE * 8 + k, (x1 - x0) * YE, stride=8), :]

        def static(k, n):
            return rows(coef.at[k], n)

        next0 = pltpu.roll(rows(f, 0), 96, 1)
        next1 = pltpu.roll(rows(f, 1), 96, 1)
        last = rows(f, 7)
        jump = (next0 - last) * static(OZ, 7)
        slope = minmod((last - rows(f, 6)) * static(OZ, 6), jump)
        slope_next = minmod(jump, (next1 - next0) * pltpu.roll(static(OZ, 0), 96, 1))
        flux = face(last, next0, slope, slope_next, static(CZ, 7)) - mix[7:8, :] * jump
        for n, k, v in ((0, 7, next0), (0, 0, pltpu.roll(jump, 32, 1)), (1, 7, slope_next), (1, 0, pltpu.roll(flux, 32, 1))):
            edge.at[n].reshape(X * YE * 8, 128)[pl.ds(x0 * YE * 8 + k, (x1 - x0) * YE, stride=8), :] = v

    def advect(f, h, then, ready):
        parts = [advect_part(f, x0, x1) for x0, x1 in RANGES[h]]

        def column(y, carry):
            return tuple(step(y, c) for (_, step), c in zip(parts, carry))

        carry = tuple(start for start, _ in parts)
        for y0, y1 in ((0, YB // 2), (YB // 2, YB)):
            ready(y0, y1)
            carry = lax.fori_loop(y0, y1, column, carry, unroll=4)
            then(y0, y1)

    def advect_part(f, x0, x1):
        z_edges(f, x0, x1)
        n = x1 - x0

        def cells(e):
            return f[x0 + 2:x1 + 2, e]

        def along(k, e):
            return coef[k, x0 + 2:x1 + 2, e]

        def open_y(e):
            return along(SEA, e) * along(SEA, e + 1)

        f1, f2 = cells(1), cells(2)
        j0 = (f1 - cells(0)) * open_y(0)
        j1 = (f2 - f1) * open_y(1)
        j2 = (cells(3) - f2) * open_y(2)
        s1, s2 = minmod(j0, j1), minmod(j1, j2)
        start = (j2, s2, face(f1, f2, s1, s2, along(CY, 1)))

        def column(y, carry):
            jump, slope, before = carry
            e = y + 2
            fx = f[x0:x1 + 4, e]
            inner, following = fx[2:n + 2], cells(e + 1)
            jump_next = (cells(e + 2) - following) * open_y(e + 1)
            slope_next = minmod(jump, jump_next)
            after = face(inner, following, slope, slope_next, along(CY, e))
            total = inner - (after - before)
            sea_x = coef[SEA, x0:x1 + 4, e]
            jx = (fx[1:] - fx[:-1]) * (sea_x[1:] * sea_x[:-1])
            sx = minmod(jx[:-1], jx[1:])
            flux = face(fx[1:n + 2], fx[2:n + 3], sx[:-1], sx[1:], coef[CX, x0 + 1:x1 + 2, e])
            total = total - (flux[1:] - flux[:-1])
            edge0, edge1 = edge[0, x0:x1, e], edge[1, x0:x1, e]
            below = jnp.where(row == 7, edge0, pltpu.roll(inner, 7, 1))
            jz = (below - inner) * along(OZ, e)
            sz = minmod(jnp.where(row == 0, edge0, pltpu.roll(jz, 1, 1)), jz)
            sz_next = jnp.where(row == 7, edge1, pltpu.roll(sz, 7, 1))
            down = face(inner, below, sz, sz_next, along(CZ, e)) - mix[...] * jz
            adv[x0:x1, y] = total - (down - jnp.where(row == 0, edge1, pltpu.roll(down, 1, 1)))
            return jump_next, slope_next, after

        return start, column

    def react(h, results, y0, y1):
        length = y1 - y0
        count = 4 * length
        a = jnp.concatenate([adv[x0:x1, y0:y1].reshape((x1 - x0) * length, 8, 128) for x0, x1 in RANGES[h]], axis=0)
        att = 0.05 + 0.1 * a * a
        inc = att
        for step in (1, 2, 4):
            inc = inc + jnp.where(row >= step, pltpu.roll(inc, step, 1), 0.0)

        def spread_over(value, matrix):
            parts = jnp.concatenate(halves(value.reshape(count * 8, 128)), axis=1)
            return jnp.dot(parts, matrix[...], preferred_element_type=jnp.float32)

        both = spread_over(jnp.tanh(a), wmat)
        ahead = spread_over(inc - att, own_mat).reshape(count, 8, 128)
        past = spread_over(inc, past_mat).reshape(count, 8, 128)
        light = jnp.exp(-(ahead + past[:, 7:8, :]))
        response = (both[:, :128] + both[:, 128:]).reshape(count, 8, 128)
        change = (0.5 + light) * response
        for n, (x, result) in enumerate(zip(QUADS[h], results)):
            part = slice(n * length, (n + 1) * length)
            result[...] = a[part] + coef[SEA, x + 2, y0 + 2:y1 + 2] * change[part]

    fc2 = fc.reshape(X * YB * 8, 128)

    def give_back(h, quad):
        def turn_back(zr, carry):
            stack = [fc2[pl.ds(x * YB * 8 + zr, YB, stride=8), :] for x in quad]
            so2[pl.ds(h * 4 * NT * 8 + zr, 128, stride=8), :] = jnp.concatenate(stack, axis=0).T
            return carry

        lax.fori_loop(0, 8, turn_back, 0, unroll=8)

        def send_back(d, carry):
            to = lax.rem(g + d, G)
            pltpu.make_async_remote_copy(
                src_ref=so.at[h, :, pl.ds(2 * to, 2)], dst_ref=ro.at[h, block],
                send_sem=send_out.at[h], recv_sem=recv_out.at[h],
                device_id=(r, to), device_id_type=MESH).start()
            return carry

        lax.fori_loop(1, G, send_back, 0)
        pltpu.make_async_copy(so.at[h, :, pl.ds(2 * g, 2)], ro.at[h, block], local_sem.at[2 + h]).start()

    lax.fori_loop(0, XE // 4, spread_some, 0)

    for h in (1, 0):
        arrive_y(fa, 0, h)

        def step_1(y0, y1, h=h):
            if h == 1:
                if y1 == YB:
                    react(h, [fb.at[x + 2, 2:34] for x in QUADS[h]], 0, YB)
            else:
                react(h, [fb.at[x + 2, y0 + 2:y1 + 2] for x in QUADS[h]], y0, y1)
                x_halo(fb, 1, y0, y1)

        advect(fa, h, step_1, lambda y0, y1, h=h: arrive_x(fa, 0, 0, YB) if h == 0 and y0 == 0 else None)
        y_halo(fb, 1, h)
    for h in (1, 0):
        arrive_y(fb, 1, h)
        advect(fb, h, lambda y0, y1: None, lambda y0, y1, h=h: arrive_x(fb, 1, y0, y1) if h == 0 else None)
        react(h, [fc.at[x] for x in QUADS[h]], 0, YB)
        give_back(h, QUADS[h])

    static_halo(lambda copy: copy.wait_send())
    edges_over(lambda copy: copy.wait_send())

    @pl.when(upper > 0)
    def _():
        landed(vel_pack, send_static.at[3])

    for s, f in ((0, fa), (1, fb)):
        sent_x(f, s)
        for h in range(2):
            sent_y(f, s, h)

    for h in (1, 0):
        some = ro.at[h, 0:G - 1]
        pltpu.make_async_copy(some, some, recv_out.at[h]).wait()
        pltpu.make_async_copy(so.at[h, :, pl.ds(2 * g, 2)], ro.at[h, block], local_sem.at[2 + h]).wait()

        def restore(n, carry, h=h, quad=QUADS[h]):
            t, zq = n // 4, n % 4
            for j in range(4):
                v = block_swap([ro[h, 4 * j + i, zq, t] for i in range(4)], lane)
                for x, b in zip(quad, v):
                    tout[j, pl.ds((t * NZ + zq * 8) * X + x, 8, stride=8), :] = b
            return carry

        lax.fori_loop(0, 8, restore, 0, unroll=4)

    for j in range(4):
        put(j).start()
    for h in range(2):
        some = sb.at[0:G - 1, h]
        pltpu.make_async_copy(some, some, send_in.at[h]).wait()
        some = ro.at[h, 0:G - 1]
        pltpu.make_async_copy(some, some, send_out.at[h]).wait()
    for j in range(4):
        put(j).wait()


def shards(tracers, velocity, sea_mask, coupling, mixing):
    anywhere = pl.BlockSpec(memory_space=pl.ANY)
    vmem = pl.BlockSpec(memory_space=pltpu.VMEM)
    f32 = jnp.float32
    dma = pltpu.SemaphoreType.DMA
    out = pl.pallas_call(
        kernel,
        out_shape=jax.ShapeDtypeStruct((2 * NZ * X, G * YB), f32),
        in_specs=[anywhere] * 3 + [anywhere, anywhere],
        out_specs=anywhere,
        scratch_shapes=[
            pltpu.VMEM((NT, NT), f32),
            pltpu.SMEM((NZ,), f32),
            pltpu.VMEM((256, NC * 128), jnp.bfloat16),
            pltpu.VMEM((XE * 40, 256), f32),
            pltpu.VMEM((256, 128), jnp.bfloat16),
            pltpu.VMEM((256, 128), jnp.bfloat16),
            pltpu.VMEM((8, 128), f32),
            pltpu.VMEM((256, 256), jnp.bfloat16),
            pltpu.VMEM((3, NZ, X, YB), f32),
            pltpu.VMEM((24, X, 128), f32),
            pltpu.VMEM((24, X, 128), f32),
            pltpu.VMEM((3, NZ, X, 128), jnp.int32),
            pltpu.VMEM((4, NZ, 16, 128), f32),
            pltpu.VMEM((8, NZ, 16, 128), f32),
            pltpu.VMEM((2, NZ, 128), f32),
            pltpu.VMEM((2, NZ, 128), f32),
            pltpu.VMEM((8, 128), f32),
            pltpu.VMEM((8, 128), f32),
            pltpu.VMEM((8, 128), f32),
            pltpu.VMEM((2, NZ, 128), f32),
            pltpu.VMEM((2, NZ, 128), f32),
            pltpu.VMEM((8, 128), f32),
            pltpu.VMEM((4, 2 * NZ * X, 128), f32),
            pltpu.VMEM((4, 2 * NZ * X, 128), f32),
            pltpu.VMEM((G, 2, 4, 2, 8, 128), f32),
            pltpu.VMEM((2, 4, NT, 8, 128), f32),
            pltpu.VMEM((XE, YE, 8, 128), f32),
            pltpu.VMEM((XE, YE, 8, 128), f32),
            pltpu.VMEM((X, YB, 8, 128), f32),
            pltpu.VMEM((X, YB, 8, 128), f32),
            pltpu.VMEM((2, X, YE, 8, 128), f32),
            pltpu.VMEM((NC, XE, YE, 8, 128), f32),
            pltpu.VMEM((2, 4, NT, 8, 128), f32),
            pltpu.VMEM((2, G, 4, 2, 8, 128), f32),
            dma((6,)), dma((5,)), dma((5,)),
            dma((4,)), dma((4,)), dma((2,)), dma((2,)), dma((2, 2)), dma((3, 2)), dma((2, 2, 2)), dma((2, 2, 2)), dma((2,)), dma((2,)), dma((4,)),
        ],
        compiler_params=pltpu.CompilerParams(
            collective_id=0, has_side_effects=True, vmem_limit_bytes=60 * 2**20),
    )(tracers.reshape(2 * NZ * X, G * YB), velocity, sea_mask, coupling, mixing)
    return out.reshape(tracers.shape)


def solution(mesh):
    placed = (
        P("group", None, "region", None),
        P(None, None, "region", "group"),
        P(None, "region", None),
        P(),
        P(),
    )
    return jax.shard_map(
        shards,
        mesh=mesh,
        in_specs=placed,
        out_specs=P("group", None, "region", None),
        check_vma=False,
    )
```
